32 devices in a mesh: row: 4 (over z), col: 8 (over y, x, core).
Axes of the slice: x: 2, y: 2, z: 4, core: 2. Of those that a mesh axis runs over, the one named last changes fastest.
Arguments:
- features: bfloat16 [4096, 128], P(('row', 'col')), may hold values from -6 to 6
- deg_scale: bfloat16 [4096], P(('row', 'col')), may hold values from 0.049804688 to 0.5
- weight: bfloat16 [128, 256], replicated, may hold values from -0.5 to 0.5
- cotangent: bfloat16 [4096, 256], P(('row', 'col')), may hold values from -6 to 6
- tile_rows: int32 [4, 8, 8], P('row', 'col'), may hold values from 0 to 3, as said below
- tile_cols: int32 [4, 8, 8], P('row', 'col'), may hold values from 0 to 1, as said below
- tile_count: int32 [4, 8], P('row', 'col'), may hold values from 1 to 8, as said below
- tile_bits: int32 [4, 8, 8, 32, 256], P('row', 'col'), may hold values from 0 to 255, as said below
Outputs:
- activations: bfloat16 [4096, 256], P(('row', 'col'))
- input_grad: bfloat16 [4096, 128], P(('row', 'col'))
- weight_grad: float32 [128, 256], replicated
The draws below stay inside these ranges and needn't reach their ends.
Inputs may be any that keep to these rules, and one draw needn't show every extreme that they name: The 8 slots of one block name distinct pairs (tile_rows, tile_cols). `tile_cols`: paired with tile_rows slot by slot. `tile_count`: some block fills all 8 slots. `tile_bits`: bit k of word [a, b] of a slot is the tile's entry in row 8 a + k and column b.
All inputs are finite; a program needn't handle non-finite values.
Results may differ from the reference program's by a relative error of at most 0.0065.
Values may be sent and summed in bfloat16 or wider, within the bound.
No kernel may reach another device: no remote copies, remote signals or barrier semaphores. Data moves between devices by JAX's collectives and lax.ppermute only.
A program may use at most 64 MiB of HBM per device.

```python
import math
import jax
import jax.numpy as jnp
from jax import lax

FI = 128
FO = 256
VERT_DEV = 128
TILE = 256
ROW_BLOCKS = 4
COL_BLOCKS = 8
NV = 4096
ROW_TILES = 4
COL_TILES = 2
SLOTS = 8


def tile_positions(key):
    shared_key = jax.random.fold_in(key, 11)
    device_keys = jax.random.split(shared_key, ROW_BLOCKS * COL_BLOCKS)
    positions = ROW_TILES * COL_TILES

    def shuffle(device_key):
        return jax.random.permutation(device_key, positions)[:SLOTS]
    return jax.vmap(shuffle)(device_keys).reshape(ROW_BLOCKS, COL_BLOCKS, SLOTS).astype(jnp.int32)


def draw_tile_rows(key, part):
    shared = tile_positions(key)
    return (shared // COL_TILES).astype(jnp.int32)


def draw_tile_cols(key, part):
    shared = tile_positions(key)
    return (shared % COL_TILES).astype(jnp.int32)


def draw_tile_count(key, part):
    key = jax.random.fold_in(key, 5)
    first, second = jax.random.split(key)
    levels = jax.random.randint(first, (ROW_BLOCKS * COL_BLOCKS,), 0, 4).astype(jnp.int32)
    ranking = jax.random.permutation(second, ROW_BLOCKS * COL_BLOCKS)
    levels = levels.at[ranking[0]].set(0).at[ranking[1]].set(3)
    live_counts = jnp.maximum(jnp.right_shift(jnp.full_like(levels, SLOTS), levels), 1)
    return live_counts.reshape(ROW_BLOCKS, COL_BLOCKS).astype(jnp.int32)


def draw_tile_bits(key, part):
    key = jax.random.fold_in(key, 7)
    word_keys = jax.random.split(key, 9)
    word_shape = (ROW_BLOCKS, COL_BLOCKS, SLOTS, TILE // 8, TILE)
    combined = jnp.full(word_shape, 255, jnp.int32)
    for index in range(8):
        random_word = jax.random.randint(word_keys[index], word_shape, 0, 256).astype(jnp.int32)
        combined = jnp.bitwise_and(combined, random_word)
    place_keys = jax.random.split(word_keys[8], 5)
    first_place = jax.random.randint(place_keys[0], (), 0, ROW_BLOCKS).astype(jnp.int32)
    second_place = jax.random.randint(place_keys[1], (), 0, COL_BLOCKS).astype(jnp.int32)
    third_place = jax.random.randint(place_keys[2], (), 0, SLOTS).astype(jnp.int32)
    fourth_place = jax.random.randint(place_keys[3], (), 0, TILE // 8).astype(jnp.int32)
    fifth_place = jax.random.randint(place_keys[4], (), 0, TILE).astype(jnp.int32)
    combined = combined.at[first_place, second_place, third_place, fourth_place, fifth_place].set(255)
    return combined.astype(jnp.int32)


def steps_of(own_key, shape, pieces, low, largest):
    gain, own = 1.0, jax.random.fold_in(own_key, 6)
    for axis_at, blocks in pieces:
        heights = jnp.exp(jax.random.uniform(jax.random.fold_in(own, axis_at), (blocks,), jnp.float32, low / len(pieces), largest / len(pieces)))
        gain = gain * jnp.repeat(heights, shape[axis_at] // blocks).reshape([-1 if axis == axis_at else 1 for axis in range(len(shape))])
    return gain


def centred(key, extent, scale, most, pieces=(), held_as=jnp.bfloat16):
    drawn = scale * jax.random.normal(key, extent, jnp.float32)
    if pieces:
        drawn = drawn * steps_of(key, extent, pieces, -0.22, 0.18)
    return jnp.clip(drawn, -most, most).astype(held_as)


def setup_inputs(seed: int = 0) -> dict:
    key_list = jax.random.split(jax.random.key(seed), 9)
    return {
        "features": centred(key_list[0], (NV, FI), 1.0, 6.0, ((0, 32),)),
        "deg_scale": jnp.clip(jnp.exp(math.log(0.5) - 2.306499 * jax.random.uniform(key_list[1], (NV,), jnp.float32) ** steps_of(key_list[1], (NV,), ((0, 32),), -0.2, 0.2)), 0.049804688, 0.5).astype(jnp.bfloat16),
        "weight": centred(key_list[2], (FI, FO), FI ** -0.5, 0.5),
        "cotangent": centred(key_list[3], (NV, FO), 1.0, 6.0, ((0, 32),)),
        "tile_rows": draw_tile_rows(jax.random.fold_in(key_list[8], 71), 0),
        "tile_cols": draw_tile_cols(jax.random.fold_in(key_list[8], 71), 0),
        "tile_count": draw_tile_count(jax.random.fold_in(key_list[8], 71), 0),
        "tile_bits": draw_tile_bits(jax.random.fold_in(key_list[8], 71), 0),
    }


def unpack_tiles(packed):
    shifts = jnp.arange(8, dtype=jnp.int32)
    bit_values = jnp.bitwise_and(jnp.right_shift(packed[:, :, None, :], shifts[None, None, :, None]), 1)
    return bit_values.reshape(packed.shape[0], packed.shape[1] * 8, packed.shape[2])

def silu_slope(pre_act):
    sigmoid_value = jax.nn.sigmoid(pre_act)
    return sigmoid_value * (1.0 + pre_act * (1.0 - sigmoid_value))

def reference(features, deg_scale, weight, cotangent, tile_rows, tile_cols, tile_count, tile_bits):
    scale = deg_scale.astype(jnp.float32)
    scaled = (features.astype(jnp.float32) * scale[:, None]).astype(jnp.bfloat16)
    grid = scaled.reshape(ROW_BLOCKS, COL_BLOCKS, VERT_DEV, FI)
    slot_ids = jnp.arange(SLOTS, dtype=jnp.int32)

    def forward_block(row_pos):

        def block_step(running, col_pos):
            source = grid[:, col_pos].reshape(COL_TILES, TILE, FI)
            mask_tiles = unpack_tiles(tile_bits[row_pos, col_pos]).astype(jnp.float32)
            picked = source[tile_cols[row_pos, col_pos]].astype(jnp.float32)
            products = jnp.einsum('sab,sbf->saf', mask_tiles, picked)
            live_slots = (slot_ids < tile_count[row_pos, col_pos]).astype(jnp.float32)
            running = running.at[tile_rows[row_pos, col_pos]].add(products * live_slots[:, None, None])
            return (running, None)
        initial = jnp.zeros((ROW_TILES, TILE, FI), jnp.float32)
        running, _ = lax.scan(block_step, initial, jnp.arange(COL_BLOCKS, dtype=jnp.int32))
        return running.reshape(COL_BLOCKS * VERT_DEV, FI)
    summed = lax.map(forward_block, jnp.arange(ROW_BLOCKS, dtype=jnp.int32)).reshape(NV, FI)
    hidden = (summed * scale[:, None]).astype(jnp.bfloat16)
    pre_act = jnp.dot(hidden, weight, preferred_element_type=jnp.float32)
    activations = jax.nn.silu(pre_act).astype(jnp.bfloat16)
    slope_term = (cotangent.astype(jnp.float32) * silu_slope(pre_act)).astype(jnp.bfloat16)
    weight_grad = jnp.dot(hidden.T, slope_term, preferred_element_type=jnp.float32) / math.sqrt(NV)
    spread = jnp.dot(slope_term, weight.T, preferred_element_type=jnp.float32)
    back = (spread * scale[:, None]).astype(jnp.bfloat16)
    back_grid = back.reshape(ROW_BLOCKS, COL_BLOCKS * VERT_DEV, FI)

    def backward_block(col_pos):

        def block_step(running, row_pos):
            source = back_grid[row_pos].reshape(ROW_TILES, TILE, FI)
            mask_tiles = unpack_tiles(tile_bits[row_pos, col_pos]).astype(jnp.float32)
            picked = source[tile_rows[row_pos, col_pos]].astype(jnp.float32)
            products = jnp.einsum('sab,saf->sbf', mask_tiles, picked)
            live_slots = (slot_ids < tile_count[row_pos, col_pos]).astype(jnp.float32)
            running = running.at[tile_cols[row_pos, col_pos]].add(products * live_slots[:, None, None])
            return (running, None)
        initial = jnp.zeros((COL_TILES, TILE, FI), jnp.float32)
        running, _ = lax.scan(block_step, initial, jnp.arange(ROW_BLOCKS, dtype=jnp.int32))
        return running.reshape(ROW_BLOCKS, VERT_DEV, FI)
    column_parts = lax.map(backward_block, jnp.arange(COL_BLOCKS, dtype=jnp.int32))
    gathered = jnp.transpose(column_parts, (1, 0, 2, 3)).reshape(NV, FI)
    input_grad = (gathered * scale[:, None]).astype(jnp.bfloat16)
    return (activations, input_grad, weight_grad)
```

```python
import functools
import math

import jax
import jax.numpy as jnp
from jax import lax
from jax.experimental import pallas as pl
from jax.experimental.pallas import tpu as pltpu
from jax.sharding import PartitionSpec as P

VMEM = pl.BlockSpec(memory_space=pltpu.VMEM)
SMEM = pl.BlockSpec(memory_space=pltpu.SMEM)
LIMIT = pltpu.CompilerParams(vmem_limit_bytes=40 * 1024 * 1024)
DIRECT = 4
AXES = ("row", "col")


def struct(shape, dtype):
    return jax.ShapeDtypeStruct(shape, dtype)


def call(body, out_shape, operands, specs=None, scratch=(), flops=1 << 20, moved=1 << 20):
    single = not isinstance(out_shape, (tuple, list))
    return pl.pallas_call(
        body,
        out_shape=out_shape,
        in_specs=specs or [VMEM] * len(operands),
        out_specs=VMEM if single else [VMEM] * len(out_shape),
        scratch_shapes=list(scratch),
        compiler_params=LIMIT,
        cost_estimate=pl.CostEstimate(flops=flops, bytes_accessed=moved, transcendentals=0),
    )(*operands)


def scale_features(deg_ref, features_ref, scaled_ref, column_ref):
    size = features_ref.shape[0]
    scale_row = deg_ref[...].astype(jnp.float32)
    rows = lax.broadcasted_iota(jnp.int32, (size, size), 0)
    columns = lax.broadcasted_iota(jnp.int32, (size, size), 1)
    diagonal = jnp.where(rows == columns, scale_row, 0.0).astype(jnp.bfloat16)
    spread = jnp.dot(
        diagonal, jnp.ones((size, size), jnp.bfloat16), preferred_element_type=jnp.float32
    )
    column_ref[...] = spread
    scaled_ref[...] = (features_ref[...].astype(jnp.float32) * spread).astype(jnp.bfloat16)


def unpack_tiles(count_ref, bits_ref, after_ref, masks_ref):
    slots, words, tile_size = bits_ref.shape[2:]
    live_count = count_ref[0, 0]

    def one(slot):
        packed = jnp.where(slot < live_count, bits_ref[0, 0, slot], 0)
        repeated = jnp.broadcast_to(packed[:, None, :], (words, 8, tile_size))
        shifts = lax.broadcasted_iota(jnp.int32, (words, 8, tile_size), 1)
        bit_values = jnp.bitwise_and(jnp.right_shift(repeated, shifts), 1)
        masks_ref[slot] = (
            bit_values.reshape(words * 8, tile_size).astype(jnp.float32).astype(jnp.bfloat16)
        )

    each_slot(slots, one)


def each_slot(slots, one):
    if slots <= 8:
        for slot in range(slots):
            one(slot)
    else:
        pl.loop(0, slots)(one)


def forward_partial(me_ref, rows_ref, cols_ref, masks_ref, *refs):
    *blocks, partial_ref, source, total = refs
    slots, tile_size = masks_ref.shape[:2]
    place_blocks(me_ref, blocks, source)
    total[...] = jnp.zeros_like(total)

    def one(slot):
        place = pl.ds(pl.multiple_of(rows_ref[0, 0, slot] * tile_size, tile_size), tile_size)
        pick = pl.ds(pl.multiple_of(cols_ref[0, 0, slot] * tile_size, tile_size), tile_size)
        total[place, :] += jnp.dot(
            masks_ref[slot], source[pick, :], preferred_element_type=jnp.float32
        )

    each_slot(slots, one)
    partial_ref[...] = total[...].astype(jnp.bfloat16).reshape(partial_ref.shape)


def place_blocks(me_ref, blocks, source):
    if len(blocks) == 1:
        source[...] = blocks[0][...].reshape(source.shape)
        return
    shards, size = len(blocks), blocks[0].shape[0]
    for step, block in enumerate(blocks):
        owner = lax.rem(me_ref[0] + shards - step, shards)
        source[pl.ds(pl.multiple_of(owner * size, size), size), :] = block[...]


def vertex_part(received_ref, column_ref, deg_ref, weight_ref, cotangent_ref, act_ref, back_ref, grad_ref):
    summed = jnp.sum(received_ref[...].astype(jnp.float32), axis=0)
    hidden = (summed * column_ref[...]).astype(jnp.bfloat16)
    weight = weight_ref[...]
    pre_act = jnp.dot(hidden, weight, preferred_element_type=jnp.float32)
    sigmoid_value = 1.0 / (1.0 + jnp.exp(-pre_act))
    act_ref[...] = (pre_act * sigmoid_value).astype(jnp.bfloat16)
    slope = sigmoid_value * (1.0 + pre_act * (1.0 - sigmoid_value))
    slope_term = (cotangent_ref[...].astype(jnp.float32) * slope).astype(jnp.bfloat16)
    spread = lax.dot_general(
        weight, slope_term, (((1,), (1,)), ((), ())), preferred_element_type=jnp.float32
    )
    back = (spread * deg_ref[...].astype(jnp.float32)).astype(jnp.bfloat16)
    back_ref[...] = jnp.broadcast_to(back[None], back_ref.shape)
    local_grad = lax.dot_general(
        hidden, slope_term, (((0,), (0,)), ((), ())), preferred_element_type=jnp.float32
    )
    for half in range(grad_ref.shape[0]):
        grad_ref[half] = local_grad[:, half * 128 : (half + 1) * 128]


def backward_partial(me_ref, rows_ref, cols_ref, masks_ref, gathered_ref, *refs):
    *pieces, source, total = refs
    slots, tile_size = masks_ref.shape[:2]
    shards, _, size = gathered_ref.shape
    for shard in range(shards):
        source[:, shard * size : (shard + 1) * size] = gathered_ref[shard]
    total[...] = jnp.zeros_like(total)

    def one(slot):
        pick = pl.ds(pl.multiple_of(rows_ref[0, 0, slot] * tile_size, tile_size), tile_size)
        place = pl.ds(pl.multiple_of(cols_ref[0, 0, slot] * tile_size, tile_size), tile_size)
        total[:, place] += jnp.dot(
            source[:, pick], masks_ref[slot], preferred_element_type=jnp.float32
        )

    each_slot(slots, one)
    if len(pieces) == 1:
        for shard in range(pieces[0].shape[0]):
            pieces[0][shard] = total[:, shard * size : (shard + 1) * size].astype(jnp.bfloat16)
        return
    for step, piece in enumerate(pieces):
        owner = lax.rem(me_ref[0] + step, len(pieces))
        place = pl.ds(pl.multiple_of(owner * size, size), size)
        piece[...] = total[:, place].astype(jnp.bfloat16)


def input_part(deg_ref, *refs):
    *pieces, out_ref = refs
    if len(pieces) == 1:
        total = jnp.sum(pieces[0][...].astype(jnp.float32), axis=0)
    else:
        total = sum(piece[...].astype(jnp.float32) for piece in pieces)
    out_ref[...] = (total * deg_ref[...].astype(jnp.float32)).T.astype(jnp.bfloat16)


def sum_pieces(factor, received_ref, out_ref):
    total = jnp.sum(received_ref[...], axis=0) * factor
    out_ref[...] = jnp.broadcast_to(total[None], out_ref.shape)


def join_halves(whole_ref, out_ref):
    for half in range(whole_ref.shape[0]):
        out_ref[:, half * 128 : (half + 1) * 128] = whole_ref[half]


def shifted(block, axis, shards, step):
    return lax.ppermute(block, axis, [(source, (source + step) % shards) for source in range(shards)])


def on_device(features, deg_scale, weight, cotangent, tile_rows, tile_cols, tile_count, tile_bits):
    size, width = features.shape
    height, out_width = weight.shape
    row_shards = lax.axis_size("row")
    col_shards = lax.axis_size("col")
    devices = row_shards * col_shards
    total_verts = devices * size
    slots, words, tile_size = tile_bits.shape[2:]
    direct = row_shards <= DIRECT
    bf16, f32 = jnp.bfloat16, jnp.float32
    me = lax.axis_index("row").astype(jnp.int32).reshape(1)
    deg_row = deg_scale.reshape(1, size)
    factor = 1.0 / math.sqrt(total_verts)

    scaled, column = call(
        scale_features,
        (struct((size, width), bf16), struct((size, width), f32)),
        (deg_row, features),
    )
    if direct:
        blocks = [scaled] + [shifted(scaled, "row", row_shards, step) for step in range(1, row_shards)]
    else:
        blocks = [lax.all_gather(scaled, "row", axis=0, tiled=True)]
    masks = call(
        unpack_tiles,
        struct((slots, tile_size, tile_size), bf16),
        (tile_count, tile_bits, column),
        [SMEM, VMEM, pl.BlockSpec(memory_space=pl.ANY)],
        flops=1 << 28,
        moved=1 << 21,
    )
    indices = (me, tile_rows, tile_cols, masks)
    partial_value = call(
        forward_partial,
        struct((col_shards, size, width), bf16),
        indices + tuple(blocks),
        [SMEM] * 3 + [VMEM] * (1 + len(blocks)),
        [
            pltpu.VMEM((row_shards * size, width), bf16),
            pltpu.VMEM((col_shards * size, width), f32),
        ],
    )
    received = lax.all_to_all(partial_value, "col", 0, 0)
    halves = out_width // 128
    activations, back, local_grad = call(
        vertex_part,
        (
            struct((size, out_width), bf16),
            struct((col_shards, width, size), bf16),
            struct((halves, height, 128), f32),
        ),
        (received, column, deg_row, weight, cotangent),
    )
    gathered = lax.all_to_all(back, "col", 0, 0)
    scratch = [
        pltpu.VMEM((width, col_shards * size), bf16),
        pltpu.VMEM((width, row_shards * size), f32),
    ]
    if direct:
        piece_shapes = (struct((width, size), bf16),) * row_shards
    else:
        piece_shapes = (struct((row_shards, width, size), bf16),)
    pieces = call(
        backward_partial,
        piece_shapes,
        indices + (gathered,),
        [SMEM] * 3 + [VMEM] * 2,
        scratch,
    )
    if direct:
        arrived = [pieces[0]] + [
            shifted(pieces[step], "row", row_shards, step) for step in range(1, row_shards)
        ]
    else:
        arrived = [lax.all_to_all(pieces[0], "row", 0, 0)]
    input_grad = call(input_part, struct((size, width), bf16), (deg_row, *arrived))

    if height * out_width % (devices * 1024):
        whole = lax.psum(local_grad, AXES) * factor
    else:
        sent = lax.all_to_all(local_grad.reshape(devices, -1, 128), AXES, 0, 0)
        own = call(functools.partial(sum_pieces, factor), struct(sent.shape, f32), (sent,))
        whole = lax.all_to_all(own, AXES, 0, 0).reshape(halves, height, 128)
    weight_grad = call(join_halves, struct((height, out_width), f32), (whole,))
    return (activations, input_grad, weight_grad)


def solution(mesh):
    in_specs = (
        P(("row", "col"), None),
        P(("row", "col")),
        P(),
        P(("row", "col"), None),
        P("row", "col", None),
        P("row", "col", None),
        P("row", "col"),
        P("row", "col", None, None, None),
    )
    out_specs = (P(("row", "col"), None), P(("row", "col"), None), P())
    return jax.shard_map(
        on_device, mesh=mesh, in_specs=in_specs, out_specs=out_specs, check_vma=False
    )
```

```python
import functools
import math

import jax
import jax.numpy as jnp
from jax import lax
from jax.experimental import pallas as pl
from jax.experimental.pallas import tpu as pltpu
from jax.sharding import PartitionSpec as P

VMEM = pl.BlockSpec(memory_space=pltpu.VMEM)
ANY = pl.BlockSpec(memory_space=pl.ANY)
HBM = pl.BlockSpec(memory_space=pltpu.HBM)
SMEM = pl.BlockSpec(memory_space=pltpu.SMEM)
LIMIT = pltpu.CompilerParams(vmem_limit_bytes=40 * 1024 * 1024)
DIRECT = 4


def struct(shape, dtype):
    return jax.ShapeDtypeStruct(shape, dtype)


def call(body, out_shape, operands, specs=None, scratch=(), flops=1 << 20, moved=1 << 20):
    single = not isinstance(out_shape, (tuple, list))
    return pl.pallas_call(
        body,
        out_shape=out_shape,
        in_specs=specs or [VMEM] * len(operands),
        out_specs=VMEM if single else [VMEM] * len(out_shape),
        scratch_shapes=list(scratch),
        compiler_params=LIMIT,
        cost_estimate=pl.CostEstimate(flops=flops, bytes_accessed=moved, transcendentals=0),
    )(*operands)


def scale_features(deg_hbm, features_hbm, scaled_ref, column_ref, deg_ref, features_ref, sems):
    copies = [
        pltpu.make_async_copy(deg_hbm, deg_ref, sems.at[0]),
        pltpu.make_async_copy(features_hbm, features_ref, sems.at[1]),
    ]
    for copy in copies:
        copy.start()
    for copy in copies:
        copy.wait()
    size = features_ref.shape[0]
    scale_row = deg_ref[...].astype(jnp.float32)
    rows = lax.broadcasted_iota(jnp.int32, (size, size), 0)
    columns = lax.broadcasted_iota(jnp.int32, (size, size), 1)
    diagonal = jnp.where(rows == columns, scale_row, 0.0).astype(jnp.bfloat16)
    spread = jnp.dot(
        diagonal, jnp.ones((size, size), jnp.bfloat16), preferred_element_type=jnp.float32
    )
    column_ref[...] = spread
    scaled_ref[...] = (features_ref[...].astype(jnp.float32) * spread).astype(jnp.bfloat16)


def unpack_tiles(count_ref, bits_ref, after_ref, masks_ref):
    slots, words, tile_size = bits_ref.shape[2:]
    live_count = count_ref[0, 0]

    def one(slot):
        packed = jnp.where(slot < live_count, bits_ref[0, 0, slot], 0)
        repeated = jnp.broadcast_to(packed[:, None, :], (words, 8, tile_size))
        shifts = lax.broadcasted_iota(jnp.int32, (words, 8, tile_size), 1)
        bit_values = jnp.bitwise_and(jnp.right_shift(repeated, shifts), 1)
        masks_ref[slot] = (
            bit_values.reshape(words * 8, tile_size).astype(jnp.float32).astype(jnp.bfloat16)
        )

    each_slot(slots, one)


def each_slot(slots, one):
    if slots <= 8:
        for slot in range(slots):
            one(slot)
    else:
        pl.loop(0, slots)(one)


def forward_partial(me_ref, rows_ref, cols_ref, masks_ref, *refs):
    *blocks, partial_ref, source, total = refs
    slots, tile_size = masks_ref.shape[:2]
    place_blocks(me_ref, blocks, source)
    total[...] = jnp.zeros_like(total)

    def one(slot):
        place = pl.ds(pl.multiple_of(rows_ref[0, 0, slot] * tile_size, tile_size), tile_size)
        pick = pl.ds(pl.multiple_of(cols_ref[0, 0, slot] * tile_size, tile_size), tile_size)
        total[place, :] += jnp.dot(
            masks_ref[slot], source[pick, :], preferred_element_type=jnp.float32
        )

    each_slot(slots, one)
    partial_ref[...] = total[...].astype(jnp.bfloat16).reshape(partial_ref.shape)


def place_blocks(me_ref, blocks, source):
    if len(blocks) == 1:
        source[...] = blocks[0][...].reshape(source.shape)
        return
    shards, size = len(blocks), blocks[0].shape[0]
    for step, block in enumerate(blocks):
        owner = lax.rem(me_ref[0] + shards - step, shards)
        source[pl.ds(pl.multiple_of(owner * size, size), size), :] = block[...]


def vertex_part(received_ref, column_ref, deg_ref, weight_ref, cotangent_ref, act_ref, sent_ref):
    summed = jnp.sum(received_ref[...].astype(jnp.float32), axis=0)
    hidden = (summed * column_ref[...]).astype(jnp.bfloat16)
    weight = weight_ref[...]
    pre_act = jnp.dot(hidden, weight, preferred_element_type=jnp.float32)
    sigmoid_value = 1.0 / (1.0 + jnp.exp(-pre_act))
    act_ref[...] = (pre_act * sigmoid_value).astype(jnp.bfloat16)
    slope = sigmoid_value * (1.0 + pre_act * (1.0 - sigmoid_value))
    slope_term = (cotangent_ref[...].astype(jnp.float32) * slope).astype(jnp.bfloat16)
    spread = lax.dot_general(
        weight, slope_term, (((1,), (1,)), ((), ())), preferred_element_type=jnp.float32
    )
    back = (spread * deg_ref[...].astype(jnp.float32)).astype(jnp.bfloat16)
    local_grad = lax.dot_general(
        hidden, slope_term, (((0,), (0,)), ((), ())), preferred_element_type=jnp.float32
    ).astype(jnp.bfloat16)
    size = back.shape[1]
    halves = local_grad.shape[1] // size
    for peer in range(sent_ref.shape[0]):
        half = peer % halves
        sent_ref[peer, 0] = back
        sent_ref[peer, 1] = local_grad[:, half * size : (half + 1) * size]


def backward_partial(me_ref, rows_ref, cols_ref, masks_ref, gathered_ref, *refs):
    *pieces, source, total = refs
    slots, tile_size = masks_ref.shape[:2]
    shards, _, _, size = gathered_ref.shape
    for shard in range(shards):
        source[:, shard * size : (shard + 1) * size] = gathered_ref[shard, 0]
    total[...] = jnp.zeros_like(total)

    def one(slot):
        pick = pl.ds(pl.multiple_of(rows_ref[0, 0, slot] * tile_size, tile_size), tile_size)
        place = pl.ds(pl.multiple_of(cols_ref[0, 0, slot] * tile_size, tile_size), tile_size)
        total[:, place] += jnp.dot(
            source[:, pick], masks_ref[slot], preferred_element_type=jnp.float32
        )

    each_slot(slots, one)
    grad = jnp.sum(gathered_ref[:, 1].astype(jnp.float32), axis=0).astype(jnp.bfloat16)
    if len(pieces) == 1:
        for shard in range(pieces[0].shape[0]):
            pieces[0][shard, 0] = total[:, shard * size : (shard + 1) * size].astype(jnp.bfloat16)
            pieces[0][shard, 1] = grad
        return
    for step, piece in enumerate(pieces):
        owner = lax.rem(me_ref[0] + step, len(pieces))
        place = pl.ds(pl.multiple_of(owner * size, size), size)
        piece[0] = total[:, place].astype(jnp.bfloat16)
        piece[1] = grad


def sum_grad(factor, me_ref, *refs):
    *pieces, out_ref, ordered = refs
    if len(pieces) == 1:
        out_ref[...] = jnp.sum(pieces[0][:, 1].astype(jnp.float32), axis=0) * factor
        return
    shards = len(pieces)
    for step, piece in enumerate(pieces):
        ordered[lax.rem(me_ref[0] + shards - step, shards)] = piece[1]
    out_ref[...] = jnp.sum(ordered[...].astype(jnp.float32), axis=0) * factor


def input_part(deg_ref, *refs):
    *pieces, out_ref = refs
    if len(pieces) == 1:
        total = jnp.sum(pieces[0][:, 0].astype(jnp.float32), axis=0)
    else:
        total = sum(piece[0].astype(jnp.float32) for piece in pieces)
    out_ref[...] = (total * deg_ref[...].astype(jnp.float32)).T.astype(jnp.bfloat16)


def join_halves(half_ref, own_ref, other_ref, out_ref):
    size = own_ref.shape[1]
    half = half_ref[0]
    out_ref[:, pl.ds(pl.multiple_of(half * size, size), size)] = own_ref[...]
    out_ref[:, pl.ds(pl.multiple_of((1 - half) * size, size), size)] = other_ref[...]


def shifted(block, axis, shards, step):
    return lax.ppermute(block, axis, [(source, (source + step) % shards) for source in range(shards)])


def on_device(features, deg_scale, weight, cotangent, tile_rows, tile_cols, tile_count, tile_bits):
    size, width = features.shape
    height, out_width = weight.shape
    row_shards = lax.axis_size("row")
    col_shards = lax.axis_size("col")
    devices = row_shards * col_shards
    total_verts = devices * size
    slots, words, tile_size = tile_bits.shape[2:]
    direct = row_shards <= DIRECT
    bf16, f32 = jnp.bfloat16, jnp.float32
    me = lax.axis_index("row").astype(jnp.int32).reshape(1)
    deg_row = deg_scale.reshape(1, size)
    factor = 1.0 / math.sqrt(total_verts)

    scaled, column = call(
        scale_features,
        (struct((size, width), bf16), struct((size, width), f32)),
        (deg_row, features),
        [HBM] * 2,
        [
            pltpu.VMEM((1, size), bf16),
            pltpu.VMEM((size, width), bf16),
            pltpu.SemaphoreType.DMA((2,)),
        ],
    )
    if direct:
        blocks = [scaled] + [shifted(scaled, "row", row_shards, step) for step in range(1, row_shards)]
    else:
        blocks = [lax.all_gather(scaled, "row", axis=0, tiled=True)]
    masks = call(
        unpack_tiles,
        struct((slots, tile_size, tile_size), bf16),
        (tile_count, tile_bits, column),
        [SMEM, VMEM, ANY],
        flops=1 << 28,
        moved=1 << 21,
    )
    indices = (me, tile_rows, tile_cols, masks)
    partial_value = call(
        forward_partial,
        struct((col_shards, size, width), bf16),
        indices + tuple(blocks),
        [SMEM] * 3 + [VMEM] * (1 + len(blocks)),
        [
            pltpu.VMEM((row_shards * size, width), bf16),
            pltpu.VMEM((col_shards * size, width), f32),
        ],
    )
    received = lax.all_to_all(partial_value, "col", 0, 0)
    activations, sent = call(
        vertex_part,
        (
            struct((size, out_width), bf16),
            struct((col_shards, 2, width, size), bf16),
        ),
        (received, column, deg_row, weight, cotangent),
    )
    gathered = lax.all_to_all(sent, "col", 0, 0)
    scratch = [
        pltpu.VMEM((width, col_shards * size), bf16),
        pltpu.VMEM((width, row_shards * size), f32),
    ]
    if direct:
        piece_shapes = (struct((2, width, size), bf16),) * row_shards
    else:
        piece_shapes = (struct((row_shards, 2, width, size), bf16),)
    pieces = call(
        backward_partial,
        piece_shapes,
        indices + (gathered,),
        [SMEM] * 3 + [VMEM] * 2,
        scratch,
    )
    if direct:
        arrived = [pieces[0]] + [
            shifted(pieces[step], "row", row_shards, step) for step in range(1, row_shards)
        ]
    else:
        arrived = [lax.all_to_all(pieces[0], "row", 0, 0)]
    half_grad = call(
        functools.partial(sum_grad, factor),
        struct((height, size), f32),
        (me, *arrived),
        [SMEM] + [VMEM] * len(arrived),
        [pltpu.VMEM((row_shards, height, size), bf16)],
    )
    pairs = [(shard, shard + 1 - 2 * (shard % 2)) for shard in range(col_shards)]
    other_grad = lax.ppermute(half_grad, "col", pairs)
    input_grad = call(input_part, struct((size, width), bf16), (deg_row, *arrived))
    core = jnp.mod(lax.axis_index("col"), 2).astype(jnp.int32).reshape(1)
    weight_grad = call(
        join_halves,
        struct((height, out_width), f32),
        (core, half_grad, other_grad),
        [SMEM] + [VMEM] * 2,
    )
    return (activations, input_grad, weight_grad)


def solution(mesh):
    in_specs = (
        P(("row", "col"), None),
        P(("row", "col")),
        P(),
        P(("row", "col"), None),
        P("row", "col", None),
        P("row", "col", None),
        P("row", "col"),
        P("row", "col", None, None, None),
    )
    out_specs = (P(("row", "col"), None), P(("row", "col"), None), P())
    return jax.shard_map(
        on_device, mesh=mesh, in_specs=in_specs, out_specs=out_specs, check_vma=False
    )
```

```python
import functools
import math

import jax
import jax.numpy as jnp
from jax import lax
from jax.experimental import pallas as pl
from jax.experimental.pallas import tpu as pltpu
from jax.sharding import PartitionSpec as P

VMEM = pl.BlockSpec(memory_space=pltpu.VMEM)
SMEM = pl.BlockSpec(memory_space=pltpu.SMEM)
ANY = pl.BlockSpec(memory_space=pl.ANY)
LIMIT = pltpu.CompilerParams(vmem_limit_bytes=40 * 1024 * 1024)
FIRST_FLOPS = 1 << 32
bf16, f32 = jnp.bfloat16, jnp.float32


def struct(shape, dtype):
    return jax.ShapeDtypeStruct(shape, dtype)


def call(body, out_shape, scalars, operands, scratch=(), flops=1 << 20, after=()):
    single = not isinstance(out_shape, (tuple, list))
    return pl.pallas_call(
        body,
        out_shape=out_shape,
        in_specs=[SMEM] * len(scalars) + [VMEM] * len(operands) + [ANY] * len(after),
        out_specs=VMEM if single else [VMEM] * len(out_shape),
        scratch_shapes=list(scratch),
        compiler_params=LIMIT,
        cost_estimate=pl.CostEstimate(flops=flops, bytes_accessed=1 << 20, transcendentals=0),
    )(*scalars, *operands, *after)


def block_at(index, size):
    return pl.ds(pl.multiple_of(index * size, size), size)


def unpack_tiles(count_ref, bits_ref, deg_ref, features_ref, scaled_ref, column_ref, masks_ref):
    column = spread_scale(deg_ref[...], column_ref.shape[0])
    column_ref[...] = column
    scaled_ref[...] = (features_ref[...].astype(f32) * column).astype(bf16)

    def one(slot):
        masks_ref[slot] = unpacked(jnp.where(slot < count_ref[0, 0], bits_ref[0, 0, slot], 0))

    pl.loop(0, masks_ref.shape[0])(one)


def forward_total(rows_ref, cols_ref, masks_ref, source, total):
    slots, tile_size = masks_ref.shape[:2]
    total[...] = jnp.zeros_like(total)

    def one(slot):
        place = block_at(rows_ref[0, 0, slot], tile_size)
        pick = block_at(cols_ref[0, 0, slot], tile_size)
        total[place, :] += jnp.dot(masks_ref[slot], source[pick, :], preferred_element_type=f32)

    pl.loop(0, slots)(one)


def backward_total(rows_ref, cols_ref, masks_ref, source, total):
    slots, tile_size = masks_ref.shape[:2]
    total[...] = jnp.zeros_like(total)

    def one(slot):
        pick = block_at(rows_ref[0, 0, slot], tile_size)
        place = block_at(cols_ref[0, 0, slot], tile_size)
        total[:, place] += jnp.dot(source[:, pick], masks_ref[slot], preferred_element_type=f32)

    pl.loop(0, slots)(one)


def unpacked(packed):
    words, tile_size = packed.shape
    repeated = jnp.broadcast_to(packed[:, None, :], (words, 8, tile_size))
    shifts = lax.broadcasted_iota(jnp.int32, (words, 8, tile_size), 1)
    bit_values = jnp.bitwise_and(jnp.right_shift(repeated, shifts), 1)
    return bit_values.reshape(words * 8, tile_size).astype(f32).astype(bf16)


def spread_scale(deg, size):
    rows = lax.broadcasted_iota(jnp.int32, (size, size), 0)
    columns = lax.broadcasted_iota(jnp.int32, (size, size), 1)
    diagonal = jnp.where(rows == columns, deg.astype(f32).reshape(1, size), 0.0).astype(bf16)
    return jnp.dot(diagonal, jnp.ones((size, size), bf16), preferred_element_type=f32)


def scale_column(deg_ref, column_ref):
    column_ref[...] = spread_scale(deg_ref[...], column_ref.shape[0])


def scale_rows(column_ref, features_ref, rows_ref, cols_ref, scaled_ref):
    scaled_ref[...] = (features_ref[...].astype(f32) * column_ref[...]).astype(bf16)


def build_adjacency(count_ref, rows_ref, cols_ref, bits_ref, after_ref, adjacency_ref):
    slots, words, tile_size = bits_ref.shape[2:]
    count = count_ref[0, 0]
    for slot in range(slots):
        packed = jnp.where(slot < count, bits_ref[0, 0, slot], 0)
        place = block_at(rows_ref[0, 0, slot], tile_size), block_at(cols_ref[0, 0, slot], tile_size)
        adjacency_ref[place] = unpacked(packed)


def forward_pair(row_ref, core_ref, adjacency_ref, *refs):
    *blocks, mine_ref, other_ref, source, total = refs
    size = blocks[0].shape[0]
    for step, block in enumerate(blocks):
        source[block_at(row_ref[0] ^ step, size), :] = block[...]
    total[...] = jnp.dot(adjacency_ref[...], source[...], preferred_element_type=f32)
    core = core_ref[0]
    for chip in range(mine_ref.shape[0]):
        mine_ref[chip] = total[block_at(2 * chip + core, size), :]
        other_ref[chip] = total[block_at(2 * chip + 1 - core, size), :].astype(bf16)


def forward_chips(chip_ref, mine_ref, received_ref, own_ref, *pieces):
    chip = chip_ref[0]
    own_ref[...] = mine_ref[chip] + received_ref[chip].astype(f32)
    for step, piece in zip((3, 2, 1), pieces):
        peer = chip ^ step
        piece[...] = (mine_ref[peer] + received_ref[peer].astype(f32)).astype(bf16)


def vertex_values(summed, column_ref, deg_ref, weight_ref, cotangent_ref):
    hidden = (summed * column_ref[...]).astype(bf16)
    weight = weight_ref[...]
    pre_act = jnp.dot(hidden, weight, preferred_element_type=f32)
    sigmoid_value = 1.0 / (1.0 + jnp.exp(-pre_act))
    slope = sigmoid_value * (1.0 + pre_act * (1.0 - sigmoid_value))
    slope_term = (cotangent_ref[...].astype(f32) * slope).astype(bf16)
    spread = lax.dot_general(
        weight, slope_term, (((1,), (1,)), ((), ())), preferred_element_type=f32
    )
    back = (spread * deg_ref[...].astype(f32).reshape(1, -1)).astype(bf16)
    local_grad = lax.dot_general(
        hidden, slope_term, (((0,), (0,)), ((), ())), preferred_element_type=f32
    )
    return back, local_grad, pre_act * sigmoid_value


def vertex_chips(column_ref, deg_ref, weight_ref, cotangent_ref, own_ref, *refs):
    *received, sent_ref, active_ref = refs
    summed = own_ref[...] + sum(piece[...].astype(f32) for piece in received)
    sent_ref[0], local_grad, active_ref[...] = vertex_values(
        summed, column_ref, deg_ref, weight_ref, cotangent_ref
    )
    half = sent_ref.shape[2]
    for core in range(2):
        sent_ref[1 + core] = local_grad[:, core * half : (core + 1) * half].astype(bf16)


def write_out(active_ref, out_ref, written_ref):
    out_ref[...] = active_ref[...].astype(bf16)
    written_ref[...] = jnp.zeros_like(written_ref)


def join_chips(chip_ref, core_ref, *refs):
    *blocks, _, joined_ref, own_grad_ref, ordered = refs
    chips = len(blocks)
    for step, block in enumerate(blocks):
        joined_ref[step] = block[0]
        ordered[chip_ref[0] ^ step] = block[1:]
    grad = jnp.sum(ordered[...].astype(f32), axis=0).astype(bf16)
    second = core_ref[0] == 1
    own_grad_ref[...] = jnp.where(second, grad[1], grad[0])
    joined_ref[chips] = jnp.where(second, grad[0], grad[1])


def backward_rows(row_ref, chip_ref, core_ref, adjacency_ref, own_ref, grad_ref, received_ref, *refs):
    *pieces, source, total = refs
    chips = own_ref.shape[0] - 1
    size = own_ref.shape[2]
    chip, core = chip_ref[0], core_ref[0]
    for step in range(chips):
        peer = 2 * (chip ^ step)
        source[:, block_at(peer + core, size)] = own_ref[step]
        source[:, block_at(peer + 1 - core, size)] = received_ref[step]
    total[...] = jnp.dot(source[...], adjacency_ref[...], preferred_element_type=f32)
    grad = (grad_ref[...].astype(f32) + received_ref[chips].astype(f32)).astype(bf16)
    for step, piece in zip((3, 2, 1, 0), pieces):
        piece[0] = total[:, block_at(row_ref[0] ^ step, size)].astype(bf16)
        piece[1] = grad


def sum_grad(factor, row_ref, *refs):
    *pieces, out_ref, ordered = refs
    for step, piece in zip((3, 2, 1, 0), pieces):
        ordered[row_ref[0] ^ step] = piece[1]
    total = jnp.sum(ordered[...].astype(f32), axis=0) * factor
    out_ref[...] = total.astype(out_ref.dtype)


def input_rows(deg_ref, *refs):
    *pieces, out_ref = refs
    total = sum(piece[0].astype(f32) for piece in pieces)
    out_ref[...] = (total * deg_ref[...].astype(f32).reshape(1, -1)).T.astype(bf16)


def join_halves(core_ref, own_ref, other_ref, out_ref):
    size = own_ref.shape[1]
    half = core_ref[0]
    out_ref[:, block_at(half, size)] = own_ref[...].astype(f32)
    out_ref[:, block_at(1 - half, size)] = other_ref[...].astype(f32)


def forward_all(rows_ref, cols_ref, masks_ref, source_ref, partial_ref, total):
    forward_total(rows_ref, cols_ref, masks_ref, source_ref, total)
    partial_ref[...] = total[...].astype(bf16).reshape(partial_ref.shape)


def vertex_all(column_ref, deg_ref, weight_ref, cotangent_ref, received_ref, act_ref, back_ref, grad_ref):
    summed = jnp.sum(received_ref[...].astype(f32), axis=0)
    back_ref[...], grad_ref[...], active = vertex_values(
        summed, column_ref, deg_ref, weight_ref, cotangent_ref
    )
    act_ref[...] = active.astype(bf16)


def backward_all(rows_ref, cols_ref, masks_ref, gathered_ref, pieces_ref, source, total):
    size = gathered_ref.shape[2]
    for shard in range(gathered_ref.shape[0]):
        source[:, shard * size : (shard + 1) * size] = gathered_ref[shard]
    backward_total(rows_ref, cols_ref, masks_ref, source, total)
    for shard in range(pieces_ref.shape[0]):
        pieces_ref[shard] = total[:, shard * size : (shard + 1) * size].astype(bf16)


def input_all(deg_ref, pieces_ref, out_ref):
    total = jnp.sum(pieces_ref[...].astype(f32), axis=0)
    out_ref[...] = (total * deg_ref[...].astype(f32).reshape(1, -1)).T.astype(bf16)


def exchange(block, axis, shards, distance):
    return lax.ppermute(block, axis, [(shard, shard ^ distance) for shard in range(shards)])


def on_device(features, deg_scale, weight, cotangent, tile_rows, tile_cols, tile_count, tile_bits):
    size, width = features.shape
    height, out_width = weight.shape
    row_shards = lax.axis_size("row")
    col_shards = lax.axis_size("col")
    chips = col_shards // 2
    slots, words, tile_size = tile_bits.shape[2:]
    factor = 1.0 / math.sqrt(row_shards * col_shards * size)
    row = lax.axis_index("row").astype(jnp.int32).reshape(1)
    col = lax.axis_index("col").astype(jnp.int32)
    chip, core = (col // 2).reshape(1), (col % 2).reshape(1)
    forward_scratch = [pltpu.VMEM((col_shards * size, width), f32)]
    backward_scratch = [
        pltpu.VMEM((width, col_shards * size), bf16),
        pltpu.VMEM((width, row_shards * size), f32),
    ]
    prepared = (struct((size, width), bf16), struct((size, width), f32))
    block = struct((width, size), bf16)
    activation = struct((size, out_width), bf16)
    input_shape = struct((size, width), bf16)

    covered = slots * tile_size * tile_size == row_shards * col_shards * size * size
    if row_shards != 4 or col_shards != 8 or not covered:
        scaled, column, masks = call(
            unpack_tiles,
            prepared + (struct((slots, tile_size, tile_size), bf16),),
            (tile_count,),
            (tile_bits, deg_scale, features),
        )
        gathered = lax.all_gather(scaled, "row", axis=0, tiled=True)
        partial_value = call(
            forward_all,
            struct((col_shards, size, width), bf16),
            (tile_rows, tile_cols),
            (masks, gathered),
            forward_scratch,
        )
        received = lax.all_to_all(partial_value, "col", 0, 0)
        activations, back, local_grad = call(
            vertex_all,
            (activation, block, struct((height, out_width), f32)),
            (),
            (column, deg_scale, weight, cotangent, received),
        )
        weight_grad = lax.psum(local_grad, ("row", "col")) * factor
        pieces = call(
            backward_all,
            struct((row_shards, width, size), bf16),
            (tile_rows, tile_cols),
            (masks, lax.all_gather(back, "col")),
            backward_scratch,
        )
        arrived = lax.all_to_all(pieces, "row", 0, 0)
        input_grad = call(input_all, input_shape, (), (deg_scale, arrived))
        return (activations, input_grad, weight_grad)

    column = call(
        scale_column, struct((size, width), f32), (), (deg_scale,), flops=FIRST_FLOPS
    )
    scaled = call(scale_rows, struct((size, width), bf16), (), (column, features, tile_rows, tile_cols))
    adjacency = pl.pallas_call(
        build_adjacency,
        out_shape=struct((col_shards * size, row_shards * size), bf16),
        in_specs=[SMEM, SMEM, SMEM, VMEM, ANY],
        out_specs=VMEM,
        compiler_params=LIMIT,
        cost_estimate=pl.CostEstimate(flops=1 << 20, bytes_accessed=1 << 20, transcendentals=0),
    )(tile_count, tile_rows, tile_cols, tile_bits, scaled)
    far_first = (3, 2, 1)
    blocks = [exchange(scaled, "row", row_shards, step) for step in (1, 2, 3)]
    blocks.insert(0, scaled)
    mine, other = call(
        forward_pair,
        (struct((chips, size, width), f32), struct((chips, size, width), bf16)),
        (row, core),
        (adjacency, *blocks),
        [pltpu.VMEM((row_shards * size, width), bf16)] + forward_scratch,
    )
    own, *pieces = call(
        forward_chips,
        (struct((size, width), f32),) + (struct((size, width), bf16),) * len(far_first),
        (chip,),
        (mine, exchange(other, "col", col_shards, 1)),
    )
    received = [
        exchange(piece, "col", col_shards, 2 * step) for step, piece in zip(far_first, pieces)
    ]
    sent, active = call(
        vertex_chips,
        (struct((3, width, size), bf16), struct((size, out_width), f32)),
        (),
        (column, deg_scale, weight, cotangent, own, *received),
    )
    activations, written = call(write_out, (activation, struct((8, 128), f32)), (), (active,))
    received = [exchange(sent, "col", col_shards, 2 * step) for step in (1, 2, 3)]
    joined, own_grad = call(
        join_chips,
        (struct((chips + 1, width, size), bf16), struct((width, size), bf16)),
        (chip, core),
        (sent, *received),
        [pltpu.VMEM((chips, 2, width, size), bf16)],
        after=(written,),
    )
    pieces = call(
        backward_rows,
        (struct((2, width, size), bf16),) * row_shards,
        (row, chip, core),
        (adjacency, joined, own_grad, exchange(joined, "col", col_shards, 1)),
        backward_scratch,
    )
    arrived = [exchange(piece, "row", row_shards, step) for step, piece in zip(far_first, pieces)]
    arrived.append(pieces[-1])
    half_grad = call(
        functools.partial(sum_grad, factor),
        struct((height, out_width // 2), bf16),
        (row,),
        arrived,
        [pltpu.VMEM((row_shards, height, out_width // 2), bf16)],
    )
    other_grad = exchange(half_grad, "col", col_shards, 1)
    input_grad = call(input_rows, input_shape, (), (deg_scale, *arrived))
    weight_grad = call(
        join_halves, struct((height, out_width), f32), (core,), (half_grad, other_grad)
    )
    return (activations, input_grad, weight_grad)


def solution(mesh):
    in_specs = (
        P(("row", "col"), None),
        P(("row", "col")),
        P(),
        P(("row", "col"), None),
        P("row", "col", None),
        P("row", "col", None),
        P("row", "col"),
        P("row", "col", None, None, None),
    )
    out_specs = (P(("row", "col"), None), P(("row", "col"), None), P())
    return jax.shard_map(
        on_device, mesh=mesh, in_specs=in_specs, out_specs=out_specs, check_vma=False
    )
```

```python
import functools
import math

import jax
import jax.numpy as jnp
from jax import lax
from jax.experimental import pallas as pl
from jax.experimental.pallas import tpu as pltpu
from jax.sharding import PartitionSpec as P

VMEM = pl.BlockSpec(memory_space=pltpu.VMEM)
SMEM = pl.BlockSpec(memory_space=pltpu.SMEM)
ANY = pl.BlockSpec(memory_space=pl.ANY)
LIMIT = pltpu.CompilerParams(vmem_limit_bytes=40 * 1024 * 1024)
FIRST_FLOPS = 1 << 32
bf16, f32 = jnp.bfloat16, jnp.float32


def struct(shape, dtype):
    return jax.ShapeDtypeStruct(shape, dtype)


def call(body, out_shape, scalars, operands, scratch=(), flops=1 << 20, after=()):
    single = not isinstance(out_shape, (tuple, list))
    return pl.pallas_call(
        body,
        out_shape=out_shape,
        in_specs=[SMEM] * len(scalars) + [VMEM] * len(operands) + [ANY] * len(after),
        out_specs=VMEM if single else [VMEM] * len(out_shape),
        scratch_shapes=list(scratch),
        compiler_params=LIMIT,
        cost_estimate=pl.CostEstimate(flops=flops, bytes_accessed=1 << 20, transcendentals=0),
    )(*scalars, *operands, *after)


def block_at(index, size):
    return pl.ds(pl.multiple_of(index * size, size), size)


def unpack_tiles(count_ref, bits_ref, deg_ref, features_ref, scaled_ref, column_ref, masks_ref):
    column = spread_scale(deg_ref[...], column_ref.shape[0])
    column_ref[...] = column
    scaled_ref[...] = (features_ref[...].astype(f32) * column).astype(bf16)

    def one(slot):
        masks_ref[slot] = unpacked(jnp.where(slot < count_ref[0, 0], bits_ref[0, 0, slot], 0))

    pl.loop(0, masks_ref.shape[0])(one)


def forward_total(rows_ref, cols_ref, masks_ref, source, total):
    slots, tile_size = masks_ref.shape[:2]
    total[...] = jnp.zeros_like(total)

    def one(slot):
        place = block_at(rows_ref[0, 0, slot], tile_size)
        pick = block_at(cols_ref[0, 0, slot], tile_size)
        total[place, :] += jnp.dot(masks_ref[slot], source[pick, :], preferred_element_type=f32)

    pl.loop(0, slots)(one)


def backward_total(rows_ref, cols_ref, masks_ref, source, total):
    slots, tile_size = masks_ref.shape[:2]
    total[...] = jnp.zeros_like(total)

    def one(slot):
        pick = block_at(rows_ref[0, 0, slot], tile_size)
        place = block_at(cols_ref[0, 0, slot], tile_size)
        total[:, place] += jnp.dot(source[:, pick], masks_ref[slot], preferred_element_type=f32)

    pl.loop(0, slots)(one)


def unpacked(packed):
    words, tile_size = packed.shape
    repeated = jnp.broadcast_to(packed[:, None, :], (words, 8, tile_size))
    shifts = lax.broadcasted_iota(jnp.int32, (words, 8, tile_size), 1)
    bit_values = jnp.bitwise_and(jnp.right_shift(repeated, shifts), 1)
    return bit_values.reshape(words * 8, tile_size).astype(f32).astype(bf16)


def spread_scale(deg, size):
    rows = lax.broadcasted_iota(jnp.int32, (size, size), 0)
    columns = lax.broadcasted_iota(jnp.int32, (size, size), 1)
    diagonal = jnp.where(rows == columns, deg.astype(f32).reshape(1, size), 0.0).astype(bf16)
    return jnp.dot(diagonal, jnp.ones((size, size), bf16), preferred_element_type=f32)


def scale_column(deg_ref, column_ref):
    column_ref[...] = spread_scale(deg_ref[...], column_ref.shape[0])


def scale_rows(column_ref, features_ref, rows_ref, cols_ref, scaled_ref):
    scaled_ref[...] = (features_ref[...].astype(f32) * column_ref[...]).astype(bf16)


def build_adjacency(count_ref, rows_ref, cols_ref, bits_ref, after_ref, adjacency_ref):
    slots, words, tile_size = bits_ref.shape[2:]
    count = count_ref[0, 0]
    for slot in range(slots):
        packed = jnp.where(slot < count, bits_ref[0, 0, slot], 0)
        place = block_at(rows_ref[0, 0, slot], tile_size), block_at(cols_ref[0, 0, slot], tile_size)
        adjacency_ref[place] = unpacked(packed)


def forward_pair(row_ref, chip_ref, core_ref, adjacency_ref, *refs):
    *blocks, mine_ref, other_ref, source, total = refs
    size = blocks[0].shape[0]
    for step, block in enumerate(blocks):
        source[block_at(row_ref[0] ^ step, size), :] = block[...]
    total[...] = jnp.dot(adjacency_ref[...], source[...], preferred_element_type=f32)
    for chip in range(mine_ref.shape[0]):
        kept = jnp.where(chip == chip_ref[0], core_ref[0], 1 - core_ref[0])
        mine_ref[chip] = total[block_at(2 * chip + kept, size), :]
        other_ref[chip] = total[block_at(2 * chip + 1 - kept, size), :].astype(bf16)


def forward_chips(chip_ref, mine_ref, received_ref, own_ref, *pieces):
    chip = chip_ref[0]
    own_ref[...] = mine_ref[chip] + received_ref[chip].astype(f32)
    for step, piece in zip((3, 2, 1), pieces):
        peer = chip ^ step
        piece[...] = (mine_ref[peer] + received_ref[peer].astype(f32)).astype(bf16)


def vertex_values(summed, column_ref, deg_ref, weight_ref, cotangent_ref):
    hidden = (summed * column_ref[...]).astype(bf16)
    weight = weight_ref[...]
    pre_act = jnp.dot(hidden, weight, preferred_element_type=f32)
    sigmoid_value = 1.0 / (1.0 + jnp.exp(-pre_act))
    slope = sigmoid_value * (1.0 + pre_act * (1.0 - sigmoid_value))
    slope_term = (cotangent_ref[...].astype(f32) * slope).astype(bf16)
    spread = lax.dot_general(
        weight, slope_term, (((1,), (1,)), ((), ())), preferred_element_type=f32
    )
    back = (spread * deg_ref[...].astype(f32).reshape(1, -1)).astype(bf16)
    local_grad = lax.dot_general(
        hidden, slope_term, (((0,), (0,)), ((), ())), preferred_element_type=f32
    )
    return back, local_grad, pre_act * sigmoid_value


def vertex_chips(column_ref, deg_ref, weight_ref, cotangent_ref, own_ref, *refs):
    *received, sent_ref, active_ref = refs
    summed = own_ref[...] + sum(piece[...].astype(f32) for piece in received)
    sent_ref[0], local_grad, active_ref[...] = vertex_values(
        summed, column_ref, deg_ref, weight_ref, cotangent_ref
    )
    half = sent_ref.shape[2]
    for core in range(2):
        sent_ref[1 + core] = local_grad[:, core * half : (core + 1) * half].astype(bf16)


def write_out(active_ref, out_ref, written_ref):
    out_ref[...] = active_ref[...].astype(bf16)
    written_ref[...] = jnp.zeros_like(written_ref)


def join_chips(core_ref, *refs):
    *blocks, _, joined_ref, own_grad_ref = refs
    chips = len(blocks)
    second = core_ref[0] == 1
    for step, block in enumerate(blocks):
        joined_ref[step] = block[0]
        joined_ref[chips + step] = jnp.where(second, block[1], block[2])
        own_grad_ref[step] = jnp.where(second, block[2], block[1])


def backward_rows(row_ref, chip_ref, core_ref, adjacency_ref, own_ref, grad_ref, received_ref, *refs):
    *pieces, source, ordered, total = refs
    chips, size = grad_ref.shape[0], grad_ref.shape[2]
    core = core_ref[0]
    for step in range(chips):
        peer = 2 * (chip_ref[0] ^ step)
        mine = peer + (1 - core if step else core)
        other = peer + (core if step else 1 - core)
        source[:, block_at(mine, size)] = own_ref[step]
        source[:, block_at(other, size)] = received_ref[step]
        ordered[mine] = grad_ref[step]
        ordered[other] = received_ref[chips + step]
    total[...] = jnp.dot(source[...], adjacency_ref[...], preferred_element_type=f32)
    grad = jnp.sum(ordered[...].astype(f32), axis=0).astype(bf16)
    for step, piece in zip((3, 2, 1, 0), pieces):
        piece[0] = total[:, block_at(row_ref[0] ^ step, size)].astype(bf16)
        piece[1] = grad


def sum_grad(factor, row_ref, *refs):
    *pieces, out_ref, ordered = refs
    for step, piece in zip((3, 2, 1, 0), pieces):
        ordered[row_ref[0] ^ step] = piece[1]
    total = jnp.sum(ordered[...].astype(f32), axis=0) * factor
    out_ref[...] = total.astype(out_ref.dtype)


def input_rows(deg_ref, *refs):
    *pieces, out_ref = refs
    total = sum(piece[0].astype(f32) for piece in pieces)
    out_ref[...] = (total * deg_ref[...].astype(f32).reshape(1, -1)).T.astype(bf16)


def join_halves(core_ref, own_ref, other_ref, out_ref):
    size = own_ref.shape[1]
    half = core_ref[0]
    out_ref[:, block_at(half, size)] = own_ref[...].astype(f32)
    out_ref[:, block_at(1 - half, size)] = other_ref[...].astype(f32)


def forward_all(rows_ref, cols_ref, masks_ref, source_ref, partial_ref, total):
    forward_total(rows_ref, cols_ref, masks_ref, source_ref, total)
    partial_ref[...] = total[...].astype(bf16).reshape(partial_ref.shape)


def vertex_all(column_ref, deg_ref, weight_ref, cotangent_ref, received_ref, act_ref, back_ref, grad_ref):
    summed = jnp.sum(received_ref[...].astype(f32), axis=0)
    back_ref[...], grad_ref[...], active = vertex_values(
        summed, column_ref, deg_ref, weight_ref, cotangent_ref
    )
    act_ref[...] = active.astype(bf16)


def backward_all(rows_ref, cols_ref, masks_ref, gathered_ref, pieces_ref, source, total):
    size = gathered_ref.shape[2]
    for shard in range(gathered_ref.shape[0]):
        source[:, shard * size : (shard + 1) * size] = gathered_ref[shard]
    backward_total(rows_ref, cols_ref, masks_ref, source, total)
    for shard in range(pieces_ref.shape[0]):
        pieces_ref[shard] = total[:, shard * size : (shard + 1) * size].astype(bf16)


def input_all(deg_ref, pieces_ref, out_ref):
    total = jnp.sum(pieces_ref[...].astype(f32), axis=0)
    out_ref[...] = (total * deg_ref[...].astype(f32).reshape(1, -1)).T.astype(bf16)


def exchange(block, axis, shards, distance):
    return lax.ppermute(block, axis, [(shard, shard ^ distance) for shard in range(shards)])


def on_device(features, deg_scale, weight, cotangent, tile_rows, tile_cols, tile_count, tile_bits):
    size, width = features.shape
    height, out_width = weight.shape
    row_shards = lax.axis_size("row")
    col_shards = lax.axis_size("col")
    chips = col_shards // 2
    slots, words, tile_size = tile_bits.shape[2:]
    factor = 1.0 / math.sqrt(row_shards * col_shards * size)
    row = lax.axis_index("row").astype(jnp.int32).reshape(1)
    col = lax.axis_index("col").astype(jnp.int32)
    chip, core = (col // 2).reshape(1), (col % 2).reshape(1)
    forward_scratch = [pltpu.VMEM((col_shards * size, width), f32)]
    backward_scratch = [
        pltpu.VMEM((width, col_shards * size), bf16),
        pltpu.VMEM((width, row_shards * size), f32),
    ]
    prepared = (struct((size, width), bf16), struct((size, width), f32))
    block = struct((width, size), bf16)
    activation = struct((size, out_width), bf16)
    input_shape = struct((size, width), bf16)

    covered = slots * tile_size * tile_size == row_shards * col_shards * size * size
    if row_shards != 4 or col_shards != 8 or not covered:
        scaled, column, masks = call(
            unpack_tiles,
            prepared + (struct((slots, tile_size, tile_size), bf16),),
            (tile_count,),
            (tile_bits, deg_scale, features),
        )
        gathered = lax.all_gather(scaled, "row", axis=0, tiled=True)
        partial_value = call(
            forward_all,
            struct((col_shards, size, width), bf16),
            (tile_rows, tile_cols),
            (masks, gathered),
            forward_scratch,
        )
        received = lax.all_to_all(partial_value, "col", 0, 0)
        activations, back, local_grad = call(
            vertex_all,
            (activation, block, struct((height, out_width), f32)),
            (),
            (column, deg_scale, weight, cotangent, received),
        )
        weight_grad = lax.psum(local_grad, ("row", "col")) * factor
        pieces = call(
            backward_all,
            struct((row_shards, width, size), bf16),
            (tile_rows, tile_cols),
            (masks, lax.all_gather(back, "col")),
            backward_scratch,
        )
        arrived = lax.all_to_all(pieces, "row", 0, 0)
        input_grad = call(input_all, input_shape, (), (deg_scale, arrived))
        return (activations, input_grad, weight_grad)

    column = call(
        scale_column, struct((size, width), f32), (), (deg_scale,), flops=FIRST_FLOPS
    )
    scaled = call(scale_rows, struct((size, width), bf16), (), (column, features, tile_rows, tile_cols))
    adjacency = pl.pallas_call(
        build_adjacency,
        out_shape=struct((col_shards * size, row_shards * size), bf16),
        in_specs=[SMEM, SMEM, SMEM, VMEM, ANY],
        out_specs=VMEM,
        compiler_params=LIMIT,
        cost_estimate=pl.CostEstimate(flops=1 << 20, bytes_accessed=1 << 20, transcendentals=0),
    )(tile_count, tile_rows, tile_cols, tile_bits, scaled)
    far_first = (3, 2, 1)
    blocks = [exchange(scaled, "row", row_shards, step) for step in (1, 2, 3)]
    blocks.insert(0, scaled)
    mine, other = call(
        forward_pair,
        (struct((chips, size, width), f32), struct((chips, size, width), bf16)),
        (row, chip, core),
        (adjacency, *blocks),
        [pltpu.VMEM((row_shards * size, width), bf16)] + forward_scratch,
    )
    own, *pieces = call(
        forward_chips,
        (struct((size, width), f32),) + (struct((size, width), bf16),) * len(far_first),
        (chip,),
        (mine, exchange(other, "col", col_shards, 1)),
    )
    received = [
        exchange(piece, "col", col_shards, 2 * step + 1) for step, piece in zip(far_first, pieces)
    ]
    sent, active = call(
        vertex_chips,
        (struct((3, width, size), bf16), struct((size, out_width), f32)),
        (),
        (column, deg_scale, weight, cotangent, own, *received),
    )
    activations, written = call(write_out, (activation, struct((8, 128), f32)), (), (active,))
    received = [exchange(sent, "col", col_shards, 2 * step + 1) for step in (1, 2, 3)]
    joined, own_grad = call(
        join_chips,
        (struct((2 * chips, width, size), bf16), struct((chips, width, size), bf16)),
        (core,),
        (sent, *received),
        after=(written,),
    )
    pieces = call(
        backward_rows,
        (struct((2, width, size), bf16),) * row_shards,
        (row, chip, core),
        (adjacency, joined, own_grad, exchange(joined, "col", col_shards, 1)),
        [
            pltpu.VMEM((width, col_shards * size), bf16),
            pltpu.VMEM((col_shards, width, size), bf16),
            pltpu.VMEM((width, row_shards * size), f32),
        ],
    )
    arrived = [exchange(piece, "row", row_shards, step) for step, piece in zip(far_first, pieces)]
    arrived.append(pieces[-1])
    half_grad = call(
        functools.partial(sum_grad, factor),
        struct((height, out_width // 2), bf16),
        (row,),
        arrived,
        [pltpu.VMEM((row_shards, height, out_width // 2), bf16)],
    )
    other_grad = exchange(half_grad, "col", col_shards, 1)
    input_grad = call(input_rows, input_shape, (), (deg_scale, *arrived))
    weight_grad = call(
        join_halves, struct((height, out_width), f32), (core,), (half_grad, other_grad)
    )
    return (activations, input_grad, weight_grad)


def solution(mesh):
    in_specs = (
        P(("row", "col"), None),
        P(("row", "col")),
        P(),
        P(("row", "col"), None),
        P("row", "col", None),
        P("row", "col", None),
        P("row", "col"),
        P("row", "col", None, None, None),
    )
    out_specs = (P(("row", "col"), None), P(("row", "col"), None), P())
    return jax.shard_map(
        on_device, mesh=mesh, in_specs=in_specs, out_specs=out_specs, check_vma=False
    )
```

```python
import functools
import math

import jax
import jax.numpy as jnp
from jax import lax
from jax.experimental import pallas as pl
from jax.experimental.pallas import tpu as pltpu
from jax.sharding import PartitionSpec as P

VMEM = pl.BlockSpec(memory_space=pltpu.VMEM)
SMEM = pl.BlockSpec(memory_space=pltpu.SMEM)
ANY = pl.BlockSpec(memory_space=pl.ANY)
LIMIT = pltpu.CompilerParams(vmem_limit_bytes=40 * 1024 * 1024)
FIRST_FLOPS = 1 << 32
bf16, f32 = jnp.bfloat16, jnp.float32


def struct(shape, dtype):
    return jax.ShapeDtypeStruct(shape, dtype)


def call(body, out_shape, scalars, operands, scratch=(), flops=1 << 20, after=()):
    single = not isinstance(out_shape, (tuple, list))
    return pl.pallas_call(
        body,
        out_shape=out_shape,
        in_specs=[SMEM] * len(scalars) + [VMEM] * len(operands) + [ANY] * len(after),
        out_specs=VMEM if single else [VMEM] * len(out_shape),
        scratch_shapes=list(scratch),
        compiler_params=LIMIT,
        cost_estimate=pl.CostEstimate(flops=flops, bytes_accessed=1 << 20, transcendentals=0),
    )(*scalars, *operands, *after)


def block_at(index, size):
    return pl.ds(pl.multiple_of(index * size, size), size)


def unpack_tiles(count_ref, bits_ref, deg_ref, features_ref, scaled_ref, column_ref, masks_ref):
    column = spread_scale(deg_ref[...], column_ref.shape[0])
    column_ref[...] = column
    scaled_ref[...] = (features_ref[...].astype(f32) * column).astype(bf16)

    def one(slot):
        masks_ref[slot] = unpacked(jnp.where(slot < count_ref[0, 0], bits_ref[0, 0, slot], 0))

    pl.loop(0, masks_ref.shape[0])(one)


def forward_total(rows_ref, cols_ref, masks_ref, source, total):
    slots, tile_size = masks_ref.shape[:2]
    total[...] = jnp.zeros_like(total)

    def one(slot):
        place = block_at(rows_ref[0, 0, slot], tile_size)
        pick = block_at(cols_ref[0, 0, slot], tile_size)
        total[place, :] += jnp.dot(masks_ref[slot], source[pick, :], preferred_element_type=f32)

    pl.loop(0, slots)(one)


def backward_total(rows_ref, cols_ref, masks_ref, source, total):
    slots, tile_size = masks_ref.shape[:2]
    total[...] = jnp.zeros_like(total)

    def one(slot):
        pick = block_at(rows_ref[0, 0, slot], tile_size)
        place = block_at(cols_ref[0, 0, slot], tile_size)
        total[:, place] += jnp.dot(source[:, pick], masks_ref[slot], preferred_element_type=f32)

    pl.loop(0, slots)(one)


def unpacked(packed):
    words, tile_size = packed.shape
    repeated = jnp.broadcast_to(packed[:, None, :], (words, 8, tile_size))
    shifts = lax.broadcasted_iota(jnp.int32, (words, 8, tile_size), 1)
    bit_values = jnp.bitwise_and(jnp.right_shift(repeated, shifts), 1)
    return bit_values.reshape(words * 8, tile_size).astype(f32).astype(bf16)


def spread_scale(deg, size):
    rows = lax.broadcasted_iota(jnp.int32, (size, size), 0)
    columns = lax.broadcasted_iota(jnp.int32, (size, size), 1)
    diagonal = jnp.where(rows == columns, deg.astype(f32).reshape(1, size), 0.0).astype(bf16)
    return jnp.dot(diagonal, jnp.ones((size, size), bf16), preferred_element_type=f32)


def scale_column(deg_ref, column_ref):
    column_ref[...] = spread_scale(deg_ref[...], column_ref.shape[0])


def scale_rows(column_ref, features_ref, rows_ref, cols_ref, scaled_ref):
    scaled_ref[...] = (features_ref[...].astype(f32) * column_ref[...]).astype(bf16)


def build_adjacency(count_ref, rows_ref, cols_ref, bits_ref, after_ref, adjacency_ref):
    slots, words, tile_size = bits_ref.shape[2:]
    count = count_ref[0, 0]
    for slot in range(slots):
        packed = jnp.where(slot < count, bits_ref[0, 0, slot], 0)
        place = block_at(rows_ref[0, 0, slot], tile_size), block_at(cols_ref[0, 0, slot], tile_size)
        adjacency_ref[place] = unpacked(packed)


def forward_pair(row_ref, chip_ref, core_ref, adjacency_ref, *refs):
    *blocks, mine_ref, other_ref, source, total = refs
    size = blocks[0].shape[0]
    for step, block in zip((0, 1, 3, 2), blocks):
        source[block_at(row_ref[0] ^ step, size), :] = block[...]
    total[...] = jnp.dot(adjacency_ref[...], source[...], preferred_element_type=f32)
    for chip in range(mine_ref.shape[0]):
        kept = jnp.where(chip == chip_ref[0], core_ref[0], 1 - core_ref[0])
        mine_ref[chip] = total[block_at(2 * chip + kept, size), :]
        other_ref[chip] = total[block_at(2 * chip + 1 - kept, size), :].astype(bf16)


def forward_chips(chip_ref, mine_ref, received_ref, own_ref, *pieces):
    chip = chip_ref[0]
    own_ref[...] = mine_ref[chip] + received_ref[chip].astype(f32)
    for step, piece in zip((3, 2, 1), pieces):
        peer = chip ^ step
        piece[...] = (mine_ref[peer] + received_ref[peer].astype(f32)).astype(bf16)


def vertex_values(summed, column_ref, deg_ref, weight_ref, cotangent_ref):
    hidden = (summed * column_ref[...]).astype(bf16)
    weight = weight_ref[...]
    pre_act = jnp.dot(hidden, weight, preferred_element_type=f32)
    sigmoid_value = 1.0 / (1.0 + jnp.exp(-pre_act))
    slope = sigmoid_value * (1.0 + pre_act * (1.0 - sigmoid_value))
    slope_term = (cotangent_ref[...].astype(f32) * slope).astype(bf16)
    spread = lax.dot_general(
        weight, slope_term, (((1,), (1,)), ((), ())), preferred_element_type=f32
    )
    back = (spread * deg_ref[...].astype(f32).reshape(1, -1)).astype(bf16)
    local_grad = lax.dot_general(
        hidden, slope_term, (((0,), (0,)), ((), ())), preferred_element_type=f32
    )
    return back, local_grad, pre_act * sigmoid_value


def vertex_chips(chip_ref, column_ref, deg_ref, weight_ref, cotangent_ref, own_ref, *refs):
    *received, far_ref, same_ref, near_ref, active_ref = refs
    summed = own_ref[...] + sum(piece[...].astype(f32) for piece in received)
    back, local_grad, active_ref[...] = vertex_values(
        summed, column_ref, deg_ref, weight_ref, cotangent_ref
    )
    local_grad = local_grad.astype(bf16)
    half = same_ref.shape[2]
    low, high = local_grad[:, :half], local_grad[:, half:]
    first = lax.rem(chip_ref[0], 2) == 0
    for sent_ref in (far_ref, same_ref, near_ref):
        sent_ref[0] = back
    same_ref[1] = jnp.where(first, low, high)
    far_ref[1] = near_ref[1] = jnp.where(first, high, low)


def write_out(active_ref, out_ref, written_ref):
    out_ref[...] = active_ref[...].astype(bf16)
    written_ref[...] = jnp.zeros_like(written_ref)


def join_chips(*refs):
    *blocks, _, joined_ref = refs
    chips = len(blocks)
    for step, block in zip((0, 3, 2, 1), blocks):
        joined_ref[step] = block[0]
        joined_ref[chips + step] = block[1]


def backward_rows(row_ref, chip_ref, core_ref, adjacency_ref, own_ref, received_ref, *refs):
    *pieces, source, ordered, total = refs
    chips, size = own_ref.shape[0] // 2, own_ref.shape[2]
    core = core_ref[0]
    for step in range(chips):
        peer = 2 * (chip_ref[0] ^ step)
        mine = peer + (1 - core if step else core)
        other = peer + (core if step else 1 - core)
        source[:, block_at(mine, size)] = own_ref[step]
        source[:, block_at(other, size)] = received_ref[step]
        ordered[mine] = own_ref[chips + step]
        ordered[other] = received_ref[chips + step]
    total[...] = jnp.dot(source[...], adjacency_ref[...], preferred_element_type=f32)
    grad = jnp.sum(ordered[...].astype(f32), axis=0).astype(bf16)
    for step, piece in zip((3, 2, 1, 0), pieces):
        piece[0] = total[:, block_at(row_ref[0] ^ step, size)].astype(bf16)
        piece[1] = grad


def sum_grad(factor, row_ref, *refs):
    *pieces, out_ref, ordered = refs
    for step, piece in zip((3, 2, 1, 0), pieces):
        ordered[row_ref[0] ^ step] = piece[1]
    total = jnp.sum(ordered[...].astype(f32), axis=0) * factor
    out_ref[...] = total.astype(out_ref.dtype)


def input_rows(deg_ref, *refs):
    *pieces, out_ref = refs
    total = sum(piece[0].astype(f32) for piece in pieces)
    out_ref[...] = (total * deg_ref[...].astype(f32).reshape(1, -1)).T.astype(bf16)


def join_halves(chip_ref, own_ref, other_ref, out_ref):
    size = own_ref.shape[1]
    half = lax.rem(chip_ref[0], 2)
    out_ref[:, block_at(half, size)] = own_ref[...].astype(f32)
    out_ref[:, block_at(1 - half, size)] = other_ref[...].astype(f32)


def forward_all(rows_ref, cols_ref, masks_ref, source_ref, partial_ref, total):
    forward_total(rows_ref, cols_ref, masks_ref, source_ref, total)
    partial_ref[...] = total[...].astype(bf16).reshape(partial_ref.shape)


def vertex_all(column_ref, deg_ref, weight_ref, cotangent_ref, received_ref, act_ref, back_ref, grad_ref):
    summed = jnp.sum(received_ref[...].astype(f32), axis=0)
    back_ref[...], grad_ref[...], active = vertex_values(
        summed, column_ref, deg_ref, weight_ref, cotangent_ref
    )
    act_ref[...] = active.astype(bf16)


def backward_all(rows_ref, cols_ref, masks_ref, gathered_ref, pieces_ref, source, total):
    size = gathered_ref.shape[2]
    for shard in range(gathered_ref.shape[0]):
        source[:, shard * size : (shard + 1) * size] = gathered_ref[shard]
    backward_total(rows_ref, cols_ref, masks_ref, source, total)
    for shard in range(pieces_ref.shape[0]):
        pieces_ref[shard] = total[:, shard * size : (shard + 1) * size].astype(bf16)


def input_all(deg_ref, pieces_ref, out_ref):
    total = jnp.sum(pieces_ref[...].astype(f32), axis=0)
    out_ref[...] = (total * deg_ref[...].astype(f32).reshape(1, -1)).T.astype(bf16)


def exchange(block, axis, shards, distance):
    return lax.ppermute(block, axis, [(shard, shard ^ distance) for shard in range(shards)])


def on_device(features, deg_scale, weight, cotangent, tile_rows, tile_cols, tile_count, tile_bits):
    size, width = features.shape
    height, out_width = weight.shape
    row_shards = lax.axis_size("row")
    col_shards = lax.axis_size("col")
    chips = col_shards // 2
    slots, words, tile_size = tile_bits.shape[2:]
    factor = 1.0 / math.sqrt(row_shards * col_shards * size)
    row = lax.axis_index("row").astype(jnp.int32).reshape(1)
    col = lax.axis_index("col").astype(jnp.int32)
    chip, core = (col // 2).reshape(1), (col % 2).reshape(1)
    forward_scratch = [pltpu.VMEM((col_shards * size, width), f32)]
    backward_scratch = [
        pltpu.VMEM((width, col_shards * size), bf16),
        pltpu.VMEM((width, row_shards * size), f32),
    ]
    prepared = (struct((size, width), bf16), struct((size, width), f32))
    block = struct((width, size), bf16)
    activation = struct((size, out_width), bf16)
    input_shape = struct((size, width), bf16)

    covered = slots * tile_size * tile_size == row_shards * col_shards * size * size
    if row_shards != 4 or col_shards != 8 or not covered:
        scaled, column, masks = call(
            unpack_tiles,
            prepared + (struct((slots, tile_size, tile_size), bf16),),
            (tile_count,),
            (tile_bits, deg_scale, features),
        )
        gathered = lax.all_gather(scaled, "row", axis=0, tiled=True)
        partial_value = call(
            forward_all,
            struct((col_shards, size, width), bf16),
            (tile_rows, tile_cols),
            (masks, gathered),
            forward_scratch,
        )
        received = lax.all_to_all(partial_value, "col", 0, 0)
        activations, back, local_grad = call(
            vertex_all,
            (activation, block, struct((height, out_width), f32)),
            (),
            (column, deg_scale, weight, cotangent, received),
        )
        weight_grad = lax.psum(local_grad, ("row", "col")) * factor
        pieces = call(
            backward_all,
            struct((row_shards, width, size), bf16),
            (tile_rows, tile_cols),
            (masks, lax.all_gather(back, "col")),
            backward_scratch,
        )
        arrived = lax.all_to_all(pieces, "row", 0, 0)
        input_grad = call(input_all, input_shape, (), (deg_scale, arrived))
        return (activations, input_grad, weight_grad)

    column = call(
        scale_column, struct((size, width), f32), (), (deg_scale,), flops=FIRST_FLOPS
    )
    scaled = call(scale_rows, struct((size, width), bf16), (), (column, features, tile_rows, tile_cols))
    adjacency = pl.pallas_call(
        build_adjacency,
        out_shape=struct((col_shards * size, row_shards * size), bf16),
        in_specs=[SMEM, SMEM, SMEM, VMEM, ANY],
        out_specs=VMEM,
        compiler_params=LIMIT,
        cost_estimate=pl.CostEstimate(flops=1 << 20, bytes_accessed=1 << 20, transcendentals=0),
    )(tile_count, tile_rows, tile_cols, tile_bits, scaled)
    far_first = (3, 2, 1)
    blocks = [exchange(scaled, "row", row_shards, step) for step in (1, 3, 2)]
    blocks.insert(0, scaled)
    mine, other = call(
        forward_pair,
        (struct((chips, size, width), f32), struct((chips, size, width), bf16)),
        (row, chip, core),
        (adjacency, *blocks),
        [pltpu.VMEM((row_shards * size, width), bf16)] + forward_scratch,
    )
    own, *pieces = call(
        forward_chips,
        (struct((size, width), f32),) + (struct((size, width), bf16),) * len(far_first),
        (chip,),
        (mine, exchange(other, "col", col_shards, 1)),
    )
    received = [
        exchange(piece, "col", col_shards, 2 * step + 1) for step, piece in zip(far_first, pieces)
    ]
    message = struct((2, width, size), bf16)
    far, same, near, active = call(
        vertex_chips,
        (message, message, message, struct((size, out_width), f32)),
        (chip,),
        (column, deg_scale, weight, cotangent, own, *received),
    )
    activations, written = call(write_out, (activation, struct((8, 128), f32)), (), (active,))
    received = [
        exchange(sent, "col", col_shards, 2 * step + 1)
        for step, sent in zip(far_first, (far, same, near))
    ]
    joined = call(
        join_chips,
        struct((2 * chips, width, size), bf16),
        (),
        (same, *received),
        after=(written,),
    )
    pieces = call(
        backward_rows,
        (message,) * row_shards,
        (row, chip, core),
        (adjacency, joined, exchange(joined, "col", col_shards, 1)),
        [
            pltpu.VMEM((width, col_shards * size), bf16),
            pltpu.VMEM((col_shards, width, size), bf16),
            pltpu.VMEM((width, row_shards * size), f32),
        ],
    )
    arrived = [exchange(piece, "row", row_shards, step) for step, piece in zip(far_first, pieces)]
    arrived.append(pieces[-1])
    half_grad = call(
        functools.partial(sum_grad, factor),
        struct((height, out_width // 2), bf16),
        (row,),
        arrived,
        [pltpu.VMEM((row_shards, height, out_width // 2), bf16)],
    )
    other_grad = exchange(half_grad, "col", col_shards, 3)
    input_grad = call(input_rows, input_shape, (), (deg_scale, *arrived))
    weight_grad = call(
        join_halves, struct((height, out_width), f32), (chip,), (half_grad, other_grad)
    )
    return (activations, input_grad, weight_grad)


def solution(mesh):
    in_specs = (
        P(("row", "col"), None),
        P(("row", "col")),
        P(),
        P(("row", "col"), None),
        P("row", "col", None),
        P("row", "col", None),
        P("row", "col"),
        P("row", "col", None, None, None),
    )
    out_specs = (P(("row", "col"), None), P(("row", "col"), None), P())
    return jax.shard_map(
        on_device, mesh=mesh, in_specs=in_specs, out_specs=out_specs, check_vma=False
    )
```

```python
import functools
import math

import jax
import jax.numpy as jnp
from jax import lax
from jax.experimental import pallas as pl
from jax.experimental.pallas import tpu as pltpu
from jax.sharding import PartitionSpec as P

VMEM = pl.BlockSpec(memory_space=pltpu.VMEM)
SMEM = pl.BlockSpec(memory_space=pltpu.SMEM)
ANY = pl.BlockSpec(memory_space=pl.ANY)
LIMIT = pltpu.CompilerParams(vmem_limit_bytes=40 * 1024 * 1024)
FIRST_FLOPS = 1 << 32
bf16, f32 = jnp.bfloat16, jnp.float32


def struct(shape, dtype):
    return jax.ShapeDtypeStruct(shape, dtype)


def call(body, out_shape, scalars, operands, scratch=(), flops=1 << 20, after=()):
    single = not isinstance(out_shape, (tuple, list))
    return pl.pallas_call(
        body,
        out_shape=out_shape,
        in_specs=[SMEM] * len(scalars) + [VMEM] * len(operands) + [ANY] * len(after),
        out_specs=VMEM if single else [VMEM] * len(out_shape),
        scratch_shapes=list(scratch),
        compiler_params=LIMIT,
        cost_estimate=pl.CostEstimate(flops=flops, bytes_accessed=1 << 20, transcendentals=0),
    )(*scalars, *operands, *after)


def block_at(index, size):
    return pl.ds(pl.multiple_of(index * size, size), size)


def unpack_tiles(count_ref, bits_ref, deg_ref, features_ref, scaled_ref, column_ref, masks_ref):
    column = spread_scale(deg_ref[...], column_ref.shape[0])
    column_ref[...] = column
    scaled_ref[...] = (features_ref[...].astype(f32) * column).astype(bf16)

    def one(slot):
        masks_ref[slot] = unpacked(jnp.where(slot < count_ref[0, 0], bits_ref[0, 0, slot], 0))

    pl.loop(0, masks_ref.shape[0])(one)


def forward_total(rows_ref, cols_ref, masks_ref, source, total):
    slots, tile_size = masks_ref.shape[:2]
    total[...] = jnp.zeros_like(total)

    def one(slot):
        place = block_at(rows_ref[0, 0, slot], tile_size)
        pick = block_at(cols_ref[0, 0, slot], tile_size)
        total[place, :] += jnp.dot(masks_ref[slot], source[pick, :], preferred_element_type=f32)

    pl.loop(0, slots)(one)


def backward_total(rows_ref, cols_ref, masks_ref, source, total):
    slots, tile_size = masks_ref.shape[:2]
    total[...] = jnp.zeros_like(total)

    def one(slot):
        pick = block_at(rows_ref[0, 0, slot], tile_size)
        place = block_at(cols_ref[0, 0, slot], tile_size)
        total[:, place] += jnp.dot(source[:, pick], masks_ref[slot], preferred_element_type=f32)

    pl.loop(0, slots)(one)


def unpacked(packed):
    words, tile_size = packed.shape
    repeated = jnp.broadcast_to(packed[:, None, :], (words, 8, tile_size))
    shifts = lax.broadcasted_iota(jnp.int32, (words, 8, tile_size), 1)
    bit_values = jnp.bitwise_and(jnp.right_shift(repeated, shifts), 1)
    return bit_values.reshape(words * 8, tile_size).astype(f32).astype(bf16)


def spread_scale(deg, size):
    rows = lax.broadcasted_iota(jnp.int32, (size, size), 0)
    columns = lax.broadcasted_iota(jnp.int32, (size, size), 1)
    diagonal = jnp.where(rows == columns, deg.astype(f32).reshape(1, size), 0.0).astype(bf16)
    return jnp.dot(diagonal, jnp.ones((size, size), bf16), preferred_element_type=f32)


def scale_column(deg_ref, column_ref):
    column_ref[...] = spread_scale(deg_ref[...], column_ref.shape[0])


def scale_rows(column_ref, features_ref, rows_ref, cols_ref, scaled_ref):
    scaled_ref[...] = (features_ref[...].astype(f32) * column_ref[...]).astype(bf16)


def build_adjacency(count_ref, rows_ref, cols_ref, bits_ref, after_ref, adjacency_ref):
    slots, words, tile_size = bits_ref.shape[2:]
    count = count_ref[0, 0]
    for slot in range(slots):
        packed = jnp.where(slot < count, bits_ref[0, 0, slot], 0)
        place = block_at(rows_ref[0, 0, slot], tile_size), block_at(cols_ref[0, 0, slot], tile_size)
        adjacency_ref[place] = unpacked(packed)


def forward_pair(row_ref, core_ref, adjacency_ref, *refs):
    *blocks, mine_ref, other_ref, source, total = refs
    size = blocks[0].shape[0]
    for step, block in zip((0, 1, 3, 2), blocks):
        source[block_at(row_ref[0] ^ step, size), :] = block[...]
    total[...] = jnp.dot(adjacency_ref[...], source[...], preferred_element_type=f32)
    core = core_ref[0]
    for chip in range(mine_ref.shape[0]):
        mine_ref[chip] = total[block_at(2 * chip + core, size), :]
        other_ref[chip] = total[block_at(2 * chip + 1 - core, size), :].astype(bf16)


def forward_chips(chip_ref, mine_ref, received_ref, own_ref, *pieces):
    chip = chip_ref[0]
    own_ref[...] = mine_ref[chip] + received_ref[chip].astype(f32)
    for step, piece in zip((3, 2, 1), pieces):
        peer = chip ^ step
        piece[...] = (mine_ref[peer] + received_ref[peer].astype(f32)).astype(bf16)


def vertex_values(summed, column_ref, deg_ref, weight_ref, cotangent_ref):
    hidden = (summed * column_ref[...]).astype(bf16)
    weight = weight_ref[...]
    pre_act = jnp.dot(hidden, weight, preferred_element_type=f32)
    sigmoid_value = 1.0 / (1.0 + jnp.exp(-pre_act))
    slope = sigmoid_value * (1.0 + pre_act * (1.0 - sigmoid_value))
    slope_term = (cotangent_ref[...].astype(f32) * slope).astype(bf16)
    spread = lax.dot_general(
        weight, slope_term, (((1,), (1,)), ((), ())), preferred_element_type=f32
    )
    back = (spread * deg_ref[...].astype(f32).reshape(1, -1)).astype(bf16)
    local_grad = lax.dot_general(
        hidden, slope_term, (((0,), (0,)), ((), ())), preferred_element_type=f32
    )
    return back, local_grad, pre_act * sigmoid_value


def vertex_chips(column_ref, deg_ref, weight_ref, cotangent_ref, own_ref, *refs):
    *received, sent_ref, active_ref = refs
    summed = own_ref[...] + sum(piece[...].astype(f32) for piece in received)
    sent_ref[0], local_grad, active_ref[...] = vertex_values(
        summed, column_ref, deg_ref, weight_ref, cotangent_ref
    )
    half = sent_ref.shape[2]
    for core in range(2):
        sent_ref[1 + core] = local_grad[:, core * half : (core + 1) * half].astype(bf16)


def write_out(active_ref, out_ref, written_ref):
    out_ref[...] = active_ref[...].astype(bf16)
    written_ref[...] = jnp.zeros_like(written_ref)


def join_chips(chip_ref, core_ref, *refs):
    *blocks, _, joined_ref, own_grad_ref, ordered = refs
    chips = len(blocks)
    for step, block in enumerate(blocks):
        joined_ref[step] = block[0]
        ordered[chip_ref[0] ^ step] = block[1:]
    grad = jnp.sum(ordered[...].astype(f32), axis=0).astype(bf16)
    second = core_ref[0] == 1
    own_grad_ref[...] = jnp.where(second, grad[1], grad[0])
    joined_ref[chips] = jnp.where(second, grad[0], grad[1])


def backward_rows(row_ref, chip_ref, core_ref, adjacency_ref, own_ref, grad_ref, received_ref, *refs):
    *pieces, source, total = refs
    chips = own_ref.shape[0] - 1
    size = own_ref.shape[2]
    chip, core = chip_ref[0], core_ref[0]
    for step in range(chips):
        peer = 2 * (chip ^ step)
        source[:, block_at(peer + core, size)] = own_ref[step]
        source[:, block_at(peer + 1 - core, size)] = received_ref[step]
    total[...] = jnp.dot(source[...], adjacency_ref[...], preferred_element_type=f32)
    grad = (grad_ref[...].astype(f32) + received_ref[chips].astype(f32)).astype(bf16)
    for step, piece in zip((2, 3, 1, 0), pieces):
        piece[0] = total[:, block_at(row_ref[0] ^ step, size)].astype(bf16)
        piece[1] = grad


def sum_grad(factor, row_ref, *refs):
    *pieces, out_ref, ordered = refs
    for step, piece in zip((2, 3, 1, 0), pieces):
        ordered[row_ref[0] ^ step] = piece[1]
    total = jnp.sum(ordered[...].astype(f32), axis=0) * factor
    out_ref[...] = total.astype(out_ref.dtype)


def input_rows(deg_ref, *refs):
    *pieces, out_ref = refs
    total = sum(piece[0].astype(f32) for piece in pieces)
    out_ref[...] = (total * deg_ref[...].astype(f32).reshape(1, -1)).T.astype(bf16)


def join_halves(core_ref, own_ref, other_ref, out_ref):
    size = own_ref.shape[1]
    half = core_ref[0]
    out_ref[:, block_at(half, size)] = own_ref[...].astype(f32)
    out_ref[:, block_at(1 - half, size)] = other_ref[...].astype(f32)


def forward_all(rows_ref, cols_ref, masks_ref, source_ref, partial_ref, total):
    forward_total(rows_ref, cols_ref, masks_ref, source_ref, total)
    partial_ref[...] = total[...].astype(bf16).reshape(partial_ref.shape)


def vertex_all(column_ref, deg_ref, weight_ref, cotangent_ref, received_ref, act_ref, back_ref, grad_ref):
    summed = jnp.sum(received_ref[...].astype(f32), axis=0)
    back_ref[...], grad_ref[...], active = vertex_values(
        summed, column_ref, deg_ref, weight_ref, cotangent_ref
    )
    act_ref[...] = active.astype(bf16)


def backward_all(rows_ref, cols_ref, masks_ref, gathered_ref, pieces_ref, source, total):
    size = gathered_ref.shape[2]
    for shard in range(gathered_ref.shape[0]):
        source[:, shard * size : (shard + 1) * size] = gathered_ref[shard]
    backward_total(rows_ref, cols_ref, masks_ref, source, total)
    for shard in range(pieces_ref.shape[0]):
        pieces_ref[shard] = total[:, shard * size : (shard + 1) * size].astype(bf16)


def input_all(deg_ref, pieces_ref, out_ref):
    total = jnp.sum(pieces_ref[...].astype(f32), axis=0)
    out_ref[...] = (total * deg_ref[...].astype(f32).reshape(1, -1)).T.astype(bf16)


def exchange(block, axis, shards, distance):
    return lax.ppermute(block, axis, [(shard, shard ^ distance) for shard in range(shards)])


def on_device(features, deg_scale, weight, cotangent, tile_rows, tile_cols, tile_count, tile_bits):
    size, width = features.shape
    height, out_width = weight.shape
    row_shards = lax.axis_size("row")
    col_shards = lax.axis_size("col")
    chips = col_shards // 2
    slots, words, tile_size = tile_bits.shape[2:]
    factor = 1.0 / math.sqrt(row_shards * col_shards * size)
    row = lax.axis_index("row").astype(jnp.int32).reshape(1)
    col = lax.axis_index("col").astype(jnp.int32)
    chip, core = (col // 2).reshape(1), (col % 2).reshape(1)
    forward_scratch = [pltpu.VMEM((col_shards * size, width), f32)]
    backward_scratch = [
        pltpu.VMEM((width, col_shards * size), bf16),
        pltpu.VMEM((width, row_shards * size), f32),
    ]
    prepared = (struct((size, width), bf16), struct((size, width), f32))
    block = struct((width, size), bf16)
    activation = struct((size, out_width), bf16)
    input_shape = struct((size, width), bf16)

    covered = slots * tile_size * tile_size == row_shards * col_shards * size * size
    if row_shards != 4 or col_shards != 8 or not covered:
        scaled, column, masks = call(
            unpack_tiles,
            prepared + (struct((slots, tile_size, tile_size), bf16),),
            (tile_count,),
            (tile_bits, deg_scale, features),
        )
        gathered = lax.all_gather(scaled, "row", axis=0, tiled=True)
        partial_value = call(
            forward_all,
            struct((col_shards, size, width), bf16),
            (tile_rows, tile_cols),
            (masks, gathered),
            forward_scratch,
        )
        received = lax.all_to_all(partial_value, "col", 0, 0)
        activations, back, local_grad = call(
            vertex_all,
            (activation, block, struct((height, out_width), f32)),
            (),
            (column, deg_scale, weight, cotangent, received),
        )
        weight_grad = lax.psum(local_grad, ("row", "col")) * factor
        pieces = call(
            backward_all,
            struct((row_shards, width, size), bf16),
            (tile_rows, tile_cols),
            (masks, lax.all_gather(back, "col")),
            backward_scratch,
        )
        arrived = lax.all_to_all(pieces, "row", 0, 0)
        input_grad = call(input_all, input_shape, (), (deg_scale, arrived))
        return (activations, input_grad, weight_grad)

    column = call(
        scale_column, struct((size, width), f32), (), (deg_scale,), flops=FIRST_FLOPS
    )
    scaled = call(scale_rows, struct((size, width), bf16), (), (column, features, tile_rows, tile_cols))
    adjacency = pl.pallas_call(
        build_adjacency,
        out_shape=struct((col_shards * size, row_shards * size), bf16),
        in_specs=[SMEM, SMEM, SMEM, VMEM, ANY],
        out_specs=VMEM,
        compiler_params=LIMIT,
        cost_estimate=pl.CostEstimate(flops=1 << 20, bytes_accessed=1 << 20, transcendentals=0),
    )(tile_count, tile_rows, tile_cols, tile_bits, scaled)
    far_first = (3, 2, 1)
    blocks = [exchange(scaled, "row", row_shards, step) for step in (1, 3, 2)]
    blocks.insert(0, scaled)
    mine, other = call(
        forward_pair,
        (struct((chips, size, width), f32), struct((chips, size, width), bf16)),
        (row, core),
        (adjacency, *blocks),
        [pltpu.VMEM((row_shards * size, width), bf16)] + forward_scratch,
    )
    own, *pieces = call(
        forward_chips,
        (struct((size, width), f32),) + (struct((size, width), bf16),) * len(far_first),
        (chip,),
        (mine, exchange(other, "col", col_shards, 1)),
    )
    received = [
        exchange(piece, "col", col_shards, 2 * step) for step, piece in zip(far_first, pieces)
    ]
    sent, active = call(
        vertex_chips,
        (struct((3, width, size), bf16), struct((size, out_width), f32)),
        (),
        (column, deg_scale, weight, cotangent, own, *received),
    )
    activations, written = call(write_out, (activation, struct((8, 128), f32)), (), (active,))
    received = [exchange(sent, "col", col_shards, 2 * step) for step in (1, 2, 3)]
    joined, own_grad = call(
        join_chips,
        (struct((chips + 1, width, size), bf16), struct((width, size), bf16)),
        (chip, core),
        (sent, *received),
        [pltpu.VMEM((chips, 2, width, size), bf16)],
        after=(written,),
    )
    pieces = call(
        backward_rows,
        (struct((2, width, size), bf16),) * row_shards,
        (row, chip, core),
        (adjacency, joined, own_grad, exchange(joined, "col", col_shards, 1)),
        backward_scratch,
    )
    arrived = [exchange(piece, "row", row_shards, step) for step, piece in zip((2, 3, 1), pieces)]
    arrived.append(pieces[-1])
    half_grad = call(
        functools.partial(sum_grad, factor),
        struct((height, out_width // 2), bf16),
        (row,),
        arrived,
        [pltpu.VMEM((row_shards, height, out_width // 2), bf16)],
    )
    other_grad = exchange(half_grad, "col", col_shards, 1)
    input_grad = call(input_rows, input_shape, (), (deg_scale, *arrived))
    weight_grad = call(
        join_halves, struct((height, out_width), f32), (core,), (half_grad, other_grad)
    )
    return (activations, input_grad, weight_grad)


def solution(mesh):
    in_specs = (
        P(("row", "col"), None),
        P(("row", "col")),
        P(),
        P(("row", "col"), None),
        P("row", "col", None),
        P("row", "col", None),
        P("row", "col"),
        P("row", "col", None, None, None),
    )
    out_specs = (P(("row", "col"), None), P(("row", "col"), None), P())
    return jax.shard_map(
        on_device, mesh=mesh, in_specs=in_specs, out_specs=out_specs, check_vma=False
    )
```

```python
import functools
import math

import jax
import jax.numpy as jnp
from jax import lax
from jax.experimental import pallas as pl
from jax.experimental.pallas import tpu as pltpu
from jax.sharding import PartitionSpec as P

VMEM = pl.BlockSpec(memory_space=pltpu.VMEM)
SMEM = pl.BlockSpec(memory_space=pltpu.SMEM)
ANY = pl.BlockSpec(memory_space=pl.ANY)
LIMIT = pltpu.CompilerParams(vmem_limit_bytes=40 * 1024 * 1024)
FIRST_FLOPS = 1 << 32
bf16, f32 = jnp.bfloat16, jnp.float32


def struct(shape, dtype):
    return jax.ShapeDtypeStruct(shape, dtype)


def call(body, out_shape, scalars, operands, scratch=(), flops=1 << 20, after=()):
    single = not isinstance(out_shape, (tuple, list))
    return pl.pallas_call(
        body,
        out_shape=out_shape,
        in_specs=[SMEM] * len(scalars) + [VMEM] * len(operands) + [ANY] * len(after),
        out_specs=VMEM if single else [VMEM] * len(out_shape),
        scratch_shapes=list(scratch),
        compiler_params=LIMIT,
        cost_estimate=pl.CostEstimate(flops=flops, bytes_accessed=1 << 20, transcendentals=0),
    )(*scalars, *operands, *after)


def block_at(index, size):
    return pl.ds(pl.multiple_of(index * size, size), size)


def unpack_tiles(count_ref, bits_ref, deg_ref, features_ref, scaled_ref, column_ref, masks_ref):
    column = spread_scale(deg_ref[...], column_ref.shape[0])
    column_ref[...] = column
    scaled_ref[...] = (features_ref[...].astype(f32) * column).astype(bf16)

    def one(slot):
        masks_ref[slot] = unpacked(jnp.where(slot < count_ref[0, 0], bits_ref[0, 0, slot], 0))

    pl.loop(0, masks_ref.shape[0])(one)


def forward_total(rows_ref, cols_ref, masks_ref, source, total):
    slots, tile_size = masks_ref.shape[:2]
    total[...] = jnp.zeros_like(total)

    def one(slot):
        place = block_at(rows_ref[0, 0, slot], tile_size)
        pick = block_at(cols_ref[0, 0, slot], tile_size)
        total[place, :] += jnp.dot(masks_ref[slot], source[pick, :], preferred_element_type=f32)

    pl.loop(0, slots)(one)


def backward_total(rows_ref, cols_ref, masks_ref, source, total):
    slots, tile_size = masks_ref.shape[:2]
    total[...] = jnp.zeros_like(total)

    def one(slot):
        pick = block_at(rows_ref[0, 0, slot], tile_size)
        place = block_at(cols_ref[0, 0, slot], tile_size)
        total[:, place] += jnp.dot(source[:, pick], masks_ref[slot], preferred_element_type=f32)

    pl.loop(0, slots)(one)


def unpacked(packed):
    words, tile_size = packed.shape
    repeated = jnp.broadcast_to(packed[:, None, :], (words, 8, tile_size))
    shifts = lax.broadcasted_iota(jnp.int32, (words, 8, tile_size), 1)
    bit_values = jnp.bitwise_and(jnp.right_shift(repeated, shifts), 1)
    return bit_values.reshape(words * 8, tile_size).astype(f32).astype(bf16)


def spread_scale(deg, size):
    rows = lax.broadcasted_iota(jnp.int32, (size, size), 0)
    columns = lax.broadcasted_iota(jnp.int32, (size, size), 1)
    diagonal = jnp.where(rows == columns, deg.astype(f32).reshape(1, size), 0.0).astype(bf16)
    return jnp.dot(diagonal, jnp.ones((size, size), bf16), preferred_element_type=f32)


def scale_column(deg_ref, column_ref):
    column_ref[...] = spread_scale(deg_ref[...], column_ref.shape[0])


def scale_rows(column_ref, features_ref, rows_ref, cols_ref, scaled_ref):
    scaled_ref[...] = (features_ref[...].astype(f32) * column_ref[...]).astype(bf16)


def build_adjacency(count_ref, rows_ref, cols_ref, bits_ref, after_ref, adjacency_ref):
    slots, words, tile_size = bits_ref.shape[2:]
    count = count_ref[0, 0]
    for slot in range(slots):
        packed = jnp.where(slot < count, bits_ref[0, 0, slot], 0)
        place = block_at(rows_ref[0, 0, slot], tile_size), block_at(cols_ref[0, 0, slot], tile_size)
        adjacency_ref[place] = unpacked(packed)


def rows_of(core, adjacency_ref, size):
    blocks = [
        adjacency_ref[block_at(2 * chip + core, size), :]
        for chip in range(adjacency_ref.shape[0] // (2 * size))
    ]
    return jnp.concatenate(blocks, axis=0)


def forward_other(row_ref, core_ref, adjacency_ref, *refs):
    *blocks, source_ref, other_ref = refs
    size = blocks[0].shape[0]
    for step, block in zip((0, 1, 3, 2), blocks):
        source_ref[block_at(row_ref[0] ^ step, size), :] = block[...]
    rows = rows_of(1 - core_ref[0], adjacency_ref, size)
    total = jnp.dot(rows, source_ref[...], preferred_element_type=f32)
    other_ref[...] = total.astype(bf16).reshape(other_ref.shape)


def forward_mine(core_ref, adjacency_ref, source_ref, mine_ref):
    rows = rows_of(core_ref[0], adjacency_ref, mine_ref.shape[1])
    total = jnp.dot(rows, source_ref[...], preferred_element_type=f32)
    mine_ref[...] = total.reshape(mine_ref.shape)


def forward_chips(chip_ref, mine_ref, received_ref, own_ref, *pieces):
    chip = chip_ref[0]
    own_ref[...] = mine_ref[chip] + received_ref[chip].astype(f32)
    for step, piece in zip((3, 2, 1), pieces):
        peer = chip ^ step
        piece[...] = (mine_ref[peer] + received_ref[peer].astype(f32)).astype(bf16)


def vertex_values(summed, column_ref, deg_ref, weight_ref, cotangent_ref):
    hidden = (summed * column_ref[...]).astype(bf16)
    weight = weight_ref[...]
    pre_act = jnp.dot(hidden, weight, preferred_element_type=f32)
    sigmoid_value = 1.0 / (1.0 + jnp.exp(-pre_act))
    slope = sigmoid_value * (1.0 + pre_act * (1.0 - sigmoid_value))
    slope_term = (cotangent_ref[...].astype(f32) * slope).astype(bf16)
    spread = lax.dot_general(
        weight, slope_term, (((1,), (1,)), ((), ())), preferred_element_type=f32
    )
    back = (spread * deg_ref[...].astype(f32).reshape(1, -1)).astype(bf16)
    local_grad = lax.dot_general(
        hidden, slope_term, (((0,), (0,)), ((), ())), preferred_element_type=f32
    )
    return back, local_grad, pre_act * sigmoid_value


def vertex_chips(column_ref, deg_ref, weight_ref, cotangent_ref, own_ref, *refs):
    *received, sent_ref, active_ref = refs
    summed = own_ref[...] + sum(piece[...].astype(f32) for piece in received)
    sent_ref[0], local_grad, active_ref[...] = vertex_values(
        summed, column_ref, deg_ref, weight_ref, cotangent_ref
    )
    half = sent_ref.shape[2]
    for core in range(2):
        sent_ref[1 + core] = local_grad[:, core * half : (core + 1) * half].astype(bf16)


def write_out(active_ref, out_ref, written_ref):
    out_ref[...] = active_ref[...].astype(bf16)
    written_ref[...] = jnp.zeros_like(written_ref)


def join_chips(chip_ref, core_ref, *refs):
    *blocks, _, joined_ref, own_grad_ref, ordered = refs
    chips = len(blocks)
    for step, block in enumerate(blocks):
        joined_ref[step] = block[0]
        ordered[chip_ref[0] ^ step] = block[1:]
    grad = jnp.sum(ordered[...].astype(f32), axis=0)
    second = core_ref[0] == 1
    own_grad_ref[...] = jnp.where(second, grad[1], grad[0])
    joined_ref[chips] = jnp.where(second, grad[0], grad[1]).astype(bf16)


def backward_rows(row_ref, chip_ref, core_ref, adjacency_ref, own_ref, grad_ref, received_ref, *refs):
    *pieces, source, total = refs
    chips = own_ref.shape[0] - 1
    size = own_ref.shape[2]
    chip, core = chip_ref[0], core_ref[0]
    for step in range(chips):
        peer = 2 * (chip ^ step)
        source[:, block_at(peer + core, size)] = own_ref[step]
        source[:, block_at(peer + 1 - core, size)] = received_ref[step]
    total[...] = jnp.dot(source[...], adjacency_ref[...], preferred_element_type=f32)
    grad = (grad_ref[...] + received_ref[chips].astype(f32)).astype(bf16)
    for step, piece in zip((2, 3, 1, 0), pieces):
        piece[0] = total[:, block_at(row_ref[0] ^ step, size)].astype(bf16)
        piece[1] = grad


def sum_grad(factor, row_ref, *refs):
    *pieces, out_ref, ordered = refs
    for step, piece in zip((2, 3, 1, 0), pieces):
        ordered[row_ref[0] ^ step] = piece[1]
    total = jnp.sum(ordered[...].astype(f32), axis=0) * factor
    out_ref[...] = total.astype(out_ref.dtype)


def input_rows(deg_ref, *refs):
    *pieces, out_ref = refs
    total = sum(piece[0].astype(f32) for piece in pieces)
    out_ref[...] = (total * deg_ref[...].astype(f32).reshape(1, -1)).T.astype(bf16)


def join_halves(core_ref, own_ref, other_ref, out_ref):
    size = own_ref.shape[1]
    half = core_ref[0]
    out_ref[:, block_at(half, size)] = own_ref[...].astype(f32)
    out_ref[:, block_at(1 - half, size)] = other_ref[...].astype(f32)


def forward_all(rows_ref, cols_ref, masks_ref, source_ref, partial_ref, total):
    forward_total(rows_ref, cols_ref, masks_ref, source_ref, total)
    partial_ref[...] = total[...].astype(bf16).reshape(partial_ref.shape)


def vertex_all(column_ref, deg_ref, weight_ref, cotangent_ref, received_ref, act_ref, back_ref, grad_ref):
    summed = jnp.sum(received_ref[...].astype(f32), axis=0)
    back_ref[...], grad_ref[...], active = vertex_values(
        summed, column_ref, deg_ref, weight_ref, cotangent_ref
    )
    act_ref[...] = active.astype(bf16)


def backward_all(rows_ref, cols_ref, masks_ref, gathered_ref, pieces_ref, source, total):
    size = gathered_ref.shape[2]
    for shard in range(gathered_ref.shape[0]):
        source[:, shard * size : (shard + 1) * size] = gathered_ref[shard]
    backward_total(rows_ref, cols_ref, masks_ref, source, total)
    for shard in range(pieces_ref.shape[0]):
        pieces_ref[shard] = total[:, shard * size : (shard + 1) * size].astype(bf16)


def input_all(deg_ref, pieces_ref, out_ref):
    total = jnp.sum(pieces_ref[...].astype(f32), axis=0)
    out_ref[...] = (total * deg_ref[...].astype(f32).reshape(1, -1)).T.astype(bf16)


def exchange(block, axis, shards, distance):
    return lax.ppermute(block, axis, [(shard, shard ^ distance) for shard in range(shards)])


def on_device(features, deg_scale, weight, cotangent, tile_rows, tile_cols, tile_count, tile_bits):
    size, width = features.shape
    height, out_width = weight.shape
    row_shards = lax.axis_size("row")
    col_shards = lax.axis_size("col")
    chips = col_shards // 2
    slots, words, tile_size = tile_bits.shape[2:]
    factor = 1.0 / math.sqrt(row_shards * col_shards * size)
    row = lax.axis_index("row").astype(jnp.int32).reshape(1)
    col = lax.axis_index("col").astype(jnp.int32)
    chip, core = (col // 2).reshape(1), (col % 2).reshape(1)
    forward_scratch = [pltpu.VMEM((col_shards * size, width), f32)]
    backward_scratch = [
        pltpu.VMEM((width, col_shards * size), bf16),
        pltpu.VMEM((width, row_shards * size), f32),
    ]
    prepared = (struct((size, width), bf16), struct((size, width), f32))
    block = struct((width, size), bf16)
    activation = struct((size, out_width), bf16)
    input_shape = struct((size, width), bf16)

    covered = slots * tile_size * tile_size == row_shards * col_shards * size * size
    if row_shards != 4 or col_shards != 8 or not covered:
        scaled, column, masks = call(
            unpack_tiles,
            prepared + (struct((slots, tile_size, tile_size), bf16),),
            (tile_count,),
            (tile_bits, deg_scale, features),
        )
        gathered = lax.all_gather(scaled, "row", axis=0, tiled=True)
        partial_value = call(
            forward_all,
            struct((col_shards, size, width), bf16),
            (tile_rows, tile_cols),
            (masks, gathered),
            forward_scratch,
        )
        received = lax.all_to_all(partial_value, "col", 0, 0)
        activations, back, local_grad = call(
            vertex_all,
            (activation, block, struct((height, out_width), f32)),
            (),
            (column, deg_scale, weight, cotangent, received),
        )
        weight_grad = lax.psum(local_grad, ("row", "col")) * factor
        pieces = call(
            backward_all,
            struct((row_shards, width, size), bf16),
            (tile_rows, tile_cols),
            (masks, lax.all_gather(back, "col")),
            backward_scratch,
        )
        arrived = lax.all_to_all(pieces, "row", 0, 0)
        input_grad = call(input_all, input_shape, (), (deg_scale, arrived))
        return (activations, input_grad, weight_grad)

    column = call(
        scale_column, struct((size, width), f32), (), (deg_scale,), flops=FIRST_FLOPS
    )
    scaled = call(scale_rows, struct((size, width), bf16), (), (column, features, tile_rows, tile_cols))
    adjacency = pl.pallas_call(
        build_adjacency,
        out_shape=struct((col_shards * size, row_shards * size), bf16),
        in_specs=[SMEM, SMEM, SMEM, VMEM, ANY],
        out_specs=VMEM,
        compiler_params=LIMIT,
        cost_estimate=pl.CostEstimate(flops=1 << 20, bytes_accessed=1 << 20, transcendentals=0),
    )(tile_count, tile_rows, tile_cols, tile_bits, scaled)
    far_first = (3, 2, 1)
    blocks = [exchange(scaled, "row", row_shards, step) for step in (1, 3, 2)]
    blocks.insert(0, scaled)
    source, other = call(
        forward_other,
        (struct((row_shards * size, width), bf16), struct((chips, size, width), bf16)),
        (row, core),
        (adjacency, *blocks),
    )
    mine = call(
        forward_mine, struct((chips, size, width), f32), (core,), (adjacency, source)
    )
    own, *pieces = call(
        forward_chips,
        (struct((size, width), f32),) + (struct((size, width), bf16),) * len(far_first),
        (chip,),
        (mine, exchange(other, "col", col_shards, 1)),
    )
    received = [
        exchange(piece, "col", col_shards, 2 * step) for step, piece in zip(far_first, pieces)
    ]
    sent, active = call(
        vertex_chips,
        (struct((3, width, size), bf16), struct((size, out_width), f32)),
        (),
        (column, deg_scale, weight, cotangent, own, *received),
    )
    activations, written = call(write_out, (activation, struct((8, 128), f32)), (), (active,))
    received = [exchange(sent, "col", col_shards, 2 * step) for step in (1, 2, 3)]
    joined, own_grad = call(
        join_chips,
        (struct((chips + 1, width, size), bf16), struct((width, size), f32)),
        (chip, core),
        (sent, *received),
        [pltpu.VMEM((chips, 2, width, size), bf16)],
        after=(written,),
    )
    pieces = call(
        backward_rows,
        (struct((2, width, size), bf16),) * row_shards,
        (row, chip, core),
        (adjacency, joined, own_grad, exchange(joined, "col", col_shards, 1)),
        backward_scratch,
    )
    arrived = [exchange(piece, "row", row_shards, step) for step, piece in zip((2, 3, 1), pieces)]
    arrived.append(pieces[-1])
    half_grad = call(
        functools.partial(sum_grad, factor),
        struct((height, out_width // 2), f32),
        (row,),
        arrived,
        [pltpu.VMEM((row_shards, height, out_width // 2), bf16)],
    )
    other_grad = exchange(half_grad, "col", col_shards, 1)
    input_grad = call(input_rows, input_shape, (), (deg_scale, *arrived))
    weight_grad = call(
        join_halves, struct((height, out_width), f32), (core,), (half_grad, other_grad)
    )
    return (activations, input_grad, weight_grad)


def solution(mesh):
    in_specs = (
        P(("row", "col"), None),
        P(("row", "col")),
        P(),
        P(("row", "col"), None),
        P("row", "col", None),
        P("row", "col", None),
        P("row", "col"),
        P("row", "col", None, None, None),
    )
    out_specs = (P(("row", "col"), None), P(("row", "col"), None), P())
    return jax.shard_map(
        on_device, mesh=mesh, in_specs=in_specs, out_specs=out_specs, check_vma=False
    )
```

```python
import functools
import math

import jax
import jax.numpy as jnp
from jax import lax
from jax.experimental import pallas as pl
from jax.experimental.pallas import tpu as pltpu
from jax.sharding import PartitionSpec as P

VMEM = pl.BlockSpec(memory_space=pltpu.VMEM)
SMEM = pl.BlockSpec(memory_space=pltpu.SMEM)
ANY = pl.BlockSpec(memory_space=pl.ANY)
LIMIT = pltpu.CompilerParams(vmem_limit_bytes=40 * 1024 * 1024)
FIRST_FLOPS = 1 << 32
bf16, f32 = jnp.bfloat16, jnp.float32


def struct(shape, dtype):
    return jax.ShapeDtypeStruct(shape, dtype)


def call(body, out_shape, scalars, operands, scratch=(), flops=1 << 20, after=()):
    single = not isinstance(out_shape, (tuple, list))
    return pl.pallas_call(
        body,
        out_shape=out_shape,
        in_specs=[SMEM] * len(scalars) + [VMEM] * len(operands) + [ANY] * len(after),
        out_specs=VMEM if single else [VMEM] * len(out_shape),
        scratch_shapes=list(scratch),
        compiler_params=LIMIT,
        cost_estimate=pl.CostEstimate(flops=flops, bytes_accessed=1 << 20, transcendentals=0),
    )(*scalars, *operands, *after)


def block_at(index, size):
    return pl.ds(pl.multiple_of(index * size, size), size)


def unpack_tiles(count_ref, bits_ref, deg_ref, features_ref, scaled_ref, column_ref, masks_ref):
    column = spread_scale(deg_ref[...], column_ref.shape[0])
    column_ref[...] = column
    scaled_ref[...] = (features_ref[...].astype(f32) * column).astype(bf16)

    def one(slot):
        masks_ref[slot] = unpacked(jnp.where(slot < count_ref[0, 0], bits_ref[0, 0, slot], 0))

    pl.loop(0, masks_ref.shape[0])(one)


def forward_total(rows_ref, cols_ref, masks_ref, source, total):
    slots, tile_size = masks_ref.shape[:2]
    total[...] = jnp.zeros_like(total)

    def one(slot):
        place = block_at(rows_ref[0, 0, slot], tile_size)
        pick = block_at(cols_ref[0, 0, slot], tile_size)
        total[place, :] += jnp.dot(masks_ref[slot], source[pick, :], preferred_element_type=f32)

    pl.loop(0, slots)(one)


def backward_total(rows_ref, cols_ref, masks_ref, source, total):
    slots, tile_size = masks_ref.shape[:2]
    total[...] = jnp.zeros_like(total)

    def one(slot):
        pick = block_at(rows_ref[0, 0, slot], tile_size)
        place = block_at(cols_ref[0, 0, slot], tile_size)
        total[:, place] += jnp.dot(source[:, pick], masks_ref[slot], preferred_element_type=f32)

    pl.loop(0, slots)(one)


def unpacked(packed):
    words, tile_size = packed.shape
    repeated = jnp.broadcast_to(packed[:, None, :], (words, 8, tile_size))
    shifts = lax.broadcasted_iota(jnp.int32, (words, 8, tile_size), 1)
    bit_values = jnp.bitwise_and(jnp.right_shift(repeated, shifts), 1)
    return bit_values.reshape(words * 8, tile_size).astype(f32).astype(bf16)


def spread_scale(deg, size):
    rows = lax.broadcasted_iota(jnp.int32, (size, size), 0)
    columns = lax.broadcasted_iota(jnp.int32, (size, size), 1)
    diagonal = jnp.where(rows == columns, deg.astype(f32).reshape(1, size), 0.0).astype(bf16)
    return jnp.dot(diagonal, jnp.ones((size, size), bf16), preferred_element_type=f32)


def scale_column(deg_ref, column_ref):
    column_ref[...] = spread_scale(deg_ref[...], column_ref.shape[0])


def scale_rows(column_ref, features_ref, rows_ref, cols_ref, scaled_ref):
    scaled_ref[...] = (features_ref[...].astype(f32) * column_ref[...]).astype(bf16)


def build_adjacency(count_ref, rows_ref, cols_ref, bits_ref, after_ref, adjacency_ref):
    slots, words, tile_size = bits_ref.shape[2:]
    count = count_ref[0, 0]
    for slot in range(slots):
        packed = jnp.where(slot < count, bits_ref[0, 0, slot], 0)
        place = block_at(rows_ref[0, 0, slot], tile_size), block_at(cols_ref[0, 0, slot], tile_size)
        adjacency_ref[place] = unpacked(packed)


def rows_of(core, adjacency_ref, size):
    blocks = [
        adjacency_ref[block_at(2 * chip + core, size), :]
        for chip in range(adjacency_ref.shape[0] // (2 * size))
    ]
    return jnp.concatenate(blocks, axis=0)


def forward_other(row_ref, core_ref, adjacency_ref, *refs):
    *blocks, source_ref, other_ref = refs
    size = blocks[0].shape[0]
    for step, block in zip((0, 1, 3, 2), blocks):
        source_ref[block_at(row_ref[0] ^ step, size), :] = block[...]
    rows = rows_of(1 - core_ref[0], adjacency_ref, size)
    total = jnp.dot(rows, source_ref[...], preferred_element_type=f32)
    other_ref[...] = total.astype(bf16).reshape(other_ref.shape)


def forward_mine(core_ref, adjacency_ref, source_ref, mine_ref):
    rows = rows_of(core_ref[0], adjacency_ref, mine_ref.shape[1])
    total = jnp.dot(rows, source_ref[...], preferred_element_type=f32)
    mine_ref[...] = total.reshape(mine_ref.shape)


def forward_chips(chip_ref, mine_ref, received_ref, own_ref, *pieces):
    chip = chip_ref[0]
    own_ref[...] = mine_ref[chip] + received_ref[chip].astype(f32)
    for step, piece in zip((3, 2, 1), pieces):
        peer = chip ^ step
        piece[...] = (mine_ref[peer] + received_ref[peer].astype(f32)).astype(bf16)


def vertex_values(summed, column_ref, deg_ref, weight_ref, cotangent_ref):
    hidden = (summed * column_ref[...]).astype(bf16)
    weight = weight_ref[...]
    pre_act = jnp.dot(hidden, weight, preferred_element_type=f32)
    sigmoid_value = 1.0 / (1.0 + jnp.exp(-pre_act))
    slope = sigmoid_value * (1.0 + pre_act * (1.0 - sigmoid_value))
    slope_term = (cotangent_ref[...].astype(f32) * slope).astype(bf16)
    spread = lax.dot_general(
        weight, slope_term, (((1,), (1,)), ((), ())), preferred_element_type=f32
    )
    back = (spread * deg_ref[...].astype(f32).reshape(1, -1)).astype(bf16)
    local_grad = lax.dot_general(
        hidden, slope_term, (((0,), (0,)), ((), ())), preferred_element_type=f32
    )
    return back, local_grad, pre_act * sigmoid_value


def vertex_chips(column_ref, deg_ref, weight_ref, cotangent_ref, own_ref, *refs):
    *received, sent_ref, active_ref = refs
    summed = own_ref[...] + sum(piece[...].astype(f32) for piece in received)
    sent_ref[0], local_grad, active_ref[...] = vertex_values(
        summed, column_ref, deg_ref, weight_ref, cotangent_ref
    )
    half = sent_ref.shape[2]
    for core in range(2):
        sent_ref[1 + core] = local_grad[:, core * half : (core + 1) * half].astype(bf16)


def write_out(active_ref, out_ref, written_ref):
    out_ref[...] = active_ref[...].astype(bf16)
    written_ref[...] = jnp.zeros_like(written_ref)


def join_chips(chip_ref, core_ref, *refs):
    *blocks, _, joined_ref, own_grad_ref, ordered = refs
    chips = len(blocks)
    for step, block in enumerate(blocks):
        joined_ref[step] = block[0]
        ordered[chip_ref[0] ^ step] = block[1:]
    grad = jnp.sum(ordered[...].astype(f32), axis=0)
    second = core_ref[0] == 1
    own_grad_ref[...] = jnp.where(second, grad[1], grad[0])
    joined_ref[chips] = jnp.where(second, grad[0], grad[1]).astype(bf16)


def backward_rows(row_ref, chip_ref, core_ref, adjacency_ref, own_ref, grad_ref, received_ref, *refs):
    *pieces, source, total = refs
    chips = own_ref.shape[0] - 1
    size = own_ref.shape[2]
    chip, core = chip_ref[0], core_ref[0]
    for step in range(chips):
        peer = 2 * (chip ^ step)
        source[:, block_at(peer + core, size)] = own_ref[step]
        source[:, block_at(peer + 1 - core, size)] = received_ref[step]
    total[...] = jnp.dot(source[...], adjacency_ref[...], preferred_element_type=f32)
    grad = (grad_ref[...] + received_ref[chips].astype(f32)).astype(bf16)
    for step, piece in zip((3, 1, 2, 0), pieces):
        piece[0] = total[:, block_at(row_ref[0] ^ step, size)].astype(bf16)
        piece[1] = grad


def sum_grad(factor, row_ref, *refs):
    *pieces, out_ref, ordered = refs
    for step, piece in zip((3, 1, 2, 0), pieces):
        ordered[row_ref[0] ^ step] = piece[1]
    total = jnp.sum(ordered[...].astype(f32), axis=0) * factor
    out_ref[...] = total.astype(out_ref.dtype)


def input_rows(deg_ref, *refs):
    *pieces, out_ref = refs
    total = sum(piece[0].astype(f32) for piece in pieces)
    out_ref[...] = (total * deg_ref[...].astype(f32).reshape(1, -1)).T.astype(bf16)


def join_halves(core_ref, own_ref, other_ref, out_ref):
    size = own_ref.shape[1]
    half = core_ref[0]
    out_ref[:, block_at(half, size)] = own_ref[...].astype(f32)
    out_ref[:, block_at(1 - half, size)] = other_ref[...].astype(f32)


def forward_all(rows_ref, cols_ref, masks_ref, source_ref, partial_ref, total):
    forward_total(rows_ref, cols_ref, masks_ref, source_ref, total)
    partial_ref[...] = total[...].astype(bf16).reshape(partial_ref.shape)


def vertex_all(column_ref, deg_ref, weight_ref, cotangent_ref, received_ref, act_ref, back_ref, grad_ref):
    summed = jnp.sum(received_ref[...].astype(f32), axis=0)
    back_ref[...], grad_ref[...], active = vertex_values(
        summed, column_ref, deg_ref, weight_ref, cotangent_ref
    )
    act_ref[...] = active.astype(bf16)


def backward_all(rows_ref, cols_ref, masks_ref, gathered_ref, pieces_ref, source, total):
    size = gathered_ref.shape[2]
    for shard in range(gathered_ref.shape[0]):
        source[:, shard * size : (shard + 1) * size] = gathered_ref[shard]
    backward_total(rows_ref, cols_ref, masks_ref, source, total)
    for shard in range(pieces_ref.shape[0]):
        pieces_ref[shard] = total[:, shard * size : (shard + 1) * size].astype(bf16)


def input_all(deg_ref, pieces_ref, out_ref):
    total = jnp.sum(pieces_ref[...].astype(f32), axis=0)
    out_ref[...] = (total * deg_ref[...].astype(f32).reshape(1, -1)).T.astype(bf16)


def exchange(block, axis, shards, distance):
    return lax.ppermute(block, axis, [(shard, shard ^ distance) for shard in range(shards)])


def on_device(features, deg_scale, weight, cotangent, tile_rows, tile_cols, tile_count, tile_bits):
    size, width = features.shape
    height, out_width = weight.shape
    row_shards = lax.axis_size("row")
    col_shards = lax.axis_size("col")
    chips = col_shards // 2
    slots, words, tile_size = tile_bits.shape[2:]
    factor = 1.0 / math.sqrt(row_shards * col_shards * size)
    row = lax.axis_index("row").astype(jnp.int32).reshape(1)
    col = lax.axis_index("col").astype(jnp.int32)
    chip, core = (col // 2).reshape(1), (col % 2).reshape(1)
    forward_scratch = [pltpu.VMEM((col_shards * size, width), f32)]
    backward_scratch = [
        pltpu.VMEM((width, col_shards * size), bf16),
        pltpu.VMEM((width, row_shards * size), f32),
    ]
    prepared = (struct((size, width), bf16), struct((size, width), f32))
    block = struct((width, size), bf16)
    activation = struct((size, out_width), bf16)
    input_shape = struct((size, width), bf16)

    covered = slots * tile_size * tile_size == row_shards * col_shards * size * size
    if row_shards != 4 or col_shards != 8 or not covered:
        scaled, column, masks = call(
            unpack_tiles,
            prepared + (struct((slots, tile_size, tile_size), bf16),),
            (tile_count,),
            (tile_bits, deg_scale, features),
        )
        gathered = lax.all_gather(scaled, "row", axis=0, tiled=True)
        partial_value = call(
            forward_all,
            struct((col_shards, size, width), bf16),
            (tile_rows, tile_cols),
            (masks, gathered),
            forward_scratch,
        )
        received = lax.all_to_all(partial_value, "col", 0, 0)
        activations, back, local_grad = call(
            vertex_all,
            (activation, block, struct((height, out_width), f32)),
            (),
            (column, deg_scale, weight, cotangent, received),
        )
        weight_grad = lax.psum(local_grad, ("row", "col")) * factor
        pieces = call(
            backward_all,
            struct((row_shards, width, size), bf16),
            (tile_rows, tile_cols),
            (masks, lax.all_gather(back, "col")),
            backward_scratch,
        )
        arrived = lax.all_to_all(pieces, "row", 0, 0)
        input_grad = call(input_all, input_shape, (), (deg_scale, arrived))
        return (activations, input_grad, weight_grad)

    column = call(
        scale_column, struct((size, width), f32), (), (deg_scale,), flops=FIRST_FLOPS
    )
    scaled = call(scale_rows, struct((size, width), bf16), (), (column, features, tile_rows, tile_cols))
    adjacency = pl.pallas_call(
        build_adjacency,
        out_shape=struct((col_shards * size, row_shards * size), bf16),
        in_specs=[SMEM, SMEM, SMEM, VMEM, ANY],
        out_specs=VMEM,
        compiler_params=LIMIT,
        cost_estimate=pl.CostEstimate(flops=1 << 20, bytes_accessed=1 << 20, transcendentals=0),
    )(tile_count, tile_rows, tile_cols, tile_bits, scaled)
    far_first = (3, 2, 1)
    blocks = [exchange(scaled, "row", row_shards, step) for step in (1, 3, 2)]
    blocks.insert(0, scaled)
    source, other = call(
        forward_other,
        (struct((row_shards * size, width), bf16), struct((chips, size, width), bf16)),
        (row, core),
        (adjacency, *blocks),
    )
    mine = call(
        forward_mine, struct((chips, size, width), f32), (core,), (adjacency, source)
    )
    own, *pieces = call(
        forward_chips,
        (struct((size, width), f32),) + (struct((size, width), bf16),) * len(far_first),
        (chip,),
        (mine, exchange(other, "col", col_shards, 1)),
    )
    received = [
        exchange(piece, "col", col_shards, 2 * step) for step, piece in zip(far_first, pieces)
    ]
    sent, active = call(
        vertex_chips,
        (struct((3, width, size), bf16), struct((size, out_width), f32)),
        (),
        (column, deg_scale, weight, cotangent, own, *received),
    )
    activations, written = call(write_out, (activation, struct((8, 128), f32)), (), (active,))
    received = [exchange(sent, "col", col_shards, 2 * step) for step in (1, 2, 3)]
    joined, own_grad = call(
        join_chips,
        (struct((chips + 1, width, size), bf16), struct((width, size), f32)),
        (chip, core),
        (sent, *received),
        [pltpu.VMEM((chips, 2, width, size), bf16)],
        after=(written,),
    )
    pieces = call(
        backward_rows,
        (struct((2, width, size), bf16),) * row_shards,
        (row, chip, core),
        (adjacency, joined, own_grad, exchange(joined, "col", col_shards, 1)),
        backward_scratch,
    )
    arrived = [exchange(piece, "row", row_shards, step) for step, piece in zip((3, 1, 2), pieces)]
    arrived.append(pieces[-1])
    half_grad = call(
        functools.partial(sum_grad, factor),
        struct((height, out_width // 2), f32),
        (row,),
        arrived,
        [pltpu.VMEM((row_shards, height, out_width // 2), bf16)],
    )
    other_grad = exchange(half_grad, "col", col_shards, 1)
    input_grad = call(input_rows, input_shape, (), (deg_scale, *arrived))
    weight_grad = call(
        join_halves, struct((height, out_width), f32), (core,), (half_grad, other_grad)
    )
    return (activations, input_grad, weight_grad)


def solution(mesh):
    in_specs = (
        P(("row", "col"), None),
        P(("row", "col")),
        P(),
        P(("row", "col"), None),
        P("row", "col", None),
        P("row", "col", None),
        P("row", "col"),
        P("row", "col", None, None, None),
    )
    out_specs = (P(("row", "col"), None), P(("row", "col"), None), P())
    return jax.shard_map(
        on_device, mesh=mesh, in_specs=in_specs, out_specs=out_specs, check_vma=False
    )
```

```python
import functools
import math

import jax
import jax.numpy as jnp
from jax import lax
from jax.experimental import pallas as pl
from jax.experimental.pallas import tpu as pltpu
from jax.sharding import PartitionSpec as P

VMEM = pl.BlockSpec(memory_space=pltpu.VMEM)
SMEM = pl.BlockSpec(memory_space=pltpu.SMEM)
ANY = pl.BlockSpec(memory_space=pl.ANY)
LIMIT = pltpu.CompilerParams(vmem_limit_bytes=40 * 1024 * 1024)
FIRST_FLOPS = 1 << 32
bf16, f32 = jnp.bfloat16, jnp.float32


def struct(shape, dtype):
    return jax.ShapeDtypeStruct(shape, dtype)


def call(body, out_shape, scalars, operands, scratch=(), flops=1 << 20, after=()):
    single = not isinstance(out_shape, (tuple, list))
    return pl.pallas_call(
        body,
        out_shape=out_shape,
        in_specs=[SMEM] * len(scalars) + [VMEM] * len(operands) + [ANY] * len(after),
        out_specs=VMEM if single else [VMEM] * len(out_shape),
        scratch_shapes=list(scratch),
        compiler_params=LIMIT,
        cost_estimate=pl.CostEstimate(flops=flops, bytes_accessed=1 << 20, transcendentals=0),
    )(*scalars, *operands, *after)


def block_at(index, size):
    return pl.ds(pl.multiple_of(index * size, size), size)


def unpack_tiles(count_ref, bits_ref, deg_ref, features_ref, scaled_ref, column_ref, masks_ref):
    column = spread_scale(deg_ref[...], column_ref.shape[0])
    column_ref[...] = column
    scaled_ref[...] = (features_ref[...].astype(f32) * column).astype(bf16)

    def one(slot):
        masks_ref[slot] = unpacked(jnp.where(slot < count_ref[0, 0], bits_ref[0, 0, slot], 0))

    pl.loop(0, masks_ref.shape[0])(one)


def forward_total(rows_ref, cols_ref, masks_ref, source, total):
    slots, tile_size = masks_ref.shape[:2]
    total[...] = jnp.zeros_like(total)

    def one(slot):
        place = block_at(rows_ref[0, 0, slot], tile_size)
        pick = block_at(cols_ref[0, 0, slot], tile_size)
        total[place, :] += jnp.dot(masks_ref[slot], source[pick, :], preferred_element_type=f32)

    pl.loop(0, slots)(one)


def backward_total(rows_ref, cols_ref, masks_ref, source, total):
    slots, tile_size = masks_ref.shape[:2]
    total[...] = jnp.zeros_like(total)

    def one(slot):
        pick = block_at(rows_ref[0, 0, slot], tile_size)
        place = block_at(cols_ref[0, 0, slot], tile_size)
        total[:, place] += jnp.dot(source[:, pick], masks_ref[slot], preferred_element_type=f32)

    pl.loop(0, slots)(one)


def unpacked(packed):
    words, tile_size = packed.shape
    repeated = jnp.broadcast_to(packed[:, None, :], (words, 8, tile_size))
    shifts = lax.broadcasted_iota(jnp.int32, (words, 8, tile_size), 1)
    bit_values = jnp.bitwise_and(jnp.right_shift(repeated, shifts), 1)
    return bit_values.reshape(words * 8, tile_size).astype(f32).astype(bf16)


def spread_scale(deg, size):
    rows = lax.broadcasted_iota(jnp.int32, (size, size), 0)
    columns = lax.broadcasted_iota(jnp.int32, (size, size), 1)
    diagonal = jnp.where(rows == columns, deg.astype(f32).reshape(1, size), 0.0).astype(bf16)
    return jnp.dot(diagonal, jnp.ones((size, size), bf16), preferred_element_type=f32)


def scale_column(deg_ref, column_ref):
    column_ref[...] = spread_scale(deg_ref[...], column_ref.shape[0])


def scale_rows(column_ref, features_ref, rows_ref, cols_ref, scaled_ref):
    scaled_ref[...] = (features_ref[...].astype(f32) * column_ref[...]).astype(bf16)


def build_adjacency(count_ref, rows_ref, cols_ref, bits_ref, after_ref, adjacency_ref):
    slots, words, tile_size = bits_ref.shape[2:]
    count = count_ref[0, 0]
    for slot in range(slots):
        packed = jnp.where(slot < count, bits_ref[0, 0, slot], 0)
        place = block_at(rows_ref[0, 0, slot], tile_size), block_at(cols_ref[0, 0, slot], tile_size)
        adjacency_ref[place] = unpacked(packed)


def rows_of(core, adjacency_ref, size):
    blocks = [
        adjacency_ref[block_at(2 * chip + core, size), :]
        for chip in range(adjacency_ref.shape[0] // (2 * size))
    ]
    return jnp.concatenate(blocks, axis=0)


def forward_other(row_ref, core_ref, adjacency_ref, *refs):
    *blocks, source_ref, other_ref = refs
    size = blocks[0].shape[0]
    for step, block in zip((0, 1, 3, 2), blocks):
        source_ref[block_at(row_ref[0] ^ step, size), :] = block[...]
    rows = rows_of(1 - core_ref[0], adjacency_ref, size)
    total = jnp.dot(rows, source_ref[...], preferred_element_type=f32)
    other_ref[...] = total.astype(bf16).reshape(other_ref.shape)


def forward_mine(core_ref, adjacency_ref, source_ref, mine_ref):
    rows = rows_of(core_ref[0], adjacency_ref, mine_ref.shape[1])
    total = jnp.dot(rows, source_ref[...], preferred_element_type=f32)
    mine_ref[...] = total.reshape(mine_ref.shape)


def forward_chips(chip_ref, mine_ref, received_ref, own_ref, *pieces):
    chip = chip_ref[0]
    own_ref[...] = mine_ref[chip] + received_ref[chip].astype(f32)
    for step, piece in zip((3, 2, 1), pieces):
        peer = chip ^ step
        piece[...] = (mine_ref[peer] + received_ref[peer].astype(f32)).astype(bf16)


def vertex_values(summed, column_ref, deg_ref, weight_ref, cotangent_ref):
    hidden = (summed * column_ref[...]).astype(bf16)
    weight = weight_ref[...]
    pre_act = jnp.dot(hidden, weight, preferred_element_type=f32)
    sigmoid_value = 1.0 / (1.0 + jnp.exp(-pre_act))
    slope = sigmoid_value * (1.0 + pre_act * (1.0 - sigmoid_value))
    slope_term = (cotangent_ref[...].astype(f32) * slope).astype(bf16)
    spread = lax.dot_general(
        weight, slope_term, (((1,), (1,)), ((), ())), preferred_element_type=f32
    )
    back = (spread * deg_ref[...].astype(f32).reshape(1, -1)).astype(bf16)
    local_grad = lax.dot_general(
        hidden, slope_term, (((0,), (0,)), ((), ())), preferred_element_type=f32
    )
    return back, local_grad, pre_act * sigmoid_value


def vertex_chips(column_ref, deg_ref, weight_ref, cotangent_ref, own_ref, *refs):
    *received, sent_ref, active_ref = refs
    summed = own_ref[...] + sum(piece[...].astype(f32) for piece in received)
    sent_ref[0], local_grad, active_ref[...] = vertex_values(
        summed, column_ref, deg_ref, weight_ref, cotangent_ref
    )
    half = sent_ref.shape[2]
    for core in range(2):
        sent_ref[1 + core] = local_grad[:, core * half : (core + 1) * half].astype(bf16)


def write_out(active_ref, out_ref, written_ref):
    out_ref[...] = active_ref[...].astype(bf16)
    written_ref[...] = jnp.zeros_like(written_ref)


def join_chips(chip_ref, core_ref, *refs):
    *blocks, _, joined_ref, own_grad_ref, ordered = refs
    chips = len(blocks)
    for step, block in enumerate(blocks):
        joined_ref[step] = block[0]
        ordered[chip_ref[0] ^ step] = block[1:]
    grad = jnp.sum(ordered[...].astype(f32), axis=0)
    second = core_ref[0] == 1
    own_grad_ref[...] = jnp.where(second, grad[1], grad[0])
    joined_ref[chips] = jnp.where(second, grad[0], grad[1]).astype(bf16)


def chip_blocks(chip, blocks_ref, source):
    size = source.shape[0]
    for step in range(source.shape[1] // size):
        source[:, block_at(chip ^ step, size)] = blocks_ref[step]
    return source[...]


def backward_own(chip_ref, core_ref, adjacency_ref, joined_ref, total_ref, source):
    blocks = chip_blocks(chip_ref[0], joined_ref, source)
    rows = rows_of(core_ref[0], adjacency_ref, source.shape[0])
    total_ref[...] = jnp.dot(blocks, rows, preferred_element_type=f32)


def backward_rows(
    row_ref, chip_ref, core_ref, adjacency_ref, own_ref, grad_ref, received_ref, *refs
):
    *pieces, source, total = refs
    chips, size = received_ref.shape[0] - 1, received_ref.shape[2]
    blocks = chip_blocks(chip_ref[0], received_ref, source)
    rows = rows_of(1 - core_ref[0], adjacency_ref, size)
    total[...] = own_ref[...] + jnp.dot(blocks, rows, preferred_element_type=f32)
    grad = (grad_ref[...] + received_ref[chips].astype(f32)).astype(bf16)
    for step, piece in zip((3, 1, 2, 0), pieces):
        piece[0] = total[:, block_at(row_ref[0] ^ step, size)].astype(bf16)
        piece[1] = grad


def sum_grad(factor, row_ref, *refs):
    *pieces, out_ref, ordered = refs
    for step, piece in zip((3, 1, 2, 0), pieces):
        ordered[row_ref[0] ^ step] = piece[1]
    total = jnp.sum(ordered[...].astype(f32), axis=0) * factor
    out_ref[...] = total.astype(out_ref.dtype)


def input_rows(deg_ref, *refs):
    *pieces, out_ref = refs
    total = sum(piece[0].astype(f32) for piece in pieces)
    out_ref[...] = (total * deg_ref[...].astype(f32).reshape(1, -1)).T.astype(bf16)


def join_halves(core_ref, own_ref, other_ref, out_ref):
    size = own_ref.shape[1]
    half = core_ref[0]
    out_ref[:, block_at(half, size)] = own_ref[...].astype(f32)
    out_ref[:, block_at(1 - half, size)] = other_ref[...].astype(f32)


def forward_all(rows_ref, cols_ref, masks_ref, source_ref, partial_ref, total):
    forward_total(rows_ref, cols_ref, masks_ref, source_ref, total)
    partial_ref[...] = total[...].astype(bf16).reshape(partial_ref.shape)


def vertex_all(column_ref, deg_ref, weight_ref, cotangent_ref, received_ref, act_ref, back_ref, grad_ref):
    summed = jnp.sum(received_ref[...].astype(f32), axis=0)
    back_ref[...], grad_ref[...], active = vertex_values(
        summed, column_ref, deg_ref, weight_ref, cotangent_ref
    )
    act_ref[...] = active.astype(bf16)


def backward_all(rows_ref, cols_ref, masks_ref, gathered_ref, pieces_ref, source, total):
    size = gathered_ref.shape[2]
    for shard in range(gathered_ref.shape[0]):
        source[:, shard * size : (shard + 1) * size] = gathered_ref[shard]
    backward_total(rows_ref, cols_ref, masks_ref, source, total)
    for shard in range(pieces_ref.shape[0]):
        pieces_ref[shard] = total[:, shard * size : (shard + 1) * size].astype(bf16)


def input_all(deg_ref, pieces_ref, out_ref):
    total = jnp.sum(pieces_ref[...].astype(f32), axis=0)
    out_ref[...] = (total * deg_ref[...].astype(f32).reshape(1, -1)).T.astype(bf16)


def exchange(block, axis, shards, distance):
    return lax.ppermute(block, axis, [(shard, shard ^ distance) for shard in range(shards)])


def on_device(features, deg_scale, weight, cotangent, tile_rows, tile_cols, tile_count, tile_bits):
    size, width = features.shape
    height, out_width = weight.shape
    row_shards = lax.axis_size("row")
    col_shards = lax.axis_size("col")
    chips = col_shards // 2
    slots, words, tile_size = tile_bits.shape[2:]
    factor = 1.0 / math.sqrt(row_shards * col_shards * size)
    row = lax.axis_index("row").astype(jnp.int32).reshape(1)
    col = lax.axis_index("col").astype(jnp.int32)
    chip, core = (col // 2).reshape(1), (col % 2).reshape(1)
    forward_scratch = [pltpu.VMEM((col_shards * size, width), f32)]
    backward_scratch = [
        pltpu.VMEM((width, col_shards * size), bf16),
        pltpu.VMEM((width, row_shards * size), f32),
    ]
    prepared = (struct((size, width), bf16), struct((size, width), f32))
    block = struct((width, size), bf16)
    activation = struct((size, out_width), bf16)
    input_shape = struct((size, width), bf16)

    covered = slots * tile_size * tile_size == row_shards * col_shards * size * size
    if row_shards != 4 or col_shards != 8 or not covered:
        scaled, column, masks = call(
            unpack_tiles,
            prepared + (struct((slots, tile_size, tile_size), bf16),),
            (tile_count,),
            (tile_bits, deg_scale, features),
        )
        gathered = lax.all_gather(scaled, "row", axis=0, tiled=True)
        partial_value = call(
            forward_all,
            struct((col_shards, size, width), bf16),
            (tile_rows, tile_cols),
            (masks, gathered),
            forward_scratch,
        )
        received = lax.all_to_all(partial_value, "col", 0, 0)
        activations, back, local_grad = call(
            vertex_all,
            (activation, block, struct((height, out_width), f32)),
            (),
            (column, deg_scale, weight, cotangent, received),
        )
        weight_grad = lax.psum(local_grad, ("row", "col")) * factor
        pieces = call(
            backward_all,
            struct((row_shards, width, size), bf16),
            (tile_rows, tile_cols),
            (masks, lax.all_gather(back, "col")),
            backward_scratch,
        )
        arrived = lax.all_to_all(pieces, "row", 0, 0)
        input_grad = call(input_all, input_shape, (), (deg_scale, arrived))
        return (activations, input_grad, weight_grad)

    column = call(
        scale_column, struct((size, width), f32), (), (deg_scale,), flops=FIRST_FLOPS
    )
    scaled = call(scale_rows, struct((size, width), bf16), (), (column, features, tile_rows, tile_cols))
    adjacency = pl.pallas_call(
        build_adjacency,
        out_shape=struct((col_shards * size, row_shards * size), bf16),
        in_specs=[SMEM, SMEM, SMEM, VMEM, ANY],
        out_specs=VMEM,
        compiler_params=LIMIT,
        cost_estimate=pl.CostEstimate(flops=1 << 20, bytes_accessed=1 << 20, transcendentals=0),
    )(tile_count, tile_rows, tile_cols, tile_bits, scaled)
    far_first = (3, 2, 1)
    blocks = [exchange(scaled, "row", row_shards, step) for step in (1, 3, 2)]
    blocks.insert(0, scaled)
    source, other = call(
        forward_other,
        (struct((row_shards * size, width), bf16), struct((chips, size, width), bf16)),
        (row, core),
        (adjacency, *blocks),
    )
    mine = call(
        forward_mine, struct((chips, size, width), f32), (core,), (adjacency, source)
    )
    own, *pieces = call(
        forward_chips,
        (struct((size, width), f32),) + (struct((size, width), bf16),) * len(far_first),
        (chip,),
        (mine, exchange(other, "col", col_shards, 1)),
    )
    received = [
        exchange(piece, "col", col_shards, 2 * step) for step, piece in zip(far_first, pieces)
    ]
    sent, active = call(
        vertex_chips,
        (struct((3, width, size), bf16), struct((size, out_width), f32)),
        (),
        (column, deg_scale, weight, cotangent, own, *received),
    )
    activations, written = call(write_out, (activation, struct((8, 128), f32)), (), (active,))
    received = [exchange(sent, "col", col_shards, 2 * step) for step in (1, 2, 3)]
    joined, own_grad = call(
        join_chips,
        (struct((chips + 1, width, size), bf16), struct((width, size), f32)),
        (chip, core),
        (sent, *received),
        [pltpu.VMEM((chips, 2, width, size), bf16)],
        after=(written,),
    )
    half_source = pltpu.VMEM((width, chips * size), bf16)
    own_total = call(
        backward_own,
        struct((width, row_shards * size), f32),
        (chip, core),
        (adjacency, joined),
        [half_source],
    )
    pieces = call(
        backward_rows,
        (struct((2, width, size), bf16),) * row_shards,
        (row, chip, core),
        (adjacency, own_total, own_grad, exchange(joined, "col", col_shards, 1)),
        [half_source, pltpu.VMEM((width, row_shards * size), f32)],
    )
    arrived = [exchange(piece, "row", row_shards, step) for step, piece in zip((3, 1, 2), pieces)]
    arrived.append(pieces[-1])
    half_grad = call(
        functools.partial(sum_grad, factor),
        struct((height, out_width // 2), f32),
        (row,),
        arrived,
        [pltpu.VMEM((row_shards, height, out_width // 2), bf16)],
    )
    other_grad = exchange(half_grad, "col", col_shards, 1)
    input_grad = call(input_rows, input_shape, (), (deg_scale, *arrived))
    weight_grad = call(
        join_halves, struct((height, out_width), f32), (core,), (half_grad, other_grad)
    )
    return (activations, input_grad, weight_grad)


def solution(mesh):
    in_specs = (
        P(("row", "col"), None),
        P(("row", "col")),
        P(),
        P(("row", "col"), None),
        P("row", "col", None),
        P("row", "col", None),
        P("row", "col"),
        P("row", "col", None, None, None),
    )
    out_specs = (P(("row", "col"), None), P(("row", "col"), None), P())
    return jax.shard_map(
        on_device, mesh=mesh, in_specs=in_specs, out_specs=out_specs, check_vma=False
    )
```

```python
import functools
import math

import jax
import jax.numpy as jnp
from jax import lax
from jax.experimental import pallas as pl
from jax.experimental.pallas import tpu as pltpu
from jax.sharding import PartitionSpec as P

VMEM = pl.BlockSpec(memory_space=pltpu.VMEM)
SMEM = pl.BlockSpec(memory_space=pltpu.SMEM)
ANY = pl.BlockSpec(memory_space=pl.ANY)
LIMIT = pltpu.CompilerParams(vmem_limit_bytes=40 * 1024 * 1024)
FIRST_FLOPS = 1 << 32
bf16, f32 = jnp.bfloat16, jnp.float32


def struct(shape, dtype):
    return jax.ShapeDtypeStruct(shape, dtype)


def call(body, out_shape, scalars, operands, scratch=(), flops=1 << 20, after=()):
    single = not isinstance(out_shape, (tuple, list))
    return pl.pallas_call(
        body,
        out_shape=out_shape,
        in_specs=[SMEM] * len(scalars) + [VMEM] * len(operands) + [ANY] * len(after),
        out_specs=VMEM if single else [VMEM] * len(out_shape),
        scratch_shapes=list(scratch),
        compiler_params=LIMIT,
        cost_estimate=pl.CostEstimate(flops=flops, bytes_accessed=1 << 20, transcendentals=0),
    )(*scalars, *operands, *after)


def block_at(index, size):
    return pl.ds(pl.multiple_of(index * size, size), size)


def unpack_tiles(count_ref, bits_ref, deg_ref, features_ref, scaled_ref, column_ref, masks_ref):
    column = spread_scale(deg_ref[...], column_ref.shape[0])
    column_ref[...] = column
    scaled_ref[...] = (features_ref[...].astype(f32) * column).astype(bf16)

    def one(slot):
        masks_ref[slot] = unpacked(jnp.where(slot < count_ref[0, 0], bits_ref[0, 0, slot], 0))

    pl.loop(0, masks_ref.shape[0])(one)


def forward_total(rows_ref, cols_ref, masks_ref, source, total):
    slots, tile_size = masks_ref.shape[:2]
    total[...] = jnp.zeros_like(total)

    def one(slot):
        place = block_at(rows_ref[0, 0, slot], tile_size)
        pick = block_at(cols_ref[0, 0, slot], tile_size)
        total[place, :] += jnp.dot(masks_ref[slot], source[pick, :], preferred_element_type=f32)

    pl.loop(0, slots)(one)


def backward_total(rows_ref, cols_ref, masks_ref, source, total):
    slots, tile_size = masks_ref.shape[:2]
    total[...] = jnp.zeros_like(total)

    def one(slot):
        pick = block_at(rows_ref[0, 0, slot], tile_size)
        place = block_at(cols_ref[0, 0, slot], tile_size)
        total[:, place] += jnp.dot(source[:, pick], masks_ref[slot], preferred_element_type=f32)

    pl.loop(0, slots)(one)


def unpacked(packed):
    words, tile_size = packed.shape
    repeated = jnp.broadcast_to(packed[:, None, :], (words, 8, tile_size))
    shifts = lax.broadcasted_iota(jnp.int32, (words, 8, tile_size), 1)
    bit_values = jnp.bitwise_and(jnp.right_shift(repeated, shifts), 1)
    return bit_values.reshape(words * 8, tile_size).astype(f32).astype(bf16)


def spread_scale(deg, size):
    rows = lax.broadcasted_iota(jnp.int32, (size, size), 0)
    columns = lax.broadcasted_iota(jnp.int32, (size, size), 1)
    diagonal = jnp.where(rows == columns, deg.astype(f32).reshape(1, size), 0.0).astype(bf16)
    return jnp.dot(diagonal, jnp.ones((size, size), bf16), preferred_element_type=f32)


def scale_column(deg_ref, column_ref):
    column_ref[...] = spread_scale(deg_ref[...], column_ref.shape[0])


def scale_rows(column_ref, features_ref, rows_ref, cols_ref, scaled_ref):
    scaled_ref[...] = (features_ref[...].astype(f32) * column_ref[...]).astype(bf16)


def build_adjacency(count_ref, rows_ref, cols_ref, bits_ref, after_ref, adjacency_ref):
    slots, words, tile_size = bits_ref.shape[2:]
    count = count_ref[0, 0]
    for slot in range(slots):
        packed = jnp.where(slot < count, bits_ref[0, 0, slot], 0)
        place = block_at(rows_ref[0, 0, slot], tile_size), block_at(cols_ref[0, 0, slot], tile_size)
        adjacency_ref[place] = unpacked(packed)


def rows_of(core, adjacency_ref, size):
    blocks = [
        adjacency_ref[block_at(2 * chip + core, size), :]
        for chip in range(adjacency_ref.shape[0] // (2 * size))
    ]
    return jnp.concatenate(blocks, axis=0)


def forward_other(row_ref, core_ref, adjacency_ref, *refs):
    *blocks, source_ref, other_ref = refs
    size = blocks[0].shape[0]
    for step, block in zip((0, 1, 3, 2), blocks):
        source_ref[block_at(row_ref[0] ^ step, size), :] = block[...]
    rows = rows_of(1 - core_ref[0], adjacency_ref, size)
    total = jnp.dot(rows, source_ref[...], preferred_element_type=f32)
    other_ref[...] = total.astype(bf16).reshape(other_ref.shape)


def forward_mine(core_ref, adjacency_ref, source_ref, mine_ref):
    rows = rows_of(core_ref[0], adjacency_ref, mine_ref.shape[1])
    total = jnp.dot(rows, source_ref[...], preferred_element_type=f32)
    mine_ref[...] = total.reshape(mine_ref.shape)


def forward_chips(chip_ref, mine_ref, received_ref, own_ref, *pieces):
    chip = chip_ref[0]
    own_ref[...] = mine_ref[chip] + received_ref[chip].astype(f32)
    for step, piece in zip((3, 2, 1), pieces):
        peer = chip ^ step
        piece[...] = (mine_ref[peer] + received_ref[peer].astype(f32)).astype(bf16)


def vertex_values(summed, column_ref, deg_ref, weight_ref, cotangent_ref):
    hidden = (summed * column_ref[...]).astype(bf16)
    weight = weight_ref[...]
    pre_act = jnp.dot(hidden, weight, preferred_element_type=f32)
    sigmoid_value = 1.0 / (1.0 + jnp.exp(-pre_act))
    slope = sigmoid_value * (1.0 + pre_act * (1.0 - sigmoid_value))
    slope_term = (cotangent_ref[...].astype(f32) * slope).astype(bf16)
    spread = lax.dot_general(
        weight, slope_term, (((1,), (1,)), ((), ())), preferred_element_type=f32
    )
    back = (spread * deg_ref[...].astype(f32).reshape(1, -1)).astype(bf16)
    local_grad = lax.dot_general(
        hidden, slope_term, (((0,), (0,)), ((), ())), preferred_element_type=f32
    )
    return back, local_grad, pre_act * sigmoid_value


def vertex_chips(column_ref, deg_ref, weight_ref, cotangent_ref, own_ref, *refs):
    *received, sent_ref, active_ref = refs
    summed = own_ref[...] + sum(piece[...].astype(f32) for piece in received)
    sent_ref[0], local_grad, active_ref[...] = vertex_values(
        summed, column_ref, deg_ref, weight_ref, cotangent_ref
    )
    half = sent_ref.shape[2]
    for core in range(2):
        sent_ref[1 + core] = local_grad[:, core * half : (core + 1) * half].astype(bf16)


def write_out(active_ref, out_ref, written_ref):
    out_ref[...] = active_ref[...].astype(bf16)
    written_ref[...] = jnp.zeros_like(written_ref)


def join_chips(chip_ref, core_ref, *refs):
    *blocks, _, joined_ref, own_grad_ref, ordered = refs
    chips = len(blocks)
    for step, block in enumerate(blocks):
        joined_ref[step] = block[0]
        ordered[chip_ref[0] ^ step] = block[1:]
    grad = jnp.sum(ordered[...].astype(f32), axis=0)
    second = core_ref[0] == 1
    own_grad_ref[...] = jnp.where(second, grad[1], grad[0])
    joined_ref[chips] = jnp.where(second, grad[0], grad[1]).astype(bf16)


def chip_blocks(chip, blocks_ref, source):
    size = source.shape[0]
    for step in range(source.shape[1] // size):
        source[:, block_at(chip ^ step, size)] = blocks_ref[step]
    return source[...]


def backward_own(chip_ref, core_ref, adjacency_ref, joined_ref, total_ref, source):
    blocks = chip_blocks(chip_ref[0], joined_ref, source)
    rows = rows_of(core_ref[0], adjacency_ref, source.shape[0])
    total_ref[...] = jnp.dot(blocks, rows, preferred_element_type=f32)


def backward_rows(
    row_ref, chip_ref, core_ref, adjacency_ref, own_ref, grad_ref, received_ref, *refs
):
    *pieces, source, total = refs
    chips, size = received_ref.shape[0] - 1, received_ref.shape[2]
    blocks = chip_blocks(chip_ref[0], received_ref, source)
    rows = rows_of(1 - core_ref[0], adjacency_ref, size)
    total[...] = own_ref[...] + jnp.dot(blocks, rows, preferred_element_type=f32)
    grad = (grad_ref[...] + received_ref[chips].astype(f32)).astype(bf16)
    for step, piece in zip((1, 2, 3, 0), pieces):
        owner = lax.rem(row_ref[0] + step, len(pieces))
        piece[0] = total[:, block_at(owner, size)].astype(bf16)
        piece[1] = grad


def sum_grad(factor, row_ref, *refs):
    *pieces, out_ref, ordered = refs
    for step, piece in zip((3, 2, 1, 0), pieces):
        ordered[lax.rem(row_ref[0] + step, len(pieces))] = piece[1]
    total = jnp.sum(ordered[...].astype(f32), axis=0) * factor
    out_ref[...] = total.astype(out_ref.dtype)


def input_rows(deg_ref, *refs):
    *pieces, out_ref = refs
    total = sum(piece[0].astype(f32) for piece in pieces)
    out_ref[...] = (total * deg_ref[...].astype(f32).reshape(1, -1)).T.astype(bf16)


def join_halves(core_ref, own_ref, other_ref, out_ref):
    size = own_ref.shape[1]
    half = core_ref[0]
    out_ref[:, block_at(half, size)] = own_ref[...].astype(f32)
    out_ref[:, block_at(1 - half, size)] = other_ref[...].astype(f32)


def forward_all(rows_ref, cols_ref, masks_ref, source_ref, partial_ref, total):
    forward_total(rows_ref, cols_ref, masks_ref, source_ref, total)
    partial_ref[...] = total[...].astype(bf16).reshape(partial_ref.shape)


def vertex_all(column_ref, deg_ref, weight_ref, cotangent_ref, received_ref, act_ref, back_ref, grad_ref):
    summed = jnp.sum(received_ref[...].astype(f32), axis=0)
    back_ref[...], grad_ref[...], active = vertex_values(
        summed, column_ref, deg_ref, weight_ref, cotangent_ref
    )
    act_ref[...] = active.astype(bf16)


def backward_all(rows_ref, cols_ref, masks_ref, gathered_ref, pieces_ref, source, total):
    size = gathered_ref.shape[2]
    for shard in range(gathered_ref.shape[0]):
        source[:, shard * size : (shard + 1) * size] = gathered_ref[shard]
    backward_total(rows_ref, cols_ref, masks_ref, source, total)
    for shard in range(pieces_ref.shape[0]):
        pieces_ref[shard] = total[:, shard * size : (shard + 1) * size].astype(bf16)


def input_all(deg_ref, pieces_ref, out_ref):
    total = jnp.sum(pieces_ref[...].astype(f32), axis=0)
    out_ref[...] = (total * deg_ref[...].astype(f32).reshape(1, -1)).T.astype(bf16)


def exchange(block, axis, shards, distance):
    return lax.ppermute(block, axis, [(shard, shard ^ distance) for shard in range(shards)])


def shifted(block, axis, shards, step):
    return lax.ppermute(block, axis, [(shard, (shard + step) % shards) for shard in range(shards)])


def on_device(features, deg_scale, weight, cotangent, tile_rows, tile_cols, tile_count, tile_bits):
    size, width = features.shape
    height, out_width = weight.shape
    row_shards = lax.axis_size("row")
    col_shards = lax.axis_size("col")
    chips = col_shards // 2
    slots, words, tile_size = tile_bits.shape[2:]
    factor = 1.0 / math.sqrt(row_shards * col_shards * size)
    row = lax.axis_index("row").astype(jnp.int32).reshape(1)
    col = lax.axis_index("col").astype(jnp.int32)
    chip, core = (col // 2).reshape(1), (col % 2).reshape(1)
    forward_scratch = [pltpu.VMEM((col_shards * size, width), f32)]
    backward_scratch = [
        pltpu.VMEM((width, col_shards * size), bf16),
        pltpu.VMEM((width, row_shards * size), f32),
    ]
    prepared = (struct((size, width), bf16), struct((size, width), f32))
    block = struct((width, size), bf16)
    activation = struct((size, out_width), bf16)
    input_shape = struct((size, width), bf16)

    covered = slots * tile_size * tile_size == row_shards * col_shards * size * size
    if row_shards != 4 or col_shards != 8 or not covered:
        scaled, column, masks = call(
            unpack_tiles,
            prepared + (struct((slots, tile_size, tile_size), bf16),),
            (tile_count,),
            (tile_bits, deg_scale, features),
        )
        gathered = lax.all_gather(scaled, "row", axis=0, tiled=True)
        partial_value = call(
            forward_all,
            struct((col_shards, size, width), bf16),
            (tile_rows, tile_cols),
            (masks, gathered),
            forward_scratch,
        )
        received = lax.all_to_all(partial_value, "col", 0, 0)
        activations, back, local_grad = call(
            vertex_all,
            (activation, block, struct((height, out_width), f32)),
            (),
            (column, deg_scale, weight, cotangent, received),
        )
        weight_grad = lax.psum(local_grad, ("row", "col")) * factor
        pieces = call(
            backward_all,
            struct((row_shards, width, size), bf16),
            (tile_rows, tile_cols),
            (masks, lax.all_gather(back, "col")),
            backward_scratch,
        )
        arrived = lax.all_to_all(pieces, "row", 0, 0)
        input_grad = call(input_all, input_shape, (), (deg_scale, arrived))
        return (activations, input_grad, weight_grad)

    column = call(
        scale_column, struct((size, width), f32), (), (deg_scale,), flops=FIRST_FLOPS
    )
    scaled = call(scale_rows, struct((size, width), bf16), (), (column, features, tile_rows, tile_cols))
    adjacency = pl.pallas_call(
        build_adjacency,
        out_shape=struct((col_shards * size, row_shards * size), bf16),
        in_specs=[SMEM, SMEM, SMEM, VMEM, ANY],
        out_specs=VMEM,
        compiler_params=LIMIT,
        cost_estimate=pl.CostEstimate(flops=1 << 20, bytes_accessed=1 << 20, transcendentals=0),
    )(tile_count, tile_rows, tile_cols, tile_bits, scaled)
    far_first = (3, 2, 1)
    blocks = [exchange(scaled, "row", row_shards, step) for step in (1, 3, 2)]
    blocks.insert(0, scaled)
    source, other = call(
        forward_other,
        (struct((row_shards * size, width), bf16), struct((chips, size, width), bf16)),
        (row, core),
        (adjacency, *blocks),
    )
    mine = call(
        forward_mine, struct((chips, size, width), f32), (core,), (adjacency, source)
    )
    own, *pieces = call(
        forward_chips,
        (struct((size, width), f32),) + (struct((size, width), bf16),) * len(far_first),
        (chip,),
        (mine, exchange(other, "col", col_shards, 1)),
    )
    received = [
        exchange(piece, "col", col_shards, 2 * step) for step, piece in zip(far_first, pieces)
    ]
    sent, active = call(
        vertex_chips,
        (struct((3, width, size), bf16), struct((size, out_width), f32)),
        (),
        (column, deg_scale, weight, cotangent, own, *received),
    )
    activations, written = call(write_out, (activation, struct((8, 128), f32)), (), (active,))
    received = [exchange(sent, "col", col_shards, 2 * step) for step in (1, 2, 3)]
    joined, own_grad = call(
        join_chips,
        (struct((chips + 1, width, size), bf16), struct((width, size), f32)),
        (chip, core),
        (sent, *received),
        [pltpu.VMEM((chips, 2, width, size), bf16)],
        after=(written,),
    )
    half_source = pltpu.VMEM((width, chips * size), bf16)
    own_total = call(
        backward_own,
        struct((width, row_shards * size), f32),
        (chip, core),
        (adjacency, joined),
        [half_source],
    )
    pieces = call(
        backward_rows,
        (struct((2, width, size), bf16),) * row_shards,
        (row, chip, core),
        (adjacency, own_total, own_grad, exchange(joined, "col", col_shards, 1)),
        [half_source, pltpu.VMEM((width, row_shards * size), f32)],
    )
    arrived = [shifted(piece, "row", row_shards, step) for step, piece in zip((1, 2, 3), pieces)]
    arrived.append(pieces[-1])
    half_grad = call(
        functools.partial(sum_grad, factor),
        struct((height, out_width // 2), f32),
        (row,),
        arrived,
        [pltpu.VMEM((row_shards, height, out_width // 2), bf16)],
    )
    other_grad = exchange(half_grad, "col", col_shards, 1)
    input_grad = call(input_rows, input_shape, (), (deg_scale, *arrived))
    weight_grad = call(
        join_halves, struct((height, out_width), f32), (core,), (half_grad, other_grad)
    )
    return (activations, input_grad, weight_grad)


def solution(mesh):
    in_specs = (
        P(("row", "col"), None),
        P(("row", "col")),
        P(),
        P(("row", "col"), None),
        P("row", "col", None),
        P("row", "col", None),
        P("row", "col"),
        P("row", "col", None, None, None),
    )
    out_specs = (P(("row", "col"), None), P(("row", "col"), None), P())
    return jax.shard_map(
        on_device, mesh=mesh, in_specs=in_specs, out_specs=out_specs, check_vma=False
    )
```

```python
import functools
import math

import jax
import jax.numpy as jnp
from jax import lax
from jax.experimental import pallas as pl
from jax.experimental.pallas import tpu as pltpu
from jax.sharding import PartitionSpec as P

VMEM = pl.BlockSpec(memory_space=pltpu.VMEM)
SMEM = pl.BlockSpec(memory_space=pltpu.SMEM)
ANY = pl.BlockSpec(memory_space=pl.ANY)
LIMIT = pltpu.CompilerParams(vmem_limit_bytes=40 * 1024 * 1024)
FIRST_FLOPS = 1 << 32
bf16, f32 = jnp.bfloat16, jnp.float32


def struct(shape, dtype):
    return jax.ShapeDtypeStruct(shape, dtype)


def call(body, out_shape, scalars, operands, scratch=(), flops=1 << 20, after=()):
    single = not isinstance(out_shape, (tuple, list))
    return pl.pallas_call(
        body,
        out_shape=out_shape,
        in_specs=[SMEM] * len(scalars) + [VMEM] * len(operands) + [ANY] * len(after),
        out_specs=VMEM if single else [VMEM] * len(out_shape),
        scratch_shapes=list(scratch),
        compiler_params=LIMIT,
        cost_estimate=pl.CostEstimate(flops=flops, bytes_accessed=1 << 20, transcendentals=0),
    )(*scalars, *operands, *after)


def block_at(index, size):
    return pl.ds(pl.multiple_of(index * size, size), size)


def unpack_tiles(count_ref, bits_ref, deg_ref, features_ref, scaled_ref, column_ref, masks_ref):
    column = spread_scale(deg_ref[...], column_ref.shape[0])
    column_ref[...] = column
    scaled_ref[...] = (features_ref[...].astype(f32) * column).astype(bf16)

    def one(slot):
        masks_ref[slot] = unpacked(jnp.where(slot < count_ref[0, 0], bits_ref[0, 0, slot], 0))

    pl.loop(0, masks_ref.shape[0])(one)


def forward_total(rows_ref, cols_ref, masks_ref, source, total):
    slots, tile_size = masks_ref.shape[:2]
    total[...] = jnp.zeros_like(total)

    def one(slot):
        place = block_at(rows_ref[0, 0, slot], tile_size)
        pick = block_at(cols_ref[0, 0, slot], tile_size)
        total[place, :] += jnp.dot(masks_ref[slot], source[pick, :], preferred_element_type=f32)

    pl.loop(0, slots)(one)


def backward_total(rows_ref, cols_ref, masks_ref, source, total):
    slots, tile_size = masks_ref.shape[:2]
    total[...] = jnp.zeros_like(total)

    def one(slot):
        pick = block_at(rows_ref[0, 0, slot], tile_size)
        place = block_at(cols_ref[0, 0, slot], tile_size)
        total[:, place] += jnp.dot(source[:, pick], masks_ref[slot], preferred_element_type=f32)

    pl.loop(0, slots)(one)


def unpacked(packed):
    words, tile_size = packed.shape
    repeated = jnp.broadcast_to(packed[:, None, :], (words, 8, tile_size))
    shifts = lax.broadcasted_iota(jnp.int32, (words, 8, tile_size), 1)
    bit_values = jnp.bitwise_and(jnp.right_shift(repeated, shifts), 1)
    return bit_values.reshape(words * 8, tile_size).astype(f32).astype(bf16)


def spread_scale(deg, size):
    rows = lax.broadcasted_iota(jnp.int32, (size, size), 0)
    columns = lax.broadcasted_iota(jnp.int32, (size, size), 1)
    diagonal = jnp.where(rows == columns, deg.astype(f32).reshape(1, size), 0.0).astype(bf16)
    return jnp.dot(diagonal, jnp.ones((size, size), bf16), preferred_element_type=f32)


def scale_column(deg_ref, column_ref):
    column_ref[...] = spread_scale(deg_ref[...], column_ref.shape[0])


def scale_rows(column_ref, features_ref, rows_ref, cols_ref, scaled_ref):
    scaled_ref[...] = (features_ref[...].astype(f32) * column_ref[...]).astype(bf16)


def build_adjacency(count_ref, rows_ref, cols_ref, bits_ref, after_ref, adjacency_ref):
    slots, words, tile_size = bits_ref.shape[2:]
    count = count_ref[0, 0]
    for slot in range(slots):
        packed = jnp.where(slot < count, bits_ref[0, 0, slot], 0)
        place = block_at(rows_ref[0, 0, slot], tile_size), block_at(cols_ref[0, 0, slot], tile_size)
        adjacency_ref[place] = unpacked(packed)


def rows_of(core, adjacency_ref, size):
    blocks = [
        adjacency_ref[block_at(2 * chip + core, size), :]
        for chip in range(adjacency_ref.shape[0] // (2 * size))
    ]
    return jnp.concatenate(blocks, axis=0)


def forward_other(row_ref, core_ref, adjacency_ref, *refs):
    *blocks, source_ref, other_ref = refs
    size = blocks[0].shape[0]
    for step, block in zip((0, 1, 3, 2), blocks):
        source_ref[block_at(row_ref[0] ^ step, size), :] = block[...]
    rows = rows_of(1 - core_ref[0], adjacency_ref, size)
    total = jnp.dot(rows, source_ref[...], preferred_element_type=f32)
    other_ref[...] = total.astype(bf16).reshape(other_ref.shape)


def forward_mine(core_ref, adjacency_ref, source_ref, mine_ref):
    rows = rows_of(core_ref[0], adjacency_ref, mine_ref.shape[1])
    total = jnp.dot(rows, source_ref[...], preferred_element_type=f32)
    mine_ref[...] = total.reshape(mine_ref.shape)


def forward_chips(chip_ref, mine_ref, received_ref, own_ref, *pieces):
    chip = chip_ref[0]
    own_ref[...] = mine_ref[chip] + received_ref[chip].astype(f32)
    for step, piece in zip((3, 2, 1), pieces):
        peer = chip ^ step
        piece[...] = (mine_ref[peer] + received_ref[peer].astype(f32)).astype(bf16)


def vertex_values(summed, column_ref, deg_ref, weight_ref, cotangent_ref):
    hidden = (summed * column_ref[...]).astype(bf16)
    weight = weight_ref[...]
    pre_act = jnp.dot(hidden, weight, preferred_element_type=f32)
    sigmoid_value = 1.0 / (1.0 + jnp.exp(-pre_act))
    slope = sigmoid_value * (1.0 + pre_act * (1.0 - sigmoid_value))
    slope_term = (cotangent_ref[...].astype(f32) * slope).astype(bf16)
    spread = lax.dot_general(
        weight, slope_term, (((1,), (1,)), ((), ())), preferred_element_type=f32
    )
    back = (spread * deg_ref[...].astype(f32).reshape(1, -1)).astype(bf16)
    local_grad = lax.dot_general(
        hidden, slope_term, (((0,), (0,)), ((), ())), preferred_element_type=f32
    )
    return back, local_grad, pre_act * sigmoid_value


def vertex_chips(column_ref, deg_ref, weight_ref, cotangent_ref, own_ref, *refs):
    *received, sent_ref, active_ref = refs
    summed = own_ref[...] + sum(piece[...].astype(f32) for piece in received)
    sent_ref[0], local_grad, active_ref[...] = vertex_values(
        summed, column_ref, deg_ref, weight_ref, cotangent_ref
    )
    half = sent_ref.shape[2]
    for core in range(2):
        sent_ref[1 + core] = local_grad[:, core * half : (core + 1) * half].astype(bf16)


def write_out(active_ref, out_ref, written_ref):
    out_ref[...] = active_ref[...].astype(bf16)
    written_ref[...] = jnp.zeros_like(written_ref)


def join_chips(chip_ref, core_ref, *refs):
    *blocks, _, joined_ref, own_grad_ref, ordered = refs
    chips = len(blocks)
    for step, block in enumerate(blocks):
        joined_ref[step] = block[0]
        ordered[chip_ref[0] ^ step] = block[1:]
    grad = jnp.sum(ordered[...].astype(f32), axis=0)
    second = core_ref[0] == 1
    own_grad_ref[...] = jnp.where(second, grad[1], grad[0])
    joined_ref[chips] = jnp.where(second, grad[0], grad[1]).astype(bf16)


def chip_blocks(chip, blocks_ref, source):
    size = source.shape[0]
    for step in range(source.shape[1] // size):
        source[:, block_at(chip ^ step, size)] = blocks_ref[step]
    return source[...]


def backward_own(chip_ref, core_ref, adjacency_ref, joined_ref, total_ref, source):
    blocks = chip_blocks(chip_ref[0], joined_ref, source)
    rows = rows_of(core_ref[0], adjacency_ref, source.shape[0])
    total_ref[...] = jnp.dot(blocks, rows, preferred_element_type=f32)


def backward_rows(
    row_ref, chip_ref, core_ref, adjacency_ref, own_ref, grad_ref, received_ref, *refs
):
    *pieces, source, total = refs
    chips, size = received_ref.shape[0] - 1, received_ref.shape[2]
    blocks = chip_blocks(chip_ref[0], received_ref, source)
    rows = rows_of(1 - core_ref[0], adjacency_ref, size)
    total[...] = own_ref[...] + jnp.dot(blocks, rows, preferred_element_type=f32)
    grad = (grad_ref[...] + received_ref[chips].astype(f32)).astype(bf16)
    for step, piece in zip((2, 1, 3, 0), pieces):
        owner = lax.rem(row_ref[0] + step, len(pieces))
        piece[0] = total[:, block_at(owner, size)].astype(bf16)
        piece[1] = grad


def sum_grad(factor, row_ref, *refs):
    *pieces, out_ref, ordered = refs
    for step, piece in zip((2, 3, 1, 0), pieces):
        ordered[lax.rem(row_ref[0] + step, len(pieces))] = piece[1]
    total = jnp.sum(ordered[...].astype(f32), axis=0) * factor
    out_ref[...] = total.astype(out_ref.dtype)


def input_rows(deg_ref, *refs):
    *pieces, out_ref = refs
    total = sum(piece[0].astype(f32) for piece in pieces)
    out_ref[...] = (total * deg_ref[...].astype(f32).reshape(1, -1)).T.astype(bf16)


def join_halves(core_ref, own_ref, other_ref, out_ref):
    size = own_ref.shape[1]
    half = core_ref[0]
    out_ref[:, block_at(half, size)] = own_ref[...].astype(f32)
    out_ref[:, block_at(1 - half, size)] = other_ref[...].astype(f32)


def forward_all(rows_ref, cols_ref, masks_ref, source_ref, partial_ref, total):
    forward_total(rows_ref, cols_ref, masks_ref, source_ref, total)
    partial_ref[...] = total[...].astype(bf16).reshape(partial_ref.shape)


def vertex_all(column_ref, deg_ref, weight_ref, cotangent_ref, received_ref, act_ref, back_ref, grad_ref):
    summed = jnp.sum(received_ref[...].astype(f32), axis=0)
    back_ref[...], grad_ref[...], active = vertex_values(
        summed, column_ref, deg_ref, weight_ref, cotangent_ref
    )
    act_ref[...] = active.astype(bf16)


def backward_all(rows_ref, cols_ref, masks_ref, gathered_ref, pieces_ref, source, total):
    size = gathered_ref.shape[2]
    for shard in range(gathered_ref.shape[0]):
        source[:, shard * size : (shard + 1) * size] = gathered_ref[shard]
    backward_total(rows_ref, cols_ref, masks_ref, source, total)
    for shard in range(pieces_ref.shape[0]):
        pieces_ref[shard] = total[:, shard * size : (shard + 1) * size].astype(bf16)


def input_all(deg_ref, pieces_ref, out_ref):
    total = jnp.sum(pieces_ref[...].astype(f32), axis=0)
    out_ref[...] = (total * deg_ref[...].astype(f32).reshape(1, -1)).T.astype(bf16)


def exchange(block, axis, shards, distance):
    return lax.ppermute(block, axis, [(shard, shard ^ distance) for shard in range(shards)])


def shifted(block, axis, shards, step):
    return lax.ppermute(block, axis, [(shard, (shard + step) % shards) for shard in range(shards)])


def on_device(features, deg_scale, weight, cotangent, tile_rows, tile_cols, tile_count, tile_bits):
    size, width = features.shape
    height, out_width = weight.shape
    row_shards = lax.axis_size("row")
    col_shards = lax.axis_size("col")
    chips = col_shards // 2
    slots, words, tile_size = tile_bits.shape[2:]
    factor = 1.0 / math.sqrt(row_shards * col_shards * size)
    row = lax.axis_index("row").astype(jnp.int32).reshape(1)
    col = lax.axis_index("col").astype(jnp.int32)
    chip, core = (col // 2).reshape(1), (col % 2).reshape(1)
    forward_scratch = [pltpu.VMEM((col_shards * size, width), f32)]
    backward_scratch = [
        pltpu.VMEM((width, col_shards * size), bf16),
        pltpu.VMEM((width, row_shards * size), f32),
    ]
    prepared = (struct((size, width), bf16), struct((size, width), f32))
    block = struct((width, size), bf16)
    activation = struct((size, out_width), bf16)
    input_shape = struct((size, width), bf16)

    covered = slots * tile_size * tile_size == row_shards * col_shards * size * size
    if row_shards != 4 or col_shards != 8 or not covered:
        scaled, column, masks = call(
            unpack_tiles,
            prepared + (struct((slots, tile_size, tile_size), bf16),),
            (tile_count,),
            (tile_bits, deg_scale, features),
        )
        gathered = lax.all_gather(scaled, "row", axis=0, tiled=True)
        partial_value = call(
            forward_all,
            struct((col_shards, size, width), bf16),
            (tile_rows, tile_cols),
            (masks, gathered),
            forward_scratch,
        )
        received = lax.all_to_all(partial_value, "col", 0, 0)
        activations, back, local_grad = call(
            vertex_all,
            (activation, block, struct((height, out_width), f32)),
            (),
            (column, deg_scale, weight, cotangent, received),
        )
        weight_grad = lax.psum(local_grad, ("row", "col")) * factor
        pieces = call(
            backward_all,
            struct((row_shards, width, size), bf16),
            (tile_rows, tile_cols),
            (masks, lax.all_gather(back, "col")),
            backward_scratch,
        )
        arrived = lax.all_to_all(pieces, "row", 0, 0)
        input_grad = call(input_all, input_shape, (), (deg_scale, arrived))
        return (activations, input_grad, weight_grad)

    column = call(
        scale_column, struct((size, width), f32), (), (deg_scale,), flops=FIRST_FLOPS
    )
    scaled = call(scale_rows, struct((size, width), bf16), (), (column, features, tile_rows, tile_cols))
    adjacency = pl.pallas_call(
        build_adjacency,
        out_shape=struct((col_shards * size, row_shards * size), bf16),
        in_specs=[SMEM, SMEM, SMEM, VMEM, ANY],
        out_specs=VMEM,
        compiler_params=LIMIT,
        cost_estimate=pl.CostEstimate(flops=1 << 20, bytes_accessed=1 << 20, transcendentals=0),
    )(tile_count, tile_rows, tile_cols, tile_bits, scaled)
    far_first = (3, 2, 1)
    blocks = [exchange(scaled, "row", row_shards, step) for step in (1, 3, 2)]
    blocks.insert(0, scaled)
    source, other = call(
        forward_other,
        (struct((row_shards * size, width), bf16), struct((chips, size, width), bf16)),
        (row, core),
        (adjacency, *blocks),
    )
    mine = call(
        forward_mine, struct((chips, size, width), f32), (core,), (adjacency, source)
    )
    own, *pieces = call(
        forward_chips,
        (struct((size, width), f32),) + (struct((size, width), bf16),) * len(far_first),
        (chip,),
        (mine, exchange(other, "col", col_shards, 1)),
    )
    received = [
        exchange(piece, "col", col_shards, 2 * step) for step, piece in zip(far_first, pieces)
    ]
    sent, active = call(
        vertex_chips,
        (struct((3, width, size), bf16), struct((size, out_width), f32)),
        (),
        (column, deg_scale, weight, cotangent, own, *received),
    )
    activations, written = call(write_out, (activation, struct((8, 128), f32)), (), (active,))
    received = [exchange(sent, "col", col_shards, 2 * step) for step in (1, 2, 3)]
    joined, own_grad = call(
        join_chips,
        (struct((chips + 1, width, size), bf16), struct((width, size), f32)),
        (chip, core),
        (sent, *received),
        [pltpu.VMEM((chips, 2, width, size), bf16)],
        after=(written,),
    )
    half_source = pltpu.VMEM((width, chips * size), bf16)
    own_total = call(
        backward_own,
        struct((width, row_shards * size), f32),
        (chip, core),
        (adjacency, joined),
        [half_source],
    )
    pieces = call(
        backward_rows,
        (struct((2, width, size), bf16),) * row_shards,
        (row, chip, core),
        (adjacency, own_total, own_grad, exchange(joined, "col", col_shards, 1)),
        [half_source, pltpu.VMEM((width, row_shards * size), f32)],
    )
    arrived = [shifted(piece, "row", row_shards, step) for step, piece in zip((2, 1, 3), pieces)]
    arrived.append(pieces[-1])
    half_grad = call(
        functools.partial(sum_grad, factor),
        struct((height, out_width // 2), f32),
        (row,),
        arrived,
        [pltpu.VMEM((row_shards, height, out_width // 2), bf16)],
    )
    other_grad = exchange(half_grad, "col", col_shards, 1)
    input_grad = call(input_rows, input_shape, (), (deg_scale, *arrived))
    weight_grad = call(
        join_halves, struct((height, out_width), f32), (core,), (half_grad, other_grad)
    )
    return (activations, input_grad, weight_grad)


def solution(mesh):
    in_specs = (
        P(("row", "col"), None),
        P(("row", "col")),
        P(),
        P(("row", "col"), None),
        P("row", "col", None),
        P("row", "col", None),
        P("row", "col"),
        P("row", "col", None, None, None),
    )
    out_specs = (P(("row", "col"), None), P(("row", "col"), None), P())
    return jax.shard_map(
        on_device, mesh=mesh, in_specs=in_specs, out_specs=out_specs, check_vma=False
    )
```

```python
import functools
import math

import jax
import jax.numpy as jnp
from jax import lax
from jax.experimental import pallas as pl
from jax.experimental.pallas import tpu as pltpu
from jax.sharding import PartitionSpec as P

VMEM = pl.BlockSpec(memory_space=pltpu.VMEM)
SMEM = pl.BlockSpec(memory_space=pltpu.SMEM)
ANY = pl.BlockSpec(memory_space=pl.ANY)
LIMIT = pltpu.CompilerParams(vmem_limit_bytes=40 * 1024 * 1024)
FIRST_FLOPS = 1 << 32
bf16, f32 = jnp.bfloat16, jnp.float32


def struct(shape, dtype):
    return jax.ShapeDtypeStruct(shape, dtype)


def call(body, out_shape, scalars, operands, scratch=(), flops=1 << 20, after=()):
    single = not isinstance(out_shape, (tuple, list))
    return pl.pallas_call(
        body,
        out_shape=out_shape,
        in_specs=[SMEM] * len(scalars) + [VMEM] * len(operands) + [ANY] * len(after),
        out_specs=VMEM if single else [VMEM] * len(out_shape),
        scratch_shapes=list(scratch),
        compiler_params=LIMIT,
        cost_estimate=pl.CostEstimate(flops=flops, bytes_accessed=1 << 20, transcendentals=0),
    )(*scalars, *operands, *after)


def block_at(index, size):
    return pl.ds(pl.multiple_of(index * size, size), size)


def unpack_tiles(count_ref, bits_ref, deg_ref, features_ref, scaled_ref, column_ref, masks_ref):
    column = spread_scale(deg_ref[...], column_ref.shape[0])
    column_ref[...] = column
    scaled_ref[...] = (features_ref[...].astype(f32) * column).astype(bf16)

    def one(slot):
        masks_ref[slot] = unpacked(jnp.where(slot < count_ref[0, 0], bits_ref[0, 0, slot], 0))

    pl.loop(0, masks_ref.shape[0])(one)


def forward_total(rows_ref, cols_ref, masks_ref, source, total):
    slots, tile_size = masks_ref.shape[:2]
    total[...] = jnp.zeros_like(total)

    def one(slot):
        place = block_at(rows_ref[0, 0, slot], tile_size)
        pick = block_at(cols_ref[0, 0, slot], tile_size)
        total[place, :] += jnp.dot(masks_ref[slot], source[pick, :], preferred_element_type=f32)

    pl.loop(0, slots)(one)


def backward_total(rows_ref, cols_ref, masks_ref, source, total):
    slots, tile_size = masks_ref.shape[:2]
    total[...] = jnp.zeros_like(total)

    def one(slot):
        pick = block_at(rows_ref[0, 0, slot], tile_size)
        place = block_at(cols_ref[0, 0, slot], tile_size)
        total[:, place] += jnp.dot(source[:, pick], masks_ref[slot], preferred_element_type=f32)

    pl.loop(0, slots)(one)


def unpacked(packed):
    words, tile_size = packed.shape
    repeated = jnp.broadcast_to(packed[:, None, :], (words, 8, tile_size))
    shifts = lax.broadcasted_iota(jnp.int32, (words, 8, tile_size), 1)
    bit_values = jnp.bitwise_and(jnp.right_shift(repeated, shifts), 1)
    return bit_values.reshape(words * 8, tile_size).astype(f32).astype(bf16)


def spread_scale(deg, size):
    rows = lax.broadcasted_iota(jnp.int32, (size, size), 0)
    columns = lax.broadcasted_iota(jnp.int32, (size, size), 1)
    diagonal = jnp.where(rows == columns, deg.astype(f32).reshape(1, size), 0.0).astype(bf16)
    return jnp.dot(diagonal, jnp.ones((size, size), bf16), preferred_element_type=f32)


def scale_column(deg_ref, column_ref):
    column_ref[...] = spread_scale(deg_ref[...], column_ref.shape[0])


def scale_rows(column_ref, features_ref, rows_ref, cols_ref, scaled_ref):
    scaled_ref[...] = (features_ref[...].astype(f32) * column_ref[...]).astype(bf16)


def build_adjacency(count_ref, rows_ref, cols_ref, bits_ref, after_ref, adjacency_ref):
    slots, words, tile_size = bits_ref.shape[2:]
    count = count_ref[0, 0]
    for slot in range(slots):
        packed = jnp.where(slot < count, bits_ref[0, 0, slot], 0)
        place = block_at(rows_ref[0, 0, slot], tile_size), block_at(cols_ref[0, 0, slot], tile_size)
        adjacency_ref[place] = unpacked(packed)


def rows_of(core, adjacency_ref, size):
    blocks = [
        adjacency_ref[block_at(2 * chip + core, size), :]
        for chip in range(adjacency_ref.shape[0] // (2 * size))
    ]
    return jnp.concatenate(blocks, axis=0)


def forward_other(row_ref, core_ref, adjacency_ref, *refs):
    *blocks, source_ref, other_ref = refs
    size = blocks[0].shape[0]
    for step, block in zip((0, 1, 3, 2), blocks):
        source_ref[block_at(row_ref[0] ^ step, size), :] = block[...]
    rows = rows_of(1 - core_ref[0], adjacency_ref, size)
    total = jnp.dot(rows, source_ref[...], preferred_element_type=f32)
    other_ref[...] = total.astype(bf16).reshape(other_ref.shape)


def forward_mine(core_ref, adjacency_ref, source_ref, mine_ref):
    rows = rows_of(core_ref[0], adjacency_ref, mine_ref.shape[1])
    total = jnp.dot(rows, source_ref[...], preferred_element_type=f32)
    mine_ref[...] = total.reshape(mine_ref.shape)


def forward_chips(chip_ref, mine_ref, received_ref, own_ref, *pieces):
    chip = chip_ref[0]
    own_ref[...] = mine_ref[chip] + received_ref[chip].astype(f32)
    for step, piece in zip((3, 2, 1), pieces):
        peer = chip ^ step
        piece[...] = (mine_ref[peer] + received_ref[peer].astype(f32)).astype(bf16)


def vertex_values(summed, column_ref, deg_ref, weight_ref, cotangent_ref):
    hidden = (summed * column_ref[...]).astype(bf16)
    weight = weight_ref[...]
    pre_act = jnp.dot(hidden, weight, preferred_element_type=f32)
    sigmoid_value = 1.0 / (1.0 + jnp.exp(-pre_act))
    slope = sigmoid_value * (1.0 + pre_act * (1.0 - sigmoid_value))
    slope_term = (cotangent_ref[...].astype(f32) * slope).astype(bf16)
    spread = lax.dot_general(
        weight, slope_term, (((1,), (1,)), ((), ())), preferred_element_type=f32
    )
    back = (spread * deg_ref[...].astype(f32).reshape(1, -1)).astype(bf16)
    local_grad = lax.dot_general(
        hidden, slope_term, (((0,), (0,)), ((), ())), preferred_element_type=f32
    )
    return back, local_grad, pre_act * sigmoid_value


def vertex_chips(column_ref, deg_ref, weight_ref, cotangent_ref, own_ref, *refs):
    *received, sent_ref, active_ref = refs
    summed = own_ref[...] + sum(piece[...].astype(f32) for piece in received)
    sent_ref[0], local_grad, active_ref[...] = vertex_values(
        summed, column_ref, deg_ref, weight_ref, cotangent_ref
    )
    half = sent_ref.shape[2]
    for core in range(2):
        sent_ref[1 + core] = local_grad[:, core * half : (core + 1) * half].astype(bf16)


def write_out(active_ref, out_ref, written_ref):
    out_ref[...] = active_ref[...].astype(bf16)
    written_ref[...] = jnp.zeros_like(written_ref)


def join_chips(chip_ref, core_ref, *refs):
    *blocks, _, joined_ref, own_grad_ref, ordered = refs
    chips = len(blocks)
    for step, block in enumerate(blocks):
        joined_ref[step] = block[0]
        ordered[chip_ref[0] ^ step] = block[1:]
    grad = jnp.sum(ordered[...].astype(f32), axis=0)
    second = core_ref[0] == 1
    own_grad_ref[...] = jnp.where(second, grad[1], grad[0])
    joined_ref[chips] = jnp.where(second, grad[0], grad[1]).astype(bf16)


def chip_blocks(chip, blocks_ref, source):
    size = source.shape[0]
    for step in range(source.shape[1] // size):
        source[:, block_at(chip ^ step, size)] = blocks_ref[step]
    return source[...]


def backward_own(chip_ref, core_ref, adjacency_ref, joined_ref, total_ref, source):
    blocks = chip_blocks(chip_ref[0], joined_ref, source)
    rows = rows_of(core_ref[0], adjacency_ref, source.shape[0])
    total_ref[...] = jnp.dot(blocks, rows, preferred_element_type=f32)


def backward_rows(
    row_ref, chip_ref, core_ref, adjacency_ref, own_ref, grad_ref, received_ref, *refs
):
    *pieces, source, total = refs
    chips, size = received_ref.shape[0] - 1, received_ref.shape[2]
    blocks = chip_blocks(chip_ref[0], received_ref, source)
    rows = rows_of(1 - core_ref[0], adjacency_ref, size)
    total[...] = own_ref[...] + jnp.dot(blocks, rows, preferred_element_type=f32)
    grad = (grad_ref[...] + received_ref[chips].astype(f32)).astype(bf16)
    for step, piece in zip((1, 2, 3, 0), pieces):
        owner = lax.rem(row_ref[0] + step, len(pieces))
        piece[0] = total[:, block_at(owner, size)].astype(bf16)
        piece[1] = grad


def pack_pieces(*refs):
    *pieces, own_ref, sent_ref = refs
    count = len(pieces)
    for index, piece in enumerate(pieces):
        sent_ref[index] = piece[0]
        sent_ref[count + index] = piece[1]
    sent_ref[2 * count] = own_ref[1]


def finish(factor, row_ref, core_ref, deg_ref, own_ref, received_ref, *refs):
    *pieces, input_ref, grad_ref, ordered = refs
    count, size = len(pieces), own_ref.shape[1]
    total = sum(received_ref[index].astype(f32) for index in range(count)) + own_ref[0].astype(f32)
    input_ref[...] = (total * deg_ref[...].astype(f32).reshape(1, -1)).T.astype(bf16)
    for index, piece in enumerate(pieces):
        plane = lax.rem(row_ref[0] + count - index, count + 1)
        ordered[0, plane] = received_ref[count + index]
        ordered[1, plane] = piece[1]
    ordered[0, row_ref[0]] = own_ref[1]
    ordered[1, row_ref[0]] = received_ref[2 * count]
    for index, half in enumerate((core_ref[0], 1 - core_ref[0])):
        half_grad = jnp.sum(ordered[index].astype(f32), axis=0) * factor
        grad_ref[:, block_at(half, size)] = half_grad


def forward_all(rows_ref, cols_ref, masks_ref, source_ref, partial_ref, total):
    forward_total(rows_ref, cols_ref, masks_ref, source_ref, total)
    partial_ref[...] = total[...].astype(bf16).reshape(partial_ref.shape)


def vertex_all(column_ref, deg_ref, weight_ref, cotangent_ref, received_ref, act_ref, back_ref, grad_ref):
    summed = jnp.sum(received_ref[...].astype(f32), axis=0)
    back_ref[...], grad_ref[...], active = vertex_values(
        summed, column_ref, deg_ref, weight_ref, cotangent_ref
    )
    act_ref[...] = active.astype(bf16)


def backward_all(rows_ref, cols_ref, masks_ref, gathered_ref, pieces_ref, source, total):
    size = gathered_ref.shape[2]
    for shard in range(gathered_ref.shape[0]):
        source[:, shard * size : (shard + 1) * size] = gathered_ref[shard]
    backward_total(rows_ref, cols_ref, masks_ref, source, total)
    for shard in range(pieces_ref.shape[0]):
        pieces_ref[shard] = total[:, shard * size : (shard + 1) * size].astype(bf16)


def input_all(deg_ref, pieces_ref, out_ref):
    total = jnp.sum(pieces_ref[...].astype(f32), axis=0)
    out_ref[...] = (total * deg_ref[...].astype(f32).reshape(1, -1)).T.astype(bf16)


def exchange(block, axis, shards, distance):
    return lax.ppermute(block, axis, [(shard, shard ^ distance) for shard in range(shards)])


def crossed(block, rows, cols, step):
    pairs = [
        (row * cols + col, (row + step) % rows * cols + (col ^ 1))
        for row in range(rows)
        for col in range(cols)
    ]
    return lax.ppermute(block, ("row", "col"), pairs)


def on_device(features, deg_scale, weight, cotangent, tile_rows, tile_cols, tile_count, tile_bits):
    size, width = features.shape
    height, out_width = weight.shape
    row_shards = lax.axis_size("row")
    col_shards = lax.axis_size("col")
    chips = col_shards // 2
    slots, words, tile_size = tile_bits.shape[2:]
    factor = 1.0 / math.sqrt(row_shards * col_shards * size)
    row = lax.axis_index("row").astype(jnp.int32).reshape(1)
    col = lax.axis_index("col").astype(jnp.int32)
    chip, core = (col // 2).reshape(1), (col % 2).reshape(1)
    forward_scratch = [pltpu.VMEM((col_shards * size, width), f32)]
    backward_scratch = [
        pltpu.VMEM((width, col_shards * size), bf16),
        pltpu.VMEM((width, row_shards * size), f32),
    ]
    prepared = (struct((size, width), bf16), struct((size, width), f32))
    block = struct((width, size), bf16)
    activation = struct((size, out_width), bf16)
    input_shape = struct((size, width), bf16)

    covered = slots * tile_size * tile_size == row_shards * col_shards * size * size
    if row_shards != 4 or col_shards != 8 or not covered:
        scaled, column, masks = call(
            unpack_tiles,
            prepared + (struct((slots, tile_size, tile_size), bf16),),
            (tile_count,),
            (tile_bits, deg_scale, features),
        )
        gathered = lax.all_gather(scaled, "row", axis=0, tiled=True)
        partial_value = call(
            forward_all,
            struct((col_shards, size, width), bf16),
            (tile_rows, tile_cols),
            (masks, gathered),
            forward_scratch,
        )
        received = lax.all_to_all(partial_value, "col", 0, 0)
        activations, back, local_grad = call(
            vertex_all,
            (activation, block, struct((height, out_width), f32)),
            (),
            (column, deg_scale, weight, cotangent, received),
        )
        weight_grad = lax.psum(local_grad, ("row", "col")) * factor
        pieces = call(
            backward_all,
            struct((row_shards, width, size), bf16),
            (tile_rows, tile_cols),
            (masks, lax.all_gather(back, "col")),
            backward_scratch,
        )
        arrived = lax.all_to_all(pieces, "row", 0, 0)
        input_grad = call(input_all, input_shape, (), (deg_scale, arrived))
        return (activations, input_grad, weight_grad)

    column = call(
        scale_column, struct((size, width), f32), (), (deg_scale,), flops=FIRST_FLOPS
    )
    scaled = call(scale_rows, struct((size, width), bf16), (), (column, features, tile_rows, tile_cols))
    adjacency = pl.pallas_call(
        build_adjacency,
        out_shape=struct((col_shards * size, row_shards * size), bf16),
        in_specs=[SMEM, SMEM, SMEM, VMEM, ANY],
        out_specs=VMEM,
        compiler_params=LIMIT,
        cost_estimate=pl.CostEstimate(flops=1 << 20, bytes_accessed=1 << 20, transcendentals=0),
    )(tile_count, tile_rows, tile_cols, tile_bits, scaled)
    far_first = (3, 2, 1)
    blocks = [exchange(scaled, "row", row_shards, step) for step in (1, 3, 2)]
    blocks.insert(0, scaled)
    source, other = call(
        forward_other,
        (struct((row_shards * size, width), bf16), struct((chips, size, width), bf16)),
        (row, core),
        (adjacency, *blocks),
    )
    mine = call(
        forward_mine, struct((chips, size, width), f32), (core,), (adjacency, source)
    )
    own, *pieces = call(
        forward_chips,
        (struct((size, width), f32),) + (struct((size, width), bf16),) * len(far_first),
        (chip,),
        (mine, exchange(other, "col", col_shards, 1)),
    )
    received = [
        exchange(piece, "col", col_shards, 2 * step) for step, piece in zip(far_first, pieces)
    ]
    sent, active = call(
        vertex_chips,
        (struct((3, width, size), bf16), struct((size, out_width), f32)),
        (),
        (column, deg_scale, weight, cotangent, own, *received),
    )
    activations, written = call(write_out, (activation, struct((8, 128), f32)), (), (active,))
    received = [exchange(sent, "col", col_shards, 2 * step) for step in (1, 2, 3)]
    joined, own_grad = call(
        join_chips,
        (struct((chips + 1, width, size), bf16), struct((width, size), f32)),
        (chip, core),
        (sent, *received),
        [pltpu.VMEM((chips, 2, width, size), bf16)],
        after=(written,),
    )
    half_source = pltpu.VMEM((width, chips * size), bf16)
    own_total = call(
        backward_own,
        struct((width, row_shards * size), f32),
        (chip, core),
        (adjacency, joined),
        [half_source],
    )
    pieces = call(
        backward_rows,
        (struct((2, width, size), bf16),) * row_shards,
        (row, chip, core),
        (adjacency, own_total, own_grad, exchange(joined, "col", col_shards, 1)),
        [half_source, pltpu.VMEM((width, row_shards * size), f32)],
    )
    own_piece = pieces[-1]
    arrived = [
        crossed(piece, row_shards, col_shards, step) for step, piece in zip((1, 2, 3), pieces)
    ]
    packed = call(
        pack_pieces,
        struct((2 * len(arrived) + 1, width, size), bf16),
        (),
        (*arrived, own_piece),
    )
    input_grad, weight_grad = call(
        functools.partial(finish, factor),
        (input_shape, struct((height, out_width), f32)),
        (row, core),
        (deg_scale, own_piece, exchange(packed, "col", col_shards, 1), *arrived),
        [pltpu.VMEM((2, row_shards, height, out_width // 2), bf16)],
    )
    return (activations, input_grad, weight_grad)


def solution(mesh):
    in_specs = (
        P(("row", "col"), None),
        P(("row", "col")),
        P(),
        P(("row", "col"), None),
        P("row", "col", None),
        P("row", "col", None),
        P("row", "col"),
        P("row", "col", None, None, None),
    )
    out_specs = (P(("row", "col"), None), P(("row", "col"), None), P())
    return jax.shard_map(
        on_device, mesh=mesh, in_specs=in_specs, out_specs=out_specs, check_vma=False
    )
```

```python
import functools
import math

import jax
import jax.numpy as jnp
from jax import lax
from jax.experimental import pallas as pl
from jax.experimental.pallas import tpu as pltpu
from jax.sharding import PartitionSpec as P

VMEM = pl.BlockSpec(memory_space=pltpu.VMEM)
SMEM = pl.BlockSpec(memory_space=pltpu.SMEM)
ANY = pl.BlockSpec(memory_space=pl.ANY)
LIMIT = pltpu.CompilerParams(vmem_limit_bytes=40 * 1024 * 1024)
FIRST_FLOPS = 1 << 32
bf16, f32 = jnp.bfloat16, jnp.float32


def struct(shape, dtype):
    return jax.ShapeDtypeStruct(shape, dtype)


def call(body, out_shape, scalars, operands, scratch=(), flops=1 << 20, after=()):
    single = not isinstance(out_shape, (tuple, list))
    return pl.pallas_call(
        body,
        out_shape=out_shape,
        in_specs=[SMEM] * len(scalars) + [VMEM] * len(operands) + [ANY] * len(after),
        out_specs=VMEM if single else [VMEM] * len(out_shape),
        scratch_shapes=list(scratch),
        compiler_params=LIMIT,
        cost_estimate=pl.CostEstimate(flops=flops, bytes_accessed=1 << 20, transcendentals=0),
    )(*scalars, *operands, *after)


def block_at(index, size):
    return pl.ds(pl.multiple_of(index * size, size), size)


def unpack_tiles(count_ref, bits_ref, deg_ref, features_ref, scaled_ref, column_ref, masks_ref):
    column = spread_scale(deg_ref[...], column_ref.shape[0])
    column_ref[...] = column
    scaled_ref[...] = (features_ref[...].astype(f32) * column).astype(bf16)

    def one(slot):
        masks_ref[slot] = unpacked(jnp.where(slot < count_ref[0, 0], bits_ref[0, 0, slot], 0))

    pl.loop(0, masks_ref.shape[0])(one)


def forward_total(rows_ref, cols_ref, masks_ref, source, total):
    slots, tile_size = masks_ref.shape[:2]
    total[...] = jnp.zeros_like(total)

    def one(slot):
        place = block_at(rows_ref[0, 0, slot], tile_size)
        pick = block_at(cols_ref[0, 0, slot], tile_size)
        total[place, :] += jnp.dot(masks_ref[slot], source[pick, :], preferred_element_type=f32)

    pl.loop(0, slots)(one)


def backward_total(rows_ref, cols_ref, masks_ref, source, total):
    slots, tile_size = masks_ref.shape[:2]
    total[...] = jnp.zeros_like(total)

    def one(slot):
        pick = block_at(rows_ref[0, 0, slot], tile_size)
        place = block_at(cols_ref[0, 0, slot], tile_size)
        total[:, place] += jnp.dot(source[:, pick], masks_ref[slot], preferred_element_type=f32)

    pl.loop(0, slots)(one)


def unpacked(packed):
    words, tile_size = packed.shape
    repeated = jnp.broadcast_to(packed[:, None, :], (words, 8, tile_size))
    shifts = lax.broadcasted_iota(jnp.int32, (words, 8, tile_size), 1)
    bit_values = jnp.bitwise_and(jnp.right_shift(repeated, shifts), 1)
    return bit_values.reshape(words * 8, tile_size).astype(f32).astype(bf16)


def spread_scale(deg, size):
    rows = lax.broadcasted_iota(jnp.int32, (size, size), 0)
    columns = lax.broadcasted_iota(jnp.int32, (size, size), 1)
    diagonal = jnp.where(rows == columns, deg.astype(f32).reshape(1, size), 0.0).astype(bf16)
    return jnp.dot(diagonal, jnp.ones((size, size), bf16), preferred_element_type=f32)


def scale_column(deg_ref, column_ref):
    column_ref[...] = spread_scale(deg_ref[...], column_ref.shape[0])


def scale_rows(column_ref, features_ref, rows_ref, cols_ref, scaled_ref):
    scaled_ref[...] = (features_ref[...].astype(f32) * column_ref[...]).astype(bf16)


def build_adjacency(count_ref, rows_ref, cols_ref, bits_ref, after_ref, adjacency_ref):
    slots, words, tile_size = bits_ref.shape[2:]
    count = count_ref[0, 0]
    for slot in range(slots):
        packed = jnp.where(slot < count, bits_ref[0, 0, slot], 0)
        place = block_at(rows_ref[0, 0, slot], tile_size), block_at(cols_ref[0, 0, slot], tile_size)
        adjacency_ref[place] = unpacked(packed)


def rows_of(core, adjacency_ref, size):
    blocks = [
        adjacency_ref[block_at(2 * chip + core, size), :]
        for chip in range(adjacency_ref.shape[0] // (2 * size))
    ]
    return jnp.concatenate(blocks, axis=0)


def forward_other(row_ref, core_ref, adjacency_ref, *refs):
    *blocks, source_ref, other_ref = refs
    size = blocks[0].shape[0]
    for step, block in zip((0, 1, 3, 2), blocks):
        source_ref[block_at(row_ref[0] ^ step, size), :] = block[...]
    rows = rows_of(1 - core_ref[0], adjacency_ref, size)
    total = jnp.dot(rows, source_ref[...], preferred_element_type=f32)
    other_ref[...] = total.astype(bf16).reshape(other_ref.shape)


def forward_mine(core_ref, adjacency_ref, source_ref, mine_ref):
    rows = rows_of(core_ref[0], adjacency_ref, mine_ref.shape[1])
    total = jnp.dot(rows, source_ref[...], preferred_element_type=f32)
    mine_ref[...] = total.reshape(mine_ref.shape)


def forward_chips(chip_ref, mine_ref, received_ref, own_ref, *pieces):
    chip = chip_ref[0]
    own_ref[...] = mine_ref[chip] + received_ref[chip].astype(f32)
    for step, piece in zip((3, 2, 1), pieces):
        peer = chip ^ step
        piece[...] = (mine_ref[peer] + received_ref[peer].astype(f32)).astype(bf16)


def vertex_values(summed, column_ref, deg_ref, weight_ref, cotangent_ref):
    hidden = (summed * column_ref[...]).astype(bf16)
    weight = weight_ref[...]
    pre_act = jnp.dot(hidden, weight, preferred_element_type=f32)
    sigmoid_value = 1.0 / (1.0 + jnp.exp(-pre_act))
    slope = sigmoid_value * (1.0 + pre_act * (1.0 - sigmoid_value))
    slope_term = (cotangent_ref[...].astype(f32) * slope).astype(bf16)
    spread = lax.dot_general(
        weight, slope_term, (((1,), (1,)), ((), ())), preferred_element_type=f32
    )
    back = (spread * deg_ref[...].astype(f32).reshape(1, -1)).astype(bf16)
    local_grad = lax.dot_general(
        hidden, slope_term, (((0,), (0,)), ((), ())), preferred_element_type=f32
    )
    return back, local_grad, pre_act * sigmoid_value


def vertex_chips(column_ref, deg_ref, weight_ref, cotangent_ref, own_ref, *refs):
    *received, sent_ref, active_ref = refs
    summed = own_ref[...] + sum(piece[...].astype(f32) for piece in received)
    sent_ref[0], local_grad, active_ref[...] = vertex_values(
        summed, column_ref, deg_ref, weight_ref, cotangent_ref
    )
    half = sent_ref.shape[2]
    for core in range(2):
        sent_ref[1 + core] = local_grad[:, core * half : (core + 1) * half].astype(bf16)


def write_out(active_ref, out_ref, written_ref):
    out_ref[...] = active_ref[...].astype(bf16)
    written_ref[...] = jnp.zeros_like(written_ref)


def join_chips(chip_ref, core_ref, *refs):
    *blocks, _, joined_ref, own_grad_ref, ordered = refs
    chips = len(blocks)
    for step, block in enumerate(blocks):
        joined_ref[step] = block[0]
        ordered[chip_ref[0] ^ step] = block[1:]
    grad = jnp.sum(ordered[...].astype(f32), axis=0)
    second = core_ref[0] == 1
    own_grad_ref[...] = jnp.where(second, grad[1], grad[0])
    joined_ref[chips] = jnp.where(second, grad[0], grad[1]).astype(bf16)


def chip_blocks(chip, blocks_ref, source):
    size = source.shape[0]
    for step in range(source.shape[1] // size):
        source[:, block_at(chip ^ step, size)] = blocks_ref[step]
    return source[...]


def backward_own(chip_ref, core_ref, adjacency_ref, joined_ref, total_ref, source):
    blocks = chip_blocks(chip_ref[0], joined_ref, source)
    rows = rows_of(core_ref[0], adjacency_ref, source.shape[0])
    total_ref[...] = jnp.dot(blocks, rows, preferred_element_type=f32)


def backward_rows(
    row_ref, chip_ref, core_ref, adjacency_ref, own_ref, grad_ref, received_ref, *refs
):
    *pieces, source, total = refs
    chips, size = received_ref.shape[0] - 1, received_ref.shape[2]
    blocks = chip_blocks(chip_ref[0], received_ref, source)
    rows = rows_of(1 - core_ref[0], adjacency_ref, size)
    total[...] = own_ref[...] + jnp.dot(blocks, rows, preferred_element_type=f32)
    grad = (grad_ref[...] + received_ref[chips].astype(f32)).astype(bf16)
    for step, piece in zip((2, 1, 3, 0), pieces):
        owner = lax.rem(row_ref[0] + step, len(pieces))
        piece[0] = total[:, block_at(owner, size)].astype(bf16)
        piece[1] = grad


def pack_pieces(*refs):
    *pieces, own_ref, sent_ref = refs
    count = len(pieces)
    for index, piece in enumerate(pieces):
        sent_ref[index] = piece[0]
        sent_ref[count + index] = piece[1]
    sent_ref[2 * count] = own_ref[1]


def finish(factor, row_ref, core_ref, deg_ref, own_ref, received_ref, *refs):
    *pieces, input_ref, grad_ref, ordered = refs
    count, size = len(pieces), own_ref.shape[1]
    total = sum(received_ref[index].astype(f32) for index in range(count)) + own_ref[0].astype(f32)
    input_ref[...] = (total * deg_ref[...].astype(f32).reshape(1, -1)).T.astype(bf16)
    for index, (step, piece) in enumerate(zip((2, 1, 3), pieces)):
        plane = lax.rem(row_ref[0] + count + 1 - step, count + 1)
        ordered[0, plane] = received_ref[count + index]
        ordered[1, plane] = piece[1]
    ordered[0, row_ref[0]] = own_ref[1]
    ordered[1, row_ref[0]] = received_ref[2 * count]
    for index, half in enumerate((core_ref[0], 1 - core_ref[0])):
        half_grad = jnp.sum(ordered[index].astype(f32), axis=0) * factor
        grad_ref[:, block_at(half, size)] = half_grad


def forward_all(rows_ref, cols_ref, masks_ref, source_ref, partial_ref, total):
    forward_total(rows_ref, cols_ref, masks_ref, source_ref, total)
    partial_ref[...] = total[...].astype(bf16).reshape(partial_ref.shape)


def vertex_all(column_ref, deg_ref, weight_ref, cotangent_ref, received_ref, act_ref, back_ref, grad_ref):
    summed = jnp.sum(received_ref[...].astype(f32), axis=0)
    back_ref[...], grad_ref[...], active = vertex_values(
        summed, column_ref, deg_ref, weight_ref, cotangent_ref
    )
    act_ref[...] = active.astype(bf16)


def backward_all(rows_ref, cols_ref, masks_ref, gathered_ref, pieces_ref, source, total):
    size = gathered_ref.shape[2]
    for shard in range(gathered_ref.shape[0]):
        source[:, shard * size : (shard + 1) * size] = gathered_ref[shard]
    backward_total(rows_ref, cols_ref, masks_ref, source, total)
    for shard in range(pieces_ref.shape[0]):
        pieces_ref[shard] = total[:, shard * size : (shard + 1) * size].astype(bf16)


def input_all(deg_ref, pieces_ref, out_ref):
    total = jnp.sum(pieces_ref[...].astype(f32), axis=0)
    out_ref[...] = (total * deg_ref[...].astype(f32).reshape(1, -1)).T.astype(bf16)


def exchange(block, axis, shards, distance):
    return lax.ppermute(block, axis, [(shard, shard ^ distance) for shard in range(shards)])


def crossed(block, rows, cols, step):
    pairs = [
        (row * cols + col, (row + step) % rows * cols + (col ^ 1))
        for row in range(rows)
        for col in range(cols)
    ]
    return lax.ppermute(block, ("row", "col"), pairs)


def on_device(features, deg_scale, weight, cotangent, tile_rows, tile_cols, tile_count, tile_bits):
    size, width = features.shape
    height, out_width = weight.shape
    row_shards = lax.axis_size("row")
    col_shards = lax.axis_size("col")
    chips = col_shards // 2
    slots, words, tile_size = tile_bits.shape[2:]
    factor = 1.0 / math.sqrt(row_shards * col_shards * size)
    row = lax.axis_index("row").astype(jnp.int32).reshape(1)
    col = lax.axis_index("col").astype(jnp.int32)
    chip, core = (col // 2).reshape(1), (col % 2).reshape(1)
    forward_scratch = [pltpu.VMEM((col_shards * size, width), f32)]
    backward_scratch = [
        pltpu.VMEM((width, col_shards * size), bf16),
        pltpu.VMEM((width, row_shards * size), f32),
    ]
    prepared = (struct((size, width), bf16), struct((size, width), f32))
    block = struct((width, size), bf16)
    activation = struct((size, out_width), bf16)
    input_shape = struct((size, width), bf16)

    covered = slots * tile_size * tile_size == row_shards * col_shards * size * size
    if row_shards != 4 or col_shards != 8 or not covered:
        scaled, column, masks = call(
            unpack_tiles,
            prepared + (struct((slots, tile_size, tile_size), bf16),),
            (tile_count,),
            (tile_bits, deg_scale, features),
        )
        gathered = lax.all_gather(scaled, "row", axis=0, tiled=True)
        partial_value = call(
            forward_all,
            struct((col_shards, size, width), bf16),
            (tile_rows, tile_cols),
            (masks, gathered),
            forward_scratch,
        )
        received = lax.all_to_all(partial_value, "col", 0, 0)
        activations, back, local_grad = call(
            vertex_all,
            (activation, block, struct((height, out_width), f32)),
            (),
            (column, deg_scale, weight, cotangent, received),
        )
        weight_grad = lax.psum(local_grad, ("row", "col")) * factor
        pieces = call(
            backward_all,
            struct((row_shards, width, size), bf16),
            (tile_rows, tile_cols),
            (masks, lax.all_gather(back, "col")),
            backward_scratch,
        )
        arrived = lax.all_to_all(pieces, "row", 0, 0)
        input_grad = call(input_all, input_shape, (), (deg_scale, arrived))
        return (activations, input_grad, weight_grad)

    column = call(
        scale_column, struct((size, width), f32), (), (deg_scale,), flops=FIRST_FLOPS
    )
    scaled = call(scale_rows, struct((size, width), bf16), (), (column, features, tile_rows, tile_cols))
    adjacency = pl.pallas_call(
        build_adjacency,
        out_shape=struct((col_shards * size, row_shards * size), bf16),
        in_specs=[SMEM, SMEM, SMEM, VMEM, ANY],
        out_specs=VMEM,
        compiler_params=LIMIT,
        cost_estimate=pl.CostEstimate(flops=1 << 20, bytes_accessed=1 << 20, transcendentals=0),
    )(tile_count, tile_rows, tile_cols, tile_bits, scaled)
    far_first = (3, 2, 1)
    blocks = [exchange(scaled, "row", row_shards, step) for step in (1, 3, 2)]
    blocks.insert(0, scaled)
    source, other = call(
        forward_other,
        (struct((row_shards * size, width), bf16), struct((chips, size, width), bf16)),
        (row, core),
        (adjacency, *blocks),
    )
    mine = call(
        forward_mine, struct((chips, size, width), f32), (core,), (adjacency, source)
    )
    own, *pieces = call(
        forward_chips,
        (struct((size, width), f32),) + (struct((size, width), bf16),) * len(far_first),
        (chip,),
        (mine, exchange(other, "col", col_shards, 1)),
    )
    received = [
        exchange(piece, "col", col_shards, 2 * step) for step, piece in zip(far_first, pieces)
    ]
    sent, active = call(
        vertex_chips,
        (struct((3, width, size), bf16), struct((size, out_width), f32)),
        (),
        (column, deg_scale, weight, cotangent, own, *received),
    )
    activations, written = call(write_out, (activation, struct((8, 128), f32)), (), (active,))
    received = [exchange(sent, "col", col_shards, 2 * step) for step in (1, 2, 3)]
    joined, own_grad = call(
        join_chips,
        (struct((chips + 1, width, size), bf16), struct((width, size), f32)),
        (chip, core),
        (sent, *received),
        [pltpu.VMEM((chips, 2, width, size), bf16)],
        after=(written,),
    )
    half_source = pltpu.VMEM((width, chips * size), bf16)
    own_total = call(
        backward_own,
        struct((width, row_shards * size), f32),
        (chip, core),
        (adjacency, joined),
        [half_source],
    )
    pieces = call(
        backward_rows,
        (struct((2, width, size), bf16),) * row_shards,
        (row, chip, core),
        (adjacency, own_total, own_grad, exchange(joined, "col", col_shards, 1)),
        [half_source, pltpu.VMEM((width, row_shards * size), f32)],
    )
    own_piece = pieces[-1]
    arrived = [
        crossed(piece, row_shards, col_shards, step) for step, piece in zip((2, 1, 3), pieces)
    ]
    packed = call(
        pack_pieces,
        struct((2 * len(arrived) + 1, width, size), bf16),
        (),
        (*arrived, own_piece),
    )
    input_grad, weight_grad = call(
        functools.partial(finish, factor),
        (input_shape, struct((height, out_width), f32)),
        (row, core),
        (deg_scale, own_piece, exchange(packed, "col", col_shards, 1), *arrived),
        [pltpu.VMEM((2, row_shards, height, out_width // 2), bf16)],
    )
    return (activations, input_grad, weight_grad)


def solution(mesh):
    in_specs = (
        P(("row", "col"), None),
        P(("row", "col")),
        P(),
        P(("row", "col"), None),
        P("row", "col", None),
        P("row", "col", None),
        P("row", "col"),
        P("row", "col", None, None, None),
    )
    out_specs = (P(("row", "col"), None), P(("row", "col"), None), P())
    return jax.shard_map(
        on_device, mesh=mesh, in_specs=in_specs, out_specs=out_specs, check_vma=False
    )
```

```python
import functools
import math

import jax
import jax.numpy as jnp
from jax import lax
from jax.experimental import pallas as pl
from jax.experimental.pallas import tpu as pltpu
from jax.sharding import PartitionSpec as P

VMEM = pl.BlockSpec(memory_space=pltpu.VMEM)
SMEM = pl.BlockSpec(memory_space=pltpu.SMEM)
ANY = pl.BlockSpec(memory_space=pl.ANY)
LIMIT = pltpu.CompilerParams(vmem_limit_bytes=40 * 1024 * 1024)
FIRST_FLOPS = 1 << 32
bf16, f32 = jnp.bfloat16, jnp.float32


def struct(shape, dtype):
    return jax.ShapeDtypeStruct(shape, dtype)


def call(body, out_shape, scalars, operands, scratch=(), flops=1 << 20, after=()):
    single = not isinstance(out_shape, (tuple, list))
    return pl.pallas_call(
        body,
        out_shape=out_shape,
        in_specs=[SMEM] * len(scalars) + [VMEM] * len(operands) + [ANY] * len(after),
        out_specs=VMEM if single else [VMEM] * len(out_shape),
        scratch_shapes=list(scratch),
        compiler_params=LIMIT,
        cost_estimate=pl.CostEstimate(flops=flops, bytes_accessed=1 << 20, transcendentals=0),
    )(*scalars, *operands, *after)


def block_at(index, size):
    return pl.ds(pl.multiple_of(index * size, size), size)


def unpack_tiles(count_ref, bits_ref, deg_ref, features_ref, scaled_ref, column_ref, masks_ref):
    column = spread_scale(deg_ref[...], column_ref.shape[0])
    column_ref[...] = column
    scaled_ref[...] = (features_ref[...].astype(f32) * column).astype(bf16)

    def one(slot):
        masks_ref[slot] = unpacked(jnp.where(slot < count_ref[0, 0], bits_ref[0, 0, slot], 0))

    pl.loop(0, masks_ref.shape[0])(one)


def forward_total(rows_ref, cols_ref, masks_ref, source, total):
    slots, tile_size = masks_ref.shape[:2]
    total[...] = jnp.zeros_like(total)

    def one(slot):
        place = block_at(rows_ref[0, 0, slot], tile_size)
        pick = block_at(cols_ref[0, 0, slot], tile_size)
        total[place, :] += jnp.dot(masks_ref[slot], source[pick, :], preferred_element_type=f32)

    pl.loop(0, slots)(one)


def backward_total(rows_ref, cols_ref, masks_ref, source, total):
    slots, tile_size = masks_ref.shape[:2]
    total[...] = jnp.zeros_like(total)

    def one(slot):
        pick = block_at(rows_ref[0, 0, slot], tile_size)
        place = block_at(cols_ref[0, 0, slot], tile_size)
        total[:, place] += jnp.dot(source[:, pick], masks_ref[slot], preferred_element_type=f32)

    pl.loop(0, slots)(one)


def unpacked(packed):
    words, tile_size = packed.shape
    repeated = jnp.broadcast_to(packed[:, None, :], (words, 8, tile_size))
    shifts = lax.broadcasted_iota(jnp.int32, (words, 8, tile_size), 1)
    bit_values = jnp.bitwise_and(jnp.right_shift(repeated, shifts), 1)
    return bit_values.reshape(words * 8, tile_size).astype(f32).astype(bf16)


def spread_scale(deg, size):
    rows = lax.broadcasted_iota(jnp.int32, (size, size), 0)
    columns = lax.broadcasted_iota(jnp.int32, (size, size), 1)
    diagonal = jnp.where(rows == columns, deg.astype(f32).reshape(1, size), 0.0).astype(bf16)
    return jnp.dot(diagonal, jnp.ones((size, size), bf16), preferred_element_type=f32)


def scale_column(deg_ref, column_ref):
    column_ref[...] = spread_scale(deg_ref[...], column_ref.shape[0])


def scale_rows(column_ref, features_ref, rows_ref, cols_ref, scaled_ref):
    scaled_ref[...] = (features_ref[...].astype(f32) * column_ref[...]).astype(bf16)


def build_adjacency(count_ref, rows_ref, cols_ref, bits_ref, after_ref, adjacency_ref):
    slots, words, tile_size = bits_ref.shape[2:]
    count = count_ref[0, 0]
    for slot in range(slots):
        packed = jnp.where(slot < count, bits_ref[0, 0, slot], 0)
        place = block_at(rows_ref[0, 0, slot], tile_size), block_at(cols_ref[0, 0, slot], tile_size)
        adjacency_ref[place] = unpacked(packed)


def rows_of(core, adjacency_ref, size):
    blocks = [
        adjacency_ref[block_at(2 * chip + core, size), :]
        for chip in range(adjacency_ref.shape[0] // (2 * size))
    ]
    return jnp.concatenate(blocks, axis=0)


def forward_other(row_ref, core_ref, adjacency_ref, *refs):
    *blocks, source_ref, other_ref = refs
    size = blocks[0].shape[0]
    for step, block in enumerate(blocks):
        owner = lax.rem(row_ref[0] + step, len(blocks))
        source_ref[block_at(owner, size), :] = block[...]
    rows = rows_of(1 - core_ref[0], adjacency_ref, size)
    total = jnp.dot(rows, source_ref[...], preferred_element_type=f32)
    other_ref[...] = total.astype(bf16).reshape(other_ref.shape)


def forward_mine(core_ref, adjacency_ref, source_ref, mine_ref):
    rows = rows_of(core_ref[0], adjacency_ref, mine_ref.shape[1])
    total = jnp.dot(rows, source_ref[...], preferred_element_type=f32)
    mine_ref[...] = total.reshape(mine_ref.shape)


def forward_chips(chip_ref, mine_ref, received_ref, own_ref, *pieces):
    chip = chip_ref[0]
    own_ref[...] = mine_ref[chip] + received_ref[chip].astype(f32)
    for step, piece in zip((3, 2, 1), pieces):
        peer = chip ^ step
        piece[...] = (mine_ref[peer] + received_ref[peer].astype(f32)).astype(bf16)


def vertex_values(summed, column_ref, deg_ref, weight_ref, cotangent_ref):
    hidden = (summed * column_ref[...]).astype(bf16)
    weight = weight_ref[...]
    pre_act = jnp.dot(hidden, weight, preferred_element_type=f32)
    sigmoid_value = 1.0 / (1.0 + jnp.exp(-pre_act))
    slope = sigmoid_value * (1.0 + pre_act * (1.0 - sigmoid_value))
    slope_term = (cotangent_ref[...].astype(f32) * slope).astype(bf16)
    spread = lax.dot_general(
        weight, slope_term, (((1,), (1,)), ((), ())), preferred_element_type=f32
    )
    back = (spread * deg_ref[...].astype(f32).reshape(1, -1)).astype(bf16)
    local_grad = lax.dot_general(
        hidden, slope_term, (((0,), (0,)), ((), ())), preferred_element_type=f32
    )
    return back, local_grad, pre_act * sigmoid_value


def vertex_chips(column_ref, deg_ref, weight_ref, cotangent_ref, own_ref, *refs):
    *received, sent_ref, active_ref = refs
    summed = own_ref[...] + sum(piece[...].astype(f32) for piece in received)
    sent_ref[0], local_grad, active_ref[...] = vertex_values(
        summed, column_ref, deg_ref, weight_ref, cotangent_ref
    )
    half = sent_ref.shape[2]
    for core in range(2):
        sent_ref[1 + core] = local_grad[:, core * half : (core + 1) * half].astype(bf16)


def write_out(active_ref, out_ref, written_ref):
    out_ref[...] = active_ref[...].astype(bf16)
    written_ref[...] = jnp.zeros_like(written_ref)


def join_chips(chip_ref, core_ref, *refs):
    *blocks, _, joined_ref, own_grad_ref, ordered = refs
    chips = len(blocks)
    for step, block in enumerate(blocks):
        joined_ref[step] = block[0]
        ordered[chip_ref[0] ^ step] = block[1:]
    grad = jnp.sum(ordered[...].astype(f32), axis=0)
    second = core_ref[0] == 1
    own_grad_ref[...] = jnp.where(second, grad[1], grad[0])
    joined_ref[chips] = jnp.where(second, grad[0], grad[1]).astype(bf16)


def chip_blocks(chip, blocks_ref, source):
    size = source.shape[0]
    for step in range(source.shape[1] // size):
        source[:, block_at(chip ^ step, size)] = blocks_ref[step]
    return source[...]


def backward_own(chip_ref, core_ref, adjacency_ref, joined_ref, total_ref, source):
    blocks = chip_blocks(chip_ref[0], joined_ref, source)
    rows = rows_of(core_ref[0], adjacency_ref, source.shape[0])
    total_ref[...] = jnp.dot(blocks, rows, preferred_element_type=f32)


def backward_rows(
    row_ref, chip_ref, core_ref, adjacency_ref, own_ref, grad_ref, received_ref, *refs
):
    *pieces, source, total = refs
    chips, size = received_ref.shape[0] - 1, received_ref.shape[2]
    blocks = chip_blocks(chip_ref[0], received_ref, source)
    rows = rows_of(1 - core_ref[0], adjacency_ref, size)
    total[...] = own_ref[...] + jnp.dot(blocks, rows, preferred_element_type=f32)
    grad = (grad_ref[...] + received_ref[chips].astype(f32)).astype(bf16)
    for step, piece in zip((1, 2, 3, 0), pieces):
        owner = lax.rem(row_ref[0] + step, len(pieces))
        piece[0] = total[:, block_at(owner, size)].astype(bf16)
        piece[1] = grad


def pack_pieces(*refs):
    *pieces, own_ref, sent_ref = refs
    count = len(pieces)
    for index, piece in enumerate(pieces):
        sent_ref[index] = piece[0]
        sent_ref[count + index] = piece[1]
    sent_ref[2 * count] = own_ref[1]


def finish(factor, row_ref, core_ref, deg_ref, own_ref, received_ref, *refs):
    *pieces, input_ref, grad_ref, ordered = refs
    count, size = len(pieces), own_ref.shape[1]
    total = sum(received_ref[index].astype(f32) for index in range(count)) + own_ref[0].astype(f32)
    input_ref[...] = (total * deg_ref[...].astype(f32).reshape(1, -1)).T.astype(bf16)
    for index, piece in enumerate(pieces):
        plane = lax.rem(row_ref[0] + count - index, count + 1)
        ordered[0, plane] = received_ref[count + index]
        ordered[1, plane] = piece[1]
    ordered[0, row_ref[0]] = own_ref[1]
    ordered[1, row_ref[0]] = received_ref[2 * count]
    for index, half in enumerate((core_ref[0], 1 - core_ref[0])):
        half_grad = jnp.sum(ordered[index].astype(f32), axis=0) * factor
        grad_ref[:, block_at(half, size)] = half_grad


def forward_all(rows_ref, cols_ref, masks_ref, source_ref, partial_ref, total):
    forward_total(rows_ref, cols_ref, masks_ref, source_ref, total)
    partial_ref[...] = total[...].astype(bf16).reshape(partial_ref.shape)


def vertex_all(column_ref, deg_ref, weight_ref, cotangent_ref, received_ref, act_ref, back_ref, grad_ref):
    summed = jnp.sum(received_ref[...].astype(f32), axis=0)
    back_ref[...], grad_ref[...], active = vertex_values(
        summed, column_ref, deg_ref, weight_ref, cotangent_ref
    )
    act_ref[...] = active.astype(bf16)


def backward_all(rows_ref, cols_ref, masks_ref, gathered_ref, pieces_ref, source, total):
    size = gathered_ref.shape[2]
    for shard in range(gathered_ref.shape[0]):
        source[:, shard * size : (shard + 1) * size] = gathered_ref[shard]
    backward_total(rows_ref, cols_ref, masks_ref, source, total)
    for shard in range(pieces_ref.shape[0]):
        pieces_ref[shard] = total[:, shard * size : (shard + 1) * size].astype(bf16)


def input_all(deg_ref, pieces_ref, out_ref):
    total = jnp.sum(pieces_ref[...].astype(f32), axis=0)
    out_ref[...] = (total * deg_ref[...].astype(f32).reshape(1, -1)).T.astype(bf16)


def exchange(block, axis, shards, distance):
    return lax.ppermute(block, axis, [(shard, shard ^ distance) for shard in range(shards)])


def shifted(block, axis, shards, step):
    return lax.ppermute(block, axis, [(shard, (shard + step) % shards) for shard in range(shards)])


def crossed(block, rows, cols, step):
    pairs = [
        (row * cols + col, (row + step) % rows * cols + (col ^ 1))
        for row in range(rows)
        for col in range(cols)
    ]
    return lax.ppermute(block, ("row", "col"), pairs)


def on_device(features, deg_scale, weight, cotangent, tile_rows, tile_cols, tile_count, tile_bits):
    size, width = features.shape
    height, out_width = weight.shape
    row_shards = lax.axis_size("row")
    col_shards = lax.axis_size("col")
    chips = col_shards // 2
    slots, words, tile_size = tile_bits.shape[2:]
    factor = 1.0 / math.sqrt(row_shards * col_shards * size)
    row = lax.axis_index("row").astype(jnp.int32).reshape(1)
    col = lax.axis_index("col").astype(jnp.int32)
    chip, core = (col // 2).reshape(1), (col % 2).reshape(1)
    forward_scratch = [pltpu.VMEM((col_shards * size, width), f32)]
    backward_scratch = [
        pltpu.VMEM((width, col_shards * size), bf16),
        pltpu.VMEM((width, row_shards * size), f32),
    ]
    prepared = (struct((size, width), bf16), struct((size, width), f32))
    block = struct((width, size), bf16)
    activation = struct((size, out_width), bf16)
    input_shape = struct((size, width), bf16)

    covered = slots * tile_size * tile_size == row_shards * col_shards * size * size
    if row_shards != 4 or col_shards != 8 or not covered:
        scaled, column, masks = call(
            unpack_tiles,
            prepared + (struct((slots, tile_size, tile_size), bf16),),
            (tile_count,),
            (tile_bits, deg_scale, features),
        )
        gathered = lax.all_gather(scaled, "row", axis=0, tiled=True)
        partial_value = call(
            forward_all,
            struct((col_shards, size, width), bf16),
            (tile_rows, tile_cols),
            (masks, gathered),
            forward_scratch,
        )
        received = lax.all_to_all(partial_value, "col", 0, 0)
        activations, back, local_grad = call(
            vertex_all,
            (activation, block, struct((height, out_width), f32)),
            (),
            (column, deg_scale, weight, cotangent, received),
        )
        weight_grad = lax.psum(local_grad, ("row", "col")) * factor
        pieces = call(
            backward_all,
            struct((row_shards, width, size), bf16),
            (tile_rows, tile_cols),
            (masks, lax.all_gather(back, "col")),
            backward_scratch,
        )
        arrived = lax.all_to_all(pieces, "row", 0, 0)
        input_grad = call(input_all, input_shape, (), (deg_scale, arrived))
        return (activations, input_grad, weight_grad)

    column = call(
        scale_column, struct((size, width), f32), (), (deg_scale,), flops=FIRST_FLOPS
    )
    scaled = call(scale_rows, struct((size, width), bf16), (), (column, features, tile_rows, tile_cols))
    adjacency = pl.pallas_call(
        build_adjacency,
        out_shape=struct((col_shards * size, row_shards * size), bf16),
        in_specs=[SMEM, SMEM, SMEM, VMEM, ANY],
        out_specs=VMEM,
        compiler_params=LIMIT,
        cost_estimate=pl.CostEstimate(flops=1 << 20, bytes_accessed=1 << 20, transcendentals=0),
    )(tile_count, tile_rows, tile_cols, tile_bits, scaled)
    far_first = (3, 2, 1)
    blocks = [shifted(scaled, "row", row_shards, step) for step in (3, 2, 1)]
    blocks.insert(0, scaled)
    source, other = call(
        forward_other,
        (struct((row_shards * size, width), bf16), struct((chips, size, width), bf16)),
        (row, core),
        (adjacency, *blocks),
    )
    mine = call(
        forward_mine, struct((chips, size, width), f32), (core,), (adjacency, source)
    )
    own, *pieces = call(
        forward_chips,
        (struct((size, width), f32),) + (struct((size, width), bf16),) * len(far_first),
        (chip,),
        (mine, exchange(other, "col", col_shards, 1)),
    )
    received = [
        exchange(piece, "col", col_shards, 2 * step) for step, piece in zip(far_first, pieces)
    ]
    sent, active = call(
        vertex_chips,
        (struct((3, width, size), bf16), struct((size, out_width), f32)),
        (),
        (column, deg_scale, weight, cotangent, own, *received),
    )
    activations, written = call(write_out, (activation, struct((8, 128), f32)), (), (active,))
    received = [exchange(sent, "col", col_shards, 2 * step) for step in (1, 2, 3)]
    joined, own_grad = call(
        join_chips,
        (struct((chips + 1, width, size), bf16), struct((width, size), f32)),
        (chip, core),
        (sent, *received),
        [pltpu.VMEM((chips, 2, width, size), bf16)],
        after=(written,),
    )
    half_source = pltpu.VMEM((width, chips * size), bf16)
    own_total = call(
        backward_own,
        struct((width, row_shards * size), f32),
        (chip, core),
        (adjacency, joined),
        [half_source],
    )
    pieces = call(
        backward_rows,
        (struct((2, width, size), bf16),) * row_shards,
        (row, chip, core),
        (adjacency, own_total, own_grad, exchange(joined, "col", col_shards, 1)),
        [half_source, pltpu.VMEM((width, row_shards * size), f32)],
    )
    own_piece = pieces[-1]
    arrived = [
        crossed(piece, row_shards, col_shards, step) for step, piece in zip((1, 2, 3), pieces)
    ]
    packed = call(
        pack_pieces,
        struct((2 * len(arrived) + 1, width, size), bf16),
        (),
        (*arrived, own_piece),
    )
    input_grad, weight_grad = call(
        functools.partial(finish, factor),
        (input_shape, struct((height, out_width), f32)),
        (row, core),
        (deg_scale, own_piece, exchange(packed, "col", col_shards, 1), *arrived),
        [pltpu.VMEM((2, row_shards, height, out_width // 2), bf16)],
    )
    return (activations, input_grad, weight_grad)


def solution(mesh):
    in_specs = (
        P(("row", "col"), None),
        P(("row", "col")),
        P(),
        P(("row", "col"), None),
        P("row", "col", None),
        P("row", "col", None),
        P("row", "col"),
        P("row", "col", None, None, None),
    )
    out_specs = (P(("row", "col"), None), P(("row", "col"), None), P())
    return jax.shard_map(
        on_device, mesh=mesh, in_specs=in_specs, out_specs=out_specs, check_vma=False
    )
```

```python
import functools
import math

import jax
import jax.numpy as jnp
from jax import lax
from jax.experimental import pallas as pl
from jax.experimental.pallas import tpu as pltpu
from jax.sharding import PartitionSpec as P

VMEM = pl.BlockSpec(memory_space=pltpu.VMEM)
SMEM = pl.BlockSpec(memory_space=pltpu.SMEM)
ANY = pl.BlockSpec(memory_space=pl.ANY)
LIMIT = pltpu.CompilerParams(vmem_limit_bytes=40 * 1024 * 1024)
FIRST_FLOPS = 1 << 32
bf16, f32 = jnp.bfloat16, jnp.float32


def struct(shape, dtype):
    return jax.ShapeDtypeStruct(shape, dtype)


def call(body, out_shape, scalars, operands, scratch=(), flops=1 << 20, after=()):
    single = not isinstance(out_shape, (tuple, list))
    return pl.pallas_call(
        body,
        out_shape=out_shape,
        in_specs=[SMEM] * len(scalars) + [VMEM] * len(operands) + [ANY] * len(after),
        out_specs=VMEM if single else [VMEM] * len(out_shape),
        scratch_shapes=list(scratch),
        compiler_params=LIMIT,
        cost_estimate=pl.CostEstimate(flops=flops, bytes_accessed=1 << 20, transcendentals=0),
    )(*scalars, *operands, *after)


def block_at(index, size):
    return pl.ds(pl.multiple_of(index * size, size), size)


def unpack_tiles(count_ref, bits_ref, deg_ref, features_ref, scaled_ref, column_ref, masks_ref):
    column = spread_scale(deg_ref[...], column_ref.shape[0])
    column_ref[...] = column
    scaled_ref[...] = (features_ref[...].astype(f32) * column).astype(bf16)

    def one(slot):
        masks_ref[slot] = unpacked(jnp.where(slot < count_ref[0, 0], bits_ref[0, 0, slot], 0))

    pl.loop(0, masks_ref.shape[0])(one)


def forward_total(rows_ref, cols_ref, masks_ref, source, total):
    slots, tile_size = masks_ref.shape[:2]
    total[...] = jnp.zeros_like(total)

    def one(slot):
        place = block_at(rows_ref[0, 0, slot], tile_size)
        pick = block_at(cols_ref[0, 0, slot], tile_size)
        total[place, :] += jnp.dot(masks_ref[slot], source[pick, :], preferred_element_type=f32)

    pl.loop(0, slots)(one)


def backward_total(rows_ref, cols_ref, masks_ref, source, total):
    slots, tile_size = masks_ref.shape[:2]
    total[...] = jnp.zeros_like(total)

    def one(slot):
        pick = block_at(rows_ref[0, 0, slot], tile_size)
        place = block_at(cols_ref[0, 0, slot], tile_size)
        total[:, place] += jnp.dot(source[:, pick], masks_ref[slot], preferred_element_type=f32)

    pl.loop(0, slots)(one)


def unpacked(packed):
    words, tile_size = packed.shape
    repeated = jnp.broadcast_to(packed[:, None, :], (words, 8, tile_size))
    shifts = lax.broadcasted_iota(jnp.int32, (words, 8, tile_size), 1)
    bit_values = jnp.bitwise_and(jnp.right_shift(repeated, shifts), 1)
    return bit_values.reshape(words * 8, tile_size).astype(f32).astype(bf16)


def spread_scale(deg, size):
    rows = lax.broadcasted_iota(jnp.int32, (size, size), 0)
    columns = lax.broadcasted_iota(jnp.int32, (size, size), 1)
    diagonal = jnp.where(rows == columns, deg.astype(f32).reshape(1, size), 0.0).astype(bf16)
    return jnp.dot(diagonal, jnp.ones((size, size), bf16), preferred_element_type=f32)


def scale_column(deg_ref, column_ref):
    column_ref[...] = spread_scale(deg_ref[...], column_ref.shape[0])


def scale_rows(column_ref, features_ref, rows_ref, cols_ref, scaled_ref):
    scaled_ref[...] = (features_ref[...].astype(f32) * column_ref[...]).astype(bf16)


def build_adjacency(count_ref, rows_ref, cols_ref, bits_ref, after_ref, adjacency_ref):
    slots, words, tile_size = bits_ref.shape[2:]
    count = count_ref[0, 0]
    for slot in range(slots):
        packed = jnp.where(slot < count, bits_ref[0, 0, slot], 0)
        place = block_at(rows_ref[0, 0, slot], tile_size), block_at(cols_ref[0, 0, slot], tile_size)
        adjacency_ref[place] = unpacked(packed)


def rows_of(core, adjacency_ref, size):
    blocks = [
        adjacency_ref[block_at(2 * chip + core, size), :]
        for chip in range(adjacency_ref.shape[0] // (2 * size))
    ]
    return jnp.concatenate(blocks, axis=0)


def forward_other(row_ref, core_ref, adjacency_ref, *refs):
    *blocks, source_ref, other_ref = refs
    size = blocks[0].shape[0]
    for step, block in zip((0, 1, 3, 2), blocks):
        source_ref[block_at(row_ref[0] ^ step, size), :] = block[...]
    rows = rows_of(1 - core_ref[0], adjacency_ref, size)
    total = jnp.dot(rows, source_ref[...], preferred_element_type=f32)
    other_ref[...] = total.astype(bf16).reshape(other_ref.shape)


def forward_mine(core_ref, adjacency_ref, source_ref, mine_ref):
    rows = rows_of(core_ref[0], adjacency_ref, mine_ref.shape[1])
    total = jnp.dot(rows, source_ref[...], preferred_element_type=f32)
    mine_ref[...] = total.reshape(mine_ref.shape)


def forward_chips(chip_ref, mine_ref, received_ref, own_ref, *pieces):
    chip = chip_ref[0]
    own_ref[...] = mine_ref[chip] + received_ref[chip].astype(f32)
    for step, piece in zip((3, 2, 1), pieces):
        peer = chip ^ step
        piece[...] = (mine_ref[peer] + received_ref[peer].astype(f32)).astype(bf16)


def vertex_values(summed, column_ref, deg_ref, weight_ref, cotangent_ref):
    hidden = (summed * column_ref[...]).astype(bf16)
    weight = weight_ref[...]
    pre_act = jnp.dot(hidden, weight, preferred_element_type=f32)
    sigmoid_value = 1.0 / (1.0 + jnp.exp(-pre_act))
    slope = sigmoid_value * (1.0 + pre_act * (1.0 - sigmoid_value))
    slope_term = (cotangent_ref[...].astype(f32) * slope).astype(bf16)
    spread = lax.dot_general(
        weight, slope_term, (((1,), (1,)), ((), ())), preferred_element_type=f32
    )
    back = (spread * deg_ref[...].astype(f32).reshape(1, -1)).astype(bf16)
    local_grad = lax.dot_general(
        hidden, slope_term, (((0,), (0,)), ((), ())), preferred_element_type=f32
    )
    return back, local_grad, pre_act * sigmoid_value


def vertex_chips(column_ref, deg_ref, weight_ref, cotangent_ref, own_ref, *refs):
    *received, sent_ref, active_ref = refs
    summed = own_ref[...] + sum(piece[...].astype(f32) for piece in received)
    sent_ref[0], local_grad, active_ref[...] = vertex_values(
        summed, column_ref, deg_ref, weight_ref, cotangent_ref
    )
    half = sent_ref.shape[2]
    for core in range(2):
        sent_ref[1 + core] = local_grad[:, core * half : (core + 1) * half].astype(bf16)


def write_out(active_ref, out_ref, written_ref):
    out_ref[...] = active_ref[...].astype(bf16)
    written_ref[...] = jnp.zeros_like(written_ref)


def join_chips(chip_ref, core_ref, *refs):
    *blocks, _, joined_ref, own_grad_ref, ordered = refs
    chips = len(blocks)
    for step, block in enumerate(blocks):
        joined_ref[step] = block[0]
        ordered[chip_ref[0] ^ step] = block[1:]
    grad = jnp.sum(ordered[...].astype(f32), axis=0)
    second = core_ref[0] == 1
    own_grad_ref[...] = jnp.where(second, grad[1], grad[0])
    joined_ref[chips] = jnp.where(second, grad[0], grad[1]).astype(bf16)


def chip_blocks(chip, blocks_ref, source):
    size = source.shape[0]
    for step in range(source.shape[1] // size):
        source[:, block_at(chip ^ step, size)] = blocks_ref[step]
    return source[...]


def backward_own(chip_ref, core_ref, adjacency_ref, joined_ref, total_ref, source):
    blocks = chip_blocks(chip_ref[0], joined_ref, source)
    rows = rows_of(core_ref[0], adjacency_ref, source.shape[0])
    total_ref[...] = jnp.dot(blocks, rows, preferred_element_type=f32)


def backward_rows(
    row_ref, chip_ref, core_ref, adjacency_ref, own_ref, grad_ref, received_ref, *refs
):
    *pieces, source, total = refs
    chips, size = received_ref.shape[0] - 1, received_ref.shape[2]
    blocks = chip_blocks(chip_ref[0], received_ref, source)
    rows = rows_of(1 - core_ref[0], adjacency_ref, size)
    total[...] = own_ref[...] + jnp.dot(blocks, rows, preferred_element_type=f32)
    grad = (grad_ref[...] + received_ref[chips].astype(f32)).astype(bf16)
    for step, piece in zip((1, 2, 3, 0), pieces):
        owner = lax.rem(row_ref[0] + step, len(pieces))
        piece[0] = total[:, block_at(owner, size)].astype(bf16)
        piece[1] = grad


def pack_pieces(*refs):
    *pieces, own_ref, sent_ref = refs
    count = len(pieces)
    sent_ref[0] = sum(piece[0].astype(f32) for piece in pieces).astype(bf16)
    for index, piece in enumerate(pieces):
        sent_ref[1 + index] = piece[1]
    sent_ref[1 + count] = own_ref[1]


def finish(factor, row_ref, core_ref, deg_ref, own_ref, received_ref, *refs):
    *pieces, input_ref, grad_ref, ordered = refs
    count, size = len(pieces), own_ref.shape[1]
    total = received_ref[0].astype(f32) + own_ref[0].astype(f32)
    input_ref[...] = (total * deg_ref[...].astype(f32).reshape(1, -1)).T.astype(bf16)
    for index, piece in enumerate(pieces):
        plane = lax.rem(row_ref[0] + count - index, count + 1)
        ordered[0, plane] = received_ref[1 + index]
        ordered[1, plane] = piece[1]
    ordered[0, row_ref[0]] = own_ref[1]
    ordered[1, row_ref[0]] = received_ref[1 + count]
    for index, half in enumerate((core_ref[0], 1 - core_ref[0])):
        half_grad = jnp.sum(ordered[index].astype(f32), axis=0) * factor
        grad_ref[:, block_at(half, size)] = half_grad


def forward_all(rows_ref, cols_ref, masks_ref, source_ref, partial_ref, total):
    forward_total(rows_ref, cols_ref, masks_ref, source_ref, total)
    partial_ref[...] = total[...].astype(bf16).reshape(partial_ref.shape)


def vertex_all(column_ref, deg_ref, weight_ref, cotangent_ref, received_ref, act_ref, back_ref, grad_ref):
    summed = jnp.sum(received_ref[...].astype(f32), axis=0)
    back_ref[...], grad_ref[...], active = vertex_values(
        summed, column_ref, deg_ref, weight_ref, cotangent_ref
    )
    act_ref[...] = active.astype(bf16)


def backward_all(rows_ref, cols_ref, masks_ref, gathered_ref, pieces_ref, source, total):
    size = gathered_ref.shape[2]
    for shard in range(gathered_ref.shape[0]):
        source[:, shard * size : (shard + 1) * size] = gathered_ref[shard]
    backward_total(rows_ref, cols_ref, masks_ref, source, total)
    for shard in range(pieces_ref.shape[0]):
        pieces_ref[shard] = total[:, shard * size : (shard + 1) * size].astype(bf16)


def input_all(deg_ref, pieces_ref, out_ref):
    total = jnp.sum(pieces_ref[...].astype(f32), axis=0)
    out_ref[...] = (total * deg_ref[...].astype(f32).reshape(1, -1)).T.astype(bf16)


def exchange(block, axis, shards, distance):
    return lax.ppermute(block, axis, [(shard, shard ^ distance) for shard in range(shards)])


def crossed(block, rows, cols, step):
    pairs = [
        (row * cols + col, (row + step) % rows * cols + (col ^ 1))
        for row in range(rows)
        for col in range(cols)
    ]
    return lax.ppermute(block, ("row", "col"), pairs)


def on_device(features, deg_scale, weight, cotangent, tile_rows, tile_cols, tile_count, tile_bits):
    size, width = features.shape
    height, out_width = weight.shape
    row_shards = lax.axis_size("row")
    col_shards = lax.axis_size("col")
    chips = col_shards // 2
    slots, words, tile_size = tile_bits.shape[2:]
    factor = 1.0 / math.sqrt(row_shards * col_shards * size)
    row = lax.axis_index("row").astype(jnp.int32).reshape(1)
    col = lax.axis_index("col").astype(jnp.int32)
    chip, core = (col // 2).reshape(1), (col % 2).reshape(1)
    forward_scratch = [pltpu.VMEM((col_shards * size, width), f32)]
    backward_scratch = [
        pltpu.VMEM((width, col_shards * size), bf16),
        pltpu.VMEM((width, row_shards * size), f32),
    ]
    prepared = (struct((size, width), bf16), struct((size, width), f32))
    block = struct((width, size), bf16)
    activation = struct((size, out_width), bf16)
    input_shape = struct((size, width), bf16)

    covered = slots * tile_size * tile_size == row_shards * col_shards * size * size
    if row_shards != 4 or col_shards != 8 or not covered:
        scaled, column, masks = call(
            unpack_tiles,
            prepared + (struct((slots, tile_size, tile_size), bf16),),
            (tile_count,),
            (tile_bits, deg_scale, features),
        )
        gathered = lax.all_gather(scaled, "row", axis=0, tiled=True)
        partial_value = call(
            forward_all,
            struct((col_shards, size, width), bf16),
            (tile_rows, tile_cols),
            (masks, gathered),
            forward_scratch,
        )
        received = lax.all_to_all(partial_value, "col", 0, 0)
        activations, back, local_grad = call(
            vertex_all,
            (activation, block, struct((height, out_width), f32)),
            (),
            (column, deg_scale, weight, cotangent, received),
        )
        weight_grad = lax.psum(local_grad, ("row", "col")) * factor
        pieces = call(
            backward_all,
            struct((row_shards, width, size), bf16),
            (tile_rows, tile_cols),
            (masks, lax.all_gather(back, "col")),
            backward_scratch,
        )
        arrived = lax.all_to_all(pieces, "row", 0, 0)
        input_grad = call(input_all, input_shape, (), (deg_scale, arrived))
        return (activations, input_grad, weight_grad)

    column = call(
        scale_column, struct((size, width), f32), (), (deg_scale,), flops=FIRST_FLOPS
    )
    scaled = call(scale_rows, struct((size, width), bf16), (), (column, features, tile_rows, tile_cols))
    adjacency = pl.pallas_call(
        build_adjacency,
        out_shape=struct((col_shards * size, row_shards * size), bf16),
        in_specs=[SMEM, SMEM, SMEM, VMEM, ANY],
        out_specs=VMEM,
        compiler_params=LIMIT,
        cost_estimate=pl.CostEstimate(flops=1 << 20, bytes_accessed=1 << 20, transcendentals=0),
    )(tile_count, tile_rows, tile_cols, tile_bits, scaled)
    far_first = (3, 2, 1)
    blocks = [exchange(scaled, "row", row_shards, step) for step in (1, 3, 2)]
    blocks.insert(0, scaled)
    source, other = call(
        forward_other,
        (struct((row_shards * size, width), bf16), struct((chips, size, width), bf16)),
        (row, core),
        (adjacency, *blocks),
    )
    mine = call(
        forward_mine, struct((chips, size, width), f32), (core,), (adjacency, source)
    )
    own, *pieces = call(
        forward_chips,
        (struct((size, width), f32),) + (struct((size, width), bf16),) * len(far_first),
        (chip,),
        (mine, exchange(other, "col", col_shards, 1)),
    )
    received = [
        exchange(piece, "col", col_shards, 2 * step) for step, piece in zip(far_first, pieces)
    ]
    sent, active = call(
        vertex_chips,
        (struct((3, width, size), bf16), struct((size, out_width), f32)),
        (),
        (column, deg_scale, weight, cotangent, own, *received),
    )
    activations, written = call(write_out, (activation, struct((8, 128), f32)), (), (active,))
    received = [exchange(sent, "col", col_shards, 2 * step) for step in (1, 2, 3)]
    joined, own_grad = call(
        join_chips,
        (struct((chips + 1, width, size), bf16), struct((width, size), f32)),
        (chip, core),
        (sent, *received),
        [pltpu.VMEM((chips, 2, width, size), bf16)],
        after=(written,),
    )
    half_source = pltpu.VMEM((width, chips * size), bf16)
    own_total = call(
        backward_own,
        struct((width, row_shards * size), f32),
        (chip, core),
        (adjacency, joined),
        [half_source],
    )
    pieces = call(
        backward_rows,
        (struct((2, width, size), bf16),) * row_shards,
        (row, chip, core),
        (adjacency, own_total, own_grad, exchange(joined, "col", col_shards, 1)),
        [half_source, pltpu.VMEM((width, row_shards * size), f32)],
    )
    own_piece = pieces[-1]
    arrived = [
        crossed(piece, row_shards, col_shards, step) for step, piece in zip((1, 2, 3), pieces)
    ]
    packed = call(
        pack_pieces,
        struct((len(arrived) + 2, width, size), bf16),
        (),
        (*arrived, own_piece),
    )
    input_grad, weight_grad = call(
        functools.partial(finish, factor),
        (input_shape, struct((height, out_width), f32)),
        (row, core),
        (deg_scale, own_piece, exchange(packed, "col", col_shards, 1), *arrived),
        [pltpu.VMEM((2, row_shards, height, out_width // 2), bf16)],
    )
    return (activations, input_grad, weight_grad)


def solution(mesh):
    in_specs = (
        P(("row", "col"), None),
        P(("row", "col")),
        P(),
        P(("row", "col"), None),
        P("row", "col", None),
        P("row", "col", None),
        P("row", "col"),
        P("row", "col", None, None, None),
    )
    out_specs = (P(("row", "col"), None), P(("row", "col"), None), P())
    return jax.shard_map(
        on_device, mesh=mesh, in_specs=in_specs, out_specs=out_specs, check_vma=False
    )
```
